128 devices in a mesh: sample: 16 (over z_lo, x, core), tensor: 8 (over y, z_hi).
Axes of the slice: x: 4, y: 4, z: 4 (z_hi: 2, z_lo: 2; z = z_hi * 2 + z_lo), core: 2. Of those that a mesh axis runs over, the one named last changes fastest.
Arguments:
- branch_tokens: bfloat16 [4096, 8192], P('sample', 'tensor'), may hold values from -6 to 6
- norm_gain: bfloat16 [8192], replicated, may hold values from 0.099609375 to 1.8984375
- query_weight: bfloat16 [8192, 8192], P(None, 'tensor'), may hold values from -0.0625 to 0.0625
- key_weight: bfloat16 [8192, 1024], P(None, 'tensor'), may hold values from -0.21875 to 0.21875
- value_weight: bfloat16 [8192, 1024], P(None, 'tensor'), may hold values from -0.0625 to 0.0625
- kv_pool: bfloat16 [640, 2, 128, 1024], P('sample', None, None, 'tensor'), may hold values from -200 to 200
- parent_owner: int32 [128], replicated, may hold values from 0 to 15, as said below
- parent_pages: int32 [128], replicated, may hold values from 1 to 5
- page_table: int32 [128, 5], replicated, may hold values from 0 to 39, as said below
- child_parent: int32 [1024], replicated, may hold values from 0 to 127, as said below
Outputs:
- attn_out: bfloat16 [4096, 8192], P('sample', 'tensor')
The draws below stay inside these ranges and needn't reach their ends.
Inputs may be any that keep to these rules, and one draw needn't show every extreme that they name: `parent_owner`: every index of sample holds the pages of exactly 8 parents. `page_table`: entries are pages of the owner's pool; all 5 entries of all parents of one owner are distinct. `child_parent`: every parent is named by exactly 8 children.
All inputs are finite; a program needn't handle non-finite values.
Results may differ from the reference program's by a relative error of at most 0.007.
The reference program's roundings to bfloat16 on the way count: a program that leaves them out, or rounds other values in their place, can miss the bound.
Values may be sent and summed in bfloat16 or wider, within the bound.
No kernel may reach another device: no remote copies, remote signals or barrier semaphores. Data moves between devices by JAX's collectives and lax.ppermute only.
A program may use at most 192 MiB of HBM per device.

```python
import math
import jax
import jax.numpy as jnp
from jax import lax

MODEL_WIDTH = 8192
QUERY_HEADS = 64
KEY_VALUE_HEADS = 8
HEAD_SIZE = 128
PAGE_TOKENS = 128
CHILD_STEPS = 4
FORK = 8
PAR_DEV = 8
MOST_PATH_PAGES = 5
PARENT_NODES = 128
CHILD_NODES = 1024
POOL = 40


def placement_slots(key):
    return jax.random.permutation(key, PARENT_NODES).astype(jnp.int32)


def draw_parent_owner(key, part):
    slot_order = placement_slots(key)
    return (slot_order // PAR_DEV).astype(jnp.int32)


def draw_page_table(key, part):
    slot_order = placement_slots(key)
    key = jax.random.fold_in(key, 7)
    scores = jax.random.randint(key, (PARENT_NODES // PAR_DEV, POOL), 0, 1 << 20, dtype=jnp.int32) * POOL + jnp.arange(POOL, dtype=jnp.int32)[None, :]
    orders = jnp.argsort(scores, axis=1).astype(jnp.int32)
    owner_index = slot_order // PAR_DEV
    owner_rank = slot_order % PAR_DEV
    columns = owner_rank[:, None] * MOST_PATH_PAGES + jnp.arange(MOST_PATH_PAGES, dtype=jnp.int32)[None, :]
    return orders[owner_index[:, None], columns].astype(jnp.int32)


def draw_parent_pages(key, part):
    key = jax.random.fold_in(key, 11)
    first_key, second_key = jax.random.split(key)
    page_counts = jax.random.randint(first_key, (PARENT_NODES,), 1, MOST_PATH_PAGES + 1, dtype=jnp.int32)
    longest = jax.random.randint(second_key, (), 0, PARENT_NODES, dtype=jnp.int32)
    page_counts = page_counts.at[longest].set(MOST_PATH_PAGES)
    page_counts = page_counts.at[(longest + 1) % PARENT_NODES].set(1)
    return page_counts.astype(jnp.int32)


def draw_child_parent(key, part):
    key = jax.random.fold_in(key, 13)
    return (jax.random.permutation(key, CHILD_NODES) // FORK).astype(jnp.int32)


def draw_kv_pool(key, part):
    key = jax.random.fold_in(key, 17)
    first_key, second_key = jax.random.split(key, 2)
    cache_pool_shape = (PARENT_NODES * MOST_PATH_PAGES, PAGE_TOKENS, KEY_VALUE_HEADS * HEAD_SIZE)
    key_part = 2.0 * jnp.clip(jax.random.normal(first_key, cache_pool_shape, jnp.float32), -6.0, 6.0)
    value_part = jnp.clip(jax.random.normal(second_key, cache_pool_shape, jnp.float32), -6.0, 6.0)
    return jnp.stack([key_part, value_part], axis=1).astype(jnp.bfloat16)


def level_of(key, shape, shards, least, top_value):
    level, own = 1.0, jax.random.fold_in(key, 6)
    for axis_at, parts in shards:
        draws = jnp.exp(jax.random.uniform(jax.random.fold_in(own, axis_at), (parts,), jnp.float32, least / len(shards), top_value / len(shards)))
        level = level * jnp.repeat(draws, shape[axis_at] // parts).reshape([-1 if axis == axis_at else 1 for axis in range(len(shape))])
    return level


def bell_draw(own_key, extent, width, most, shards=(), kind=jnp.bfloat16):
    level = level_of(own_key, extent, shards, -0.22, 0.18) if shards else 1.0
    entries = jax.random.normal(own_key, extent, jnp.float32) * width * level
    return jnp.minimum(jnp.maximum(entries, -most), most).astype(kind)


def setup_inputs(seed: int = 0) -> dict:
    key_of = jax.random.split(jax.random.key(seed), 11)
    return {
        "branch_tokens": bell_draw(key_of[0], (CHILD_NODES * CHILD_STEPS, MODEL_WIDTH), 1.0, 6.0, ((0, 16), (1, 8))),
        "norm_gain": jnp.clip(1.0 + 0.18 * jax.random.normal(key_of[1], (MODEL_WIDTH,), jnp.float32), 0.099609375, 1.8984375).astype(jnp.bfloat16),
        "query_weight": bell_draw(key_of[2], (MODEL_WIDTH, QUERY_HEADS * HEAD_SIZE), MODEL_WIDTH ** -0.5, 0.0625, ((1, 8),)),
        "key_weight": bell_draw(key_of[3], (MODEL_WIDTH, KEY_VALUE_HEADS * HEAD_SIZE), (MODEL_WIDTH // 12) ** -0.5, 0.21875, ((1, 8),)),
        "value_weight": bell_draw(key_of[4], (MODEL_WIDTH, KEY_VALUE_HEADS * HEAD_SIZE), MODEL_WIDTH ** -0.5, 0.0625, ((1, 8),)),
        "kv_pool": draw_kv_pool(jax.random.fold_in(key_of[10], 71), 0),
        "parent_owner": draw_parent_owner(jax.random.fold_in(key_of[10], 71), 0),
        "parent_pages": draw_parent_pages(jax.random.fold_in(key_of[10], 71), 0),
        "page_table": draw_page_table(jax.random.fold_in(key_of[10], 71), 0),
        "child_parent": draw_child_parent(jax.random.fold_in(key_of[10], 71), 0),
    }


ROPE_THETA = 10000.0
EPSILON = 1e-06

def norm_rows(tokens, gain_row):
    row_float = tokens.astype(jnp.float32)
    mean_square = lax.optimization_barrier(jnp.mean(row_float * row_float, axis=1, keepdims=True))
    return (row_float * lax.rsqrt(mean_square + EPSILON) * gain_row.astype(jnp.float32)).astype(jnp.bfloat16)

def rotate(vectors, token_positions):
    half_width = vectors.shape[-1] // 2
    inverse_freq = ROPE_THETA ** (-2.0 * jnp.arange(half_width, dtype=jnp.float32) / vectors.shape[-1])
    angles = token_positions[:, None] * inverse_freq[None, :]
    cosine_part = jnp.cos(angles)[:, None, :]
    sine_part = jnp.sin(angles)[:, None, :]
    front_half = vectors[..., :half_width]
    back_half = vectors[..., half_width:]
    return jnp.concatenate([front_half * cosine_part - back_half * sine_part, back_half * cosine_part + front_half * sine_part], axis=-1)

def project_heads(normalized_rows, weight, token_positions, head_count):
    projected = jnp.dot(normalized_rows, weight, preferred_element_type=jnp.float32).reshape(normalized_rows.shape[0], head_count, HEAD_SIZE)
    return rotate(projected, token_positions).astype(jnp.bfloat16)

def attend(scores, value_rows, einsum_form):
    top_score = lax.optimization_barrier(jnp.max(scores, axis=-1))
    weights = jnp.exp(scores - top_score[..., None])
    weight_sum = lax.optimization_barrier(jnp.sum(weights, axis=-1))
    rounded = lax.optimization_barrier(weights.astype(jnp.bfloat16))
    weighted = jnp.einsum(einsum_form, rounded.astype(jnp.float32), value_rows.astype(jnp.float32))
    return (weighted, weight_sum, top_score)

def path_part(query_rows, path_block, counts, score_scale):
    batch_rows = path_block.shape[0]
    page_count = path_block.shape[1]
    page_len = path_block.shape[3]
    kv_heads = query_rows.shape[2]
    head_width = query_rows.shape[4]
    path_keys = path_block[:, :, 0].reshape(batch_rows, page_count * page_len, kv_heads, head_width)
    path_values = path_block[:, :, 1].reshape(batch_rows, page_count * page_len, kv_heads, head_width)
    scores = jnp.einsum('nsjgd,ntjd->nsjgt', query_rows.astype(jnp.float32), path_keys.astype(jnp.float32)) * score_scale
    live_mask = jnp.arange(page_count * page_len, dtype=jnp.int32)[None, :] < (counts * page_len)[:, None]
    scores = jnp.where(live_mask[:, None, None, None, :], scores, -jnp.inf)
    return attend(scores, path_values, 'nsjgt,ntjd->nsjgd')

def own_part(query_rows, child_keys, child_values, score_scale):
    steps_here = query_rows.shape[1]
    scores = jnp.einsum('nsjgd,nujd->nsjgu', query_rows.astype(jnp.float32), child_keys.astype(jnp.float32)) * score_scale
    causal = jnp.arange(steps_here, dtype=jnp.int32)[:, None] >= jnp.arange(steps_here, dtype=jnp.int32)[None, :]
    scores = jnp.where(causal[None, :, None, None, :], scores, -jnp.inf)
    return attend(scores, child_values, 'nsjgu,nujd->nsjgd')

def combine(path_terms, own_terms):
    path_mix, path_total, path_top = path_terms
    own_mix, own_total, own_top = own_terms
    joint_top = jnp.maximum(path_top, own_top)
    path_factor = jnp.exp(path_top - joint_top)
    own_factor = jnp.exp(own_top - joint_top)
    numerator = path_mix * path_factor[..., None] + own_mix * own_factor[..., None]
    return numerator / (path_total * path_factor + own_total * own_factor)[..., None]

def reference(branch_tokens, norm_gain, query_weight, key_weight, value_weight, kv_pool, parent_owner, parent_pages, page_table, child_parent):
    query_group_count = QUERY_HEADS // KEY_VALUE_HEADS
    score_scale = 1.0 / math.sqrt(HEAD_SIZE)
    normalized_rows = norm_rows(branch_tokens, norm_gain)
    child_page_rows = parent_pages[child_parent]
    token_positions = (jnp.repeat(child_page_rows * PAGE_TOKENS, CHILD_STEPS) + jnp.tile(jnp.arange(CHILD_STEPS, dtype=jnp.int32), CHILD_NODES)).astype(jnp.float32)
    query_rows = project_heads(normalized_rows, query_weight, token_positions, QUERY_HEADS).reshape(CHILD_NODES, CHILD_STEPS, KEY_VALUE_HEADS, query_group_count, HEAD_SIZE)
    child_keys = project_heads(normalized_rows, key_weight, token_positions, KEY_VALUE_HEADS).reshape(CHILD_NODES, CHILD_STEPS, KEY_VALUE_HEADS, HEAD_SIZE)
    child_values = jnp.dot(normalized_rows, value_weight, preferred_element_type=jnp.float32).astype(jnp.bfloat16).reshape(CHILD_NODES, CHILD_STEPS, KEY_VALUE_HEADS, HEAD_SIZE)
    global_page_index = page_table[child_parent] + (parent_owner[child_parent] * POOL)[:, None]
    block_list = CHILD_NODES // 8

    def single_block(members):
        block_queries, block_keys, block_values, block_pages, block_counts = members
        path_terms = path_part(block_queries, kv_pool[block_pages], block_counts, score_scale)
        own_terms = own_part(block_queries, block_keys, block_values, score_scale)
        return combine(path_terms, own_terms).astype(jnp.bfloat16)
    head_output = lax.map(single_block, (query_rows.reshape(block_list, 8, CHILD_STEPS, KEY_VALUE_HEADS, query_group_count, HEAD_SIZE), child_keys.reshape(block_list, 8, CHILD_STEPS, KEY_VALUE_HEADS, HEAD_SIZE), child_values.reshape(block_list, 8, CHILD_STEPS, KEY_VALUE_HEADS, HEAD_SIZE), global_page_index.reshape(block_list, 8, MOST_PATH_PAGES), child_page_rows.reshape(block_list, 8)))
    return head_output.reshape(CHILD_NODES * CHILD_STEPS, QUERY_HEADS * HEAD_SIZE)
```

```python
import functools
import math

import jax
import jax.numpy as jnp
from jax import lax
from jax.experimental import pallas as pl
from jax.experimental.pallas import tpu as pltpu
from jax.sharding import PartitionSpec as P

HEAD = 128
PAGE = 128
STEPS = 4
FORK = 8
PARENTS_HERE = 8
MOST_PAGES = 5
ROPE_THETA = 10000.0
EPSILON = 1e-06
SLOTS = 16

BF16 = jnp.bfloat16
F32 = jnp.float32


def iota(shape, dim):
    return lax.broadcasted_iota(jnp.int32, shape, dim)


def one(mask):
    return jnp.where(mask, 1.0, 0.0).astype(BF16)


def mm(a, b):
    return lax.dot_general(a, b, (((1,), (0,)), ((), ())), preferred_element_type=F32)


def mm_nt(a, b):
    return lax.dot_general(a, b, (((1,), (1,)), ((), ())), preferred_element_type=F32)


def mm_tn(a, b):
    return lax.dot_general(a, b, (((0,), (0,)), ((), ())), preferred_element_type=F32)


def route_kernel(
    slots,
    groups,
    me_ref,
    child_ref,
    owner_ref,
    pages_ref,
    table_ref,
    x_ref,
    send_ref,
    to_ref,
    from_ref,
    info_ref,
    count_ref,
):
    me = me_ref[0]
    children = child_ref.shape[1]
    parents = owner_ref.shape[1]
    rows = x_ref.shape[0]
    here = rows // STEPS
    child = child_ref[...]
    owner = owner_ref[...]
    parent_hot = one(iota((parents, children), 0) == child)
    owner_of = mm(jnp.broadcast_to(owner.astype(F32), (16, parents)).astype(BF16), parent_hot)[0:1]
    owner_mask = one(iota((groups, children), 0) == owner_of.astype(jnp.int32))
    per_home = mm(owner_mask, one(iota((children, 128), 0) // here == iota((children, 128), 1)))
    count_ref[0] = jnp.max(per_home).astype(jnp.int32)

    pick = one(iota((children, rows), 0) == me * here + iota((children, rows), 1) // STEPS)
    home_mask = mm(owner_mask, pick)
    before = one(
        (iota((rows, rows), 0) // STEPS < iota((rows, rows), 1) // STEPS)
        & (iota((rows, rows), 0) % STEPS == 0)
    )
    rank = mm(home_mask.astype(BF16), before)
    target = jnp.sum(
        home_mask * (iota((groups, rows), 0).astype(F32) * (slots * STEPS) + rank * STEPS),
        axis=0,
        keepdims=True,
    ).astype(jnp.int32) + iota((1, rows), 1) % STEPS
    to_hot = one(iota((groups * slots * STEPS, rows), 0) == target)
    to_ref[...] = to_hot
    send_ref[...] = mm(to_hot, x_ref[...]).astype(BF16)

    mine_parent = owner == me
    tri = one(iota((parents, parents), 0) < iota((parents, parents), 1))
    tri_home = one(
        (iota((128, 128), 0) < iota((128, 128), 1))
        & (iota((128, 128), 0) // here == iota((128, 128), 1) // here)
    )
    tri_block = one(iota((128, 128), 0) < iota((128, 128), 1))
    parent_rank = mm(one(jnp.broadcast_to(mine_parent, (16, parents))), tri)[0:1].astype(jnp.int32)
    mine_hot = (iota((PARENTS_HERE, parents), 0) == parent_rank) & mine_parent
    pages = jnp.sum(jnp.where(mine_hot, pages_ref[...], 0), axis=1, keepdims=True)
    mine_hot = one(mine_hot)
    table = mm(mine_hot, table_ref[...].astype(F32).astype(BF16)).astype(jnp.int32)
    info_ref[...] = jnp.where(iota((PARENTS_HERE, 8), 1) == MOST_PAGES, pages, table)
    member = mm(mine_hot, parent_hot)
    carry = jnp.zeros((PARENTS_HERE, 1), F32)
    places, spots = [], []
    for block in range(children // 128):
        part = member[:, block * 128 : (block + 1) * 128]
        ahead = mm(part.astype(BF16), tri_block) + carry
        carry = carry + jnp.sum(part, axis=1, keepdims=True)
        is_mine = jnp.sum(part, axis=0, keepdims=True)
        place = jnp.sum(
            part * (iota((PARENTS_HERE, 128), 0).astype(F32) * FORK + ahead), axis=0, keepdims=True
        )
        in_home = mm(jnp.broadcast_to(is_mine, (16, 128)).astype(BF16), tri_home)[0:1]
        home = (block * 128 + iota((1, 128), 1)) // here
        spot = home.astype(F32) * slots + in_home
        places.append(jnp.where(is_mine > 0.5, place, -1.0))
        spots.append(jnp.where(is_mine > 0.5, spot, -1.0))
    place = jnp.concatenate(places, axis=1).astype(jnp.int32)
    spot = jnp.concatenate(spots, axis=1).astype(jnp.int32)
    place_hot = one(iota((here, children), 0) == place)
    spot_hot = one(iota((groups * slots, children), 0) == spot)
    from_child = mm_nt(place_hot, spot_hot).astype(BF16)
    wide = groups * slots * STEPS
    grow_rows = one(iota((rows, here), 0) // STEPS == iota((rows, here), 1))
    grow_columns = one(
        iota((groups * slots, wide), 0) == iota((groups * slots, wide), 1) // STEPS
    )
    from_rows = mm(mm(grow_rows, from_child).astype(BF16), grow_columns)
    same_step = iota((rows, wide), 0) % STEPS == iota((rows, wide), 1) % STEPS
    from_ref[...] = jnp.where(same_step, from_rows, 0.0).astype(BF16)


def route(slots, groups, me, child_parent, parent_owner, parent_pages, page_table, rows):
    count, width = rows.shape
    wide = groups * slots * STEPS
    vmem = pl.BlockSpec(memory_space=pltpu.VMEM)
    smem = pl.BlockSpec(memory_space=pltpu.SMEM)
    return pl.pallas_call(
        functools.partial(route_kernel, slots, groups),
        out_shape=(
            jax.ShapeDtypeStruct((wide, width), BF16),
            jax.ShapeDtypeStruct((wide, count), BF16),
            jax.ShapeDtypeStruct((count, wide), BF16),
            jax.ShapeDtypeStruct((PARENTS_HERE, 8), jnp.int32),
            jax.ShapeDtypeStruct((1,), jnp.int32),
        ),
        in_specs=[smem] + [vmem] * 5,
        out_specs=(vmem, vmem, vmem, vmem, smem),
        compiler_params=pltpu.CompilerParams(vmem_limit_bytes=48 * 2**20),
    )(
        me,
        child_parent.reshape(1, -1),
        parent_owner.reshape(1, -1),
        parent_pages.reshape(1, -1),
        jnp.pad(page_table, ((0, 0), (0, 8 - page_table.shape[1]))),
        rows,
    )


def pick_kernel(hot_ref, rows_ref, out_ref):
    out_ref[...] = mm(hot_ref[...], rows_ref[...]).astype(BF16)


def pick_tn_kernel(hot_ref, rows_ref, out_ref):
    out_ref[...] = mm_tn(hot_ref[...], rows_ref[...]).astype(BF16)


def pick_rows(body, hot, rows, count):
    vmem = pl.BlockSpec(memory_space=pltpu.VMEM)
    return pl.pallas_call(
        body,
        out_shape=jax.ShapeDtypeStruct((count, rows.shape[1]), BF16),
        in_specs=[vmem, vmem],
        out_specs=vmem,
        compiler_params=pltpu.CompilerParams(vmem_limit_bytes=48 * 2**20),
    )(hot, rows)


def layer_kernel(
    width,
    order_ref,
    info_ref,
    *refs,
):
    blocks = refs[:8]
    (
        gain_ref,
        wq_ref,
        wk_ref,
        wv_ref,
        cos_ref,
        sin_ref,
        pool_ref,
        back_ref,
        out_ref,
        acc_q,
        acc_k,
        acc_v,
        scale_ref,
        x_ref,
        q_ref,
        k_ref,
        v_ref,
        o_ref,
    ) = refs[8:]
    step = pl.program_id(0)
    rows = blocks[0].shape[0]

    @pl.when(step == 0)
    def _():
        total = jnp.zeros((rows, 1), F32)
        for block in blocks:
            x = block[...].astype(F32)
            total = total + jnp.sum(x * x, axis=1, keepdims=True)
        scale_ref[...] = jnp.broadcast_to(
            lax.rsqrt(total * (1.0 / width) + EPSILON), scale_ref.shape
        )
        acc_q[...] = jnp.zeros_like(acc_q)
        acc_k[...] = jnp.zeros_like(acc_k)
        acc_v[...] = jnp.zeros_like(acc_v)

    for i, block in enumerate(blocks):

        @pl.when(step == i)
        def _(block=block):
            x = block[...].astype(F32) * scale_ref[:, 0:1] * gain_ref[0].astype(F32)
            x_ref[...] = x.astype(BF16)

    x = x_ref[...]
    acc_q[...] += mm(x, wq_ref[...])
    acc_k[...] += mm(x, wk_ref[...])
    acc_v[...] += mm(x, wv_ref[...])

    @pl.when(step == 7)
    def _():
        cos = cos_ref[...]
        sin = sin_ref[...]

        def turn(part):
            return (part * cos + pltpu.roll(part, HEAD // 2, 1) * sin).astype(BF16)

        heads = acc_q.shape[1] // HEAD
        for h in range(heads):
            cut = slice(h * HEAD, (h + 1) * HEAD)
            q_ref[:, cut] = turn(acc_q[:, cut])
        k_ref[...] = turn(acc_k[...])
        v_ref[...] = acc_v[...].astype(BF16)

        family = FORK * STEPS
        scale = 1.0 / math.sqrt(HEAD)
        row_at = iota((heads * family, family), 0) % family
        key_at = iota((heads * family, family), 1)
        own_mask = (row_at // STEPS == key_at // STEPS) & (row_at >= key_at)

        @pl.loop(0, PARENTS_HERE)
        def _(j):
            at = pl.ds(pl.multiple_of(j * family, family), family)
            q = jnp.concatenate(
                [q_ref[at, h * HEAD : (h + 1) * HEAD] for h in range(heads)], axis=0
            )
            own = jnp.where(own_mask, mm_nt(q, k_ref[at, :]) * scale, -jnp.inf)
            own_top = jnp.max(own, axis=1, keepdims=True)
            own_weight = jnp.exp(own - own_top)
            own_total = jnp.sum(own_weight, axis=1, keepdims=True)
            own_mix = mm(own_weight.astype(BF16), v_ref[at, :])
            length = info_ref[j, MOST_PAGES]
            for n in range(1, MOST_PAGES + 1):

                @pl.when(length == n)
                def _(n=n):
                    ids = [info_ref[j, i] for i in range(n)]
                    keys = jnp.concatenate([pool_ref[i, 0] for i in ids], axis=0)
                    values = jnp.concatenate([pool_ref[i, 1] for i in ids], axis=0)
                    path = mm_nt(q, keys) * scale
                    path_top = jnp.max(path, axis=1, keepdims=True)
                    weight = jnp.exp(path - path_top)
                    path_total = jnp.sum(weight, axis=1, keepdims=True)
                    path_mix = mm(weight.astype(BF16), values)
                    top = jnp.maximum(path_top, own_top)
                    path_factor = jnp.exp(path_top - top)
                    own_factor = jnp.exp(own_top - top)
                    both = path_mix * path_factor + own_mix * own_factor
                    out = both / (path_total * path_factor + own_total * own_factor)
                    out = out.astype(BF16)
                    for h in range(heads):
                        o_ref[at, h * HEAD : (h + 1) * HEAD] = out[h * family : (h + 1) * family]

        out_ref[...] = mm_tn(back_ref[...], o_ref[...]).astype(BF16)


def layer(order, info, blocks, gain, wq, wk, wv, cos, sin, pool, back):
    rows, part = blocks[0].shape
    width = wq.shape[0]
    wide = back.shape[1]

    def whole(a):
        return pl.BlockSpec(a.shape, lambda i, order, info: (0,) * a.ndim)

    return pl.pallas_call(
        functools.partial(layer_kernel, width),
        out_shape=jax.ShapeDtypeStruct((wide, wq.shape[1]), BF16),
        grid_spec=pltpu.PrefetchScalarGridSpec(
            num_scalar_prefetch=2,
            grid=(8,),
            in_specs=[whole(b) for b in blocks]
            + [pl.BlockSpec((1, 1, part), lambda i, order, info: (order[i], 0, 0))]
            + [
                pl.BlockSpec((part, w.shape[1]), lambda i, order, info: (order[i], 0))
                for w in (wq, wk, wv)
            ]
            + [whole(a) for a in (cos, sin, pool, back)],
            out_specs=pl.BlockSpec((wide, wq.shape[1]), lambda i, order, info: (0, 0)),
            scratch_shapes=[
                pltpu.VMEM((rows, wq.shape[1]), F32),
                pltpu.VMEM((rows, HEAD), F32),
                pltpu.VMEM((rows, HEAD), F32),
                pltpu.VMEM((rows, HEAD), F32),
                pltpu.VMEM((rows, part), BF16),
                pltpu.VMEM((rows, wq.shape[1]), BF16),
                pltpu.VMEM((rows, HEAD), BF16),
                pltpu.VMEM((rows, HEAD), BF16),
                pltpu.VMEM((rows, wq.shape[1]), BF16),
            ],
        ),
        compiler_params=pltpu.CompilerParams(
            vmem_limit_bytes=56 * 2**20, dimension_semantics=("arbitrary",)
        ),
    )(order, info, *blocks, gain.reshape(8, 1, part), wq, wk, wv, cos, sin, pool, back)


def moves(dy, dz):
    return [(t, ((t // 2 + dy) % 4) * 2 + (t + dz) % 2) for t in range(8)]


def gather_tensor(x):
    def shift(block, dy, dz):
        return lax.ppermute(block, "tensor", moves(dy, dz))

    found = {(0, 0): x}
    found[3, 0] = shift(x, 1, 0)
    found[1, 0] = shift(x, -1, 0)
    found[0, 1] = shift(x, 0, 1)
    found[2, 0] = shift(found[3, 0], 1, 0)
    found[1, 1] = shift(found[0, 1], -1, 0)
    found[3, 1] = shift(found[3, 0], 0, 1)
    half = x.shape[0] // 2
    low = shift(found[3, 1][:half], 1, 0)
    high = shift(found[1, 1][half:], -1, 0)
    found[2, 1] = jnp.concatenate([low, high], axis=0)
    return found


def after_route(slots, groups, arrays, routed):
    (norm_gain, query_weight, key_weight, value_weight, kv_pool) = arrays
    send, to_hot, from_hot, info = routed
    rows = from_hot.shape[0]
    wide, width = send.shape
    came = lax.all_to_all(send.reshape(groups, wide // groups, width), "sample", 0, 0)
    mine = pick_rows(pick_kernel, from_hot, came.reshape(wide, width), rows)
    found = gather_tensor(mine)
    keys = list(found)
    t = lax.axis_index("tensor")
    order = jnp.stack([((t // 2 + dy) % 4) * 2 + (t + dz) % 2 for dy, dz in keys]).astype(jnp.int32)
    pages = info[:, MOST_PAGES]
    positions = (
        jnp.repeat(pages * PAGE, FORK * STEPS)
        + jnp.tile(jnp.arange(STEPS, dtype=jnp.int32), PARENTS_HERE * FORK)
    ).astype(F32)
    half = HEAD // 2
    inverse = ROPE_THETA ** (-2.0 * jnp.arange(half, dtype=F32) / HEAD)
    angles = positions[:, None] * inverse[None, :]
    cos, sin = jnp.cos(angles), jnp.sin(angles)
    cos = jnp.concatenate([cos, cos], axis=1)
    sin = jnp.concatenate([-sin, sin], axis=1)
    back = layer(
        order,
        info,
        list(found.values()),
        norm_gain,
        query_weight,
        key_weight,
        value_weight,
        cos,
        sin,
        kv_pool,
        from_hot,
    )
    home = lax.all_to_all(back.reshape(groups, wide // groups, back.shape[1]), "sample", 0, 0)
    return pick_rows(pick_tn_kernel, to_hot, home.reshape(wide, back.shape[1]), rows)


def local(
    branch_tokens,
    norm_gain,
    query_weight,
    key_weight,
    value_weight,
    kv_pool,
    parent_owner,
    parent_pages,
    page_table,
    child_parent,
):
    groups = lax.axis_size("sample")
    me = lax.axis_index("sample").astype(jnp.int32).reshape(1)
    tables = (child_parent, parent_owner, parent_pages, page_table)
    arrays = (norm_gain, query_weight, key_weight, value_weight, kv_pool)
    *routed, most = route(SLOTS, groups, me, *tables, branch_tokens)

    def usual():
        return after_route(SLOTS, groups, arrays, routed)

    def crowded():
        slots = branch_tokens.shape[0] // STEPS
        *wider, _ = route(slots, groups, me, *tables, branch_tokens)
        return after_route(slots, groups, arrays, wider)

    return lax.cond(most[0] <= SLOTS, usual, crowded)


def solution(mesh):
    return jax.shard_map(
        local,
        mesh=mesh,
        in_specs=(
            P("sample", "tensor"),
            P(),
            P(None, "tensor"),
            P(None, "tensor"),
            P(None, "tensor"),
            P("sample", None, None, "tensor"),
            P(),
            P(),
            P(),
            P(),
        ),
        out_specs=P("sample", "tensor"),
        check_vma=False,
    )
```

```python
import functools
import math

import jax
import jax.numpy as jnp
from jax import lax
from jax.experimental import pallas as pl
from jax.experimental.pallas import tpu as pltpu
from jax.sharding import PartitionSpec as P

HEAD = 128
PAGE = 128
STEPS = 4
FORK = 8
PARENTS_HERE = 8
MOST_PAGES = 5
ROPE_THETA = 10000.0
EPSILON = 1e-06
SLOTS = 14

BF16 = jnp.bfloat16
F32 = jnp.float32


def iota(shape, dim):
    return lax.broadcasted_iota(jnp.int32, shape, dim)


def one(mask):
    return jnp.where(mask, 1.0, 0.0).astype(BF16)


def mm(a, b):
    return lax.dot_general(a, b, (((1,), (0,)), ((), ())), preferred_element_type=F32)


def mm_nt(a, b):
    return lax.dot_general(a, b, (((1,), (1,)), ((), ())), preferred_element_type=F32)


def mm_tn(a, b):
    return lax.dot_general(a, b, (((0,), (0,)), ((), ())), preferred_element_type=F32)


def route_kernel(
    slots,
    groups,
    me_ref,
    child_ref,
    owner_ref,
    pages_ref,
    table_ref,
    x_ref,
    send_ref,
    to_ref,
    from_ref,
    info_ref,
    count_ref,
):
    me = me_ref[0]
    children = child_ref.shape[1]
    parents = owner_ref.shape[1]
    rows = x_ref.shape[0]
    here = rows // STEPS
    child = child_ref[...]
    owner = owner_ref[...]
    parent_hot = one(iota((parents, children), 0) == child)
    owner_of = mm(jnp.broadcast_to(owner.astype(F32), (16, parents)).astype(BF16), parent_hot)[0:1]
    owner_mask = one(iota((groups, children), 0) == owner_of.astype(jnp.int32))
    per_home = mm(owner_mask, one(iota((children, 128), 0) // here == iota((children, 128), 1)))
    count_ref[0] = jnp.max(per_home).astype(jnp.int32)

    pick = one(iota((children, rows), 0) == me * here + iota((children, rows), 1) // STEPS)
    home_mask = mm(owner_mask, pick)
    before = one(
        (iota((rows, rows), 0) // STEPS < iota((rows, rows), 1) // STEPS)
        & (iota((rows, rows), 0) % STEPS == 0)
    )
    rank = mm(home_mask.astype(BF16), before)
    target = jnp.sum(
        home_mask * (iota((groups, rows), 0).astype(F32) * (slots * STEPS) + rank * STEPS),
        axis=0,
        keepdims=True,
    ).astype(jnp.int32) + iota((1, rows), 1) % STEPS
    to_hot = one(iota((groups * slots * STEPS, rows), 0) == target)
    to_ref[...] = to_hot
    send_ref[...] = mm(to_hot, x_ref[...]).astype(BF16)

    mine_parent = owner == me
    tri = one(iota((parents, parents), 0) < iota((parents, parents), 1))
    tri_home = one(
        (iota((128, 128), 0) < iota((128, 128), 1))
        & (iota((128, 128), 0) // here == iota((128, 128), 1) // here)
    )
    tri_block = one(iota((128, 128), 0) < iota((128, 128), 1))
    parent_rank = mm(one(jnp.broadcast_to(mine_parent, (16, parents))), tri)[0:1].astype(jnp.int32)
    mine_hot = (iota((PARENTS_HERE, parents), 0) == parent_rank) & mine_parent
    pages = jnp.sum(jnp.where(mine_hot, pages_ref[...], 0), axis=1, keepdims=True)
    mine_hot = one(mine_hot)
    table = mm(mine_hot, table_ref[...].astype(F32).astype(BF16)).astype(jnp.int32)
    info_ref[...] = jnp.where(iota((PARENTS_HERE, 8), 1) == MOST_PAGES, pages, table)
    member = mm(mine_hot, parent_hot)
    carry = jnp.zeros((PARENTS_HERE, 1), F32)
    places, spots = [], []
    for block in range(children // 128):
        part = member[:, block * 128 : (block + 1) * 128]
        ahead = mm(part.astype(BF16), tri_block) + carry
        carry = carry + jnp.sum(part, axis=1, keepdims=True)
        is_mine = jnp.sum(part, axis=0, keepdims=True)
        place = jnp.sum(
            part * (iota((PARENTS_HERE, 128), 0).astype(F32) * FORK + ahead), axis=0, keepdims=True
        )
        in_home = mm(jnp.broadcast_to(is_mine, (16, 128)).astype(BF16), tri_home)[0:1]
        home = (block * 128 + iota((1, 128), 1)) // here
        spot = home.astype(F32) * slots + in_home
        places.append(jnp.where(is_mine > 0.5, place, -1.0))
        spots.append(jnp.where(is_mine > 0.5, spot, -1.0))
    place = jnp.concatenate(places, axis=1).astype(jnp.int32)
    spot = jnp.concatenate(spots, axis=1).astype(jnp.int32)
    place_hot = one(iota((here, children), 0) == place)
    spot_hot = one(iota((groups * slots, children), 0) == spot)
    from_child = mm_nt(place_hot, spot_hot).astype(BF16)
    wide = groups * slots * STEPS
    grow_rows = one(iota((rows, here), 0) // STEPS == iota((rows, here), 1))
    grow_columns = one(
        iota((groups * slots, wide), 0) == iota((groups * slots, wide), 1) // STEPS
    )
    from_rows = mm(mm(grow_rows, from_child).astype(BF16), grow_columns)
    same_step = iota((rows, wide), 0) % STEPS == iota((rows, wide), 1) % STEPS
    from_ref[...] = jnp.where(same_step, from_rows, 0.0).astype(BF16)


def route(slots, groups, me, child_parent, parent_owner, parent_pages, page_table, rows):
    count, width = rows.shape
    wide = groups * slots * STEPS
    vmem = pl.BlockSpec(memory_space=pltpu.VMEM)
    smem = pl.BlockSpec(memory_space=pltpu.SMEM)
    return pl.pallas_call(
        functools.partial(route_kernel, slots, groups),
        out_shape=(
            jax.ShapeDtypeStruct((wide, width), BF16),
            jax.ShapeDtypeStruct((wide, count), BF16),
            jax.ShapeDtypeStruct((count, wide), BF16),
            jax.ShapeDtypeStruct((PARENTS_HERE, 8), jnp.int32),
            jax.ShapeDtypeStruct((1,), jnp.int32),
        ),
        in_specs=[smem] + [vmem] * 5,
        out_specs=(vmem, vmem, vmem, vmem, smem),
        compiler_params=pltpu.CompilerParams(vmem_limit_bytes=48 * 2**20),
    )(
        me,
        child_parent.reshape(1, -1),
        parent_owner.reshape(1, -1),
        parent_pages.reshape(1, -1),
        jnp.pad(page_table, ((0, 0), (0, 8 - page_table.shape[1]))),
        rows,
    )


def pick_tn_kernel(hot_ref, rows_ref, out_ref):
    out_ref[...] = mm_tn(hot_ref[...], rows_ref[...]).astype(BF16)


def pick_rows(body, hot, rows, count):
    vmem = pl.BlockSpec(memory_space=pltpu.VMEM)
    return pl.pallas_call(
        body,
        out_shape=jax.ShapeDtypeStruct((count, rows.shape[1]), BF16),
        in_specs=[vmem, vmem],
        out_specs=vmem,
        compiler_params=pltpu.CompilerParams(vmem_limit_bytes=48 * 2**20),
    )(hot, rows)


def pick_sum_kernel(hot_ref, rows_ref, out_ref, sum_ref):
    x = mm(hot_ref[...], rows_ref[...])
    out_ref[...] = x.astype(BF16)
    total = jnp.sum(x * x, axis=1, keepdims=True)
    total = jnp.broadcast_to(total, (total.shape[0], 128)).T
    sum_ref[...] = jnp.broadcast_to(total[0:1], sum_ref.shape[:1] + total.shape[1:])[:, None, :]


def pick_and_sum(hot, rows, copies):
    vmem = pl.BlockSpec(memory_space=pltpu.VMEM)
    count = hot.shape[0]
    return pl.pallas_call(
        pick_sum_kernel,
        out_shape=(
            jax.ShapeDtypeStruct((count, rows.shape[1]), BF16),
            jax.ShapeDtypeStruct((copies, 1, count), F32),
        ),
        in_specs=[vmem, vmem],
        out_specs=(vmem, vmem),
        compiler_params=pltpu.CompilerParams(vmem_limit_bytes=48 * 2**20),
    )(hot, rows)


def row_scale(sum_ref, width):
    total = jnp.sum(sum_ref[:, 0, :], axis=0, keepdims=True)
    scale = lax.rsqrt(total * (1.0 / width) + EPSILON)
    return jnp.broadcast_to(scale, (128, scale.shape[1])).T


def normed(x, scale, gain):
    return (x.astype(F32) * scale * gain.astype(F32)).astype(BF16)


def add_products(acc, x, wq_ref, wk_ref, wv_ref, wkv_ref):
    wide = wq_ref.shape[1]
    wkv_ref[:, :HEAD] = wk_ref[...]
    wkv_ref[:, HEAD:] = wv_ref[...]
    acc[:, :wide] += mm(x, wq_ref[...])
    acc[:, wide:] += mm(x, wkv_ref[...])


def project_kernel(width, count, first, order_ref, sum_ref, *refs):
    blocks = refs[:count]
    gain_ref, wq_ref, wk_ref, wv_ref = refs[count : count + 4]
    before = None if first else refs[count + 4]
    acc_ref, x_ref, scale_ref, wkv_ref = refs[-4:]
    step = pl.program_id(0)

    @pl.when(step == 0)
    def _():
        scale_ref[...] = row_scale(sum_ref, width)
        acc_ref[...] = jnp.zeros_like(acc_ref) if first else before[...]

    for i, block in enumerate(blocks):

        @pl.when(step == i)
        def _(block=block):
            x_ref[...] = normed(block[...], scale_ref[:, 0:1], gain_ref[0])

    add_products(acc_ref, x_ref[...], wq_ref, wk_ref, wv_ref, wkv_ref)


def project(order, sums, blocks, gain, wq, wk, wv, before=None):
    rows, part = blocks[0].shape
    columns = wq.shape[1] + wk.shape[1] + wv.shape[1]
    count = len(blocks)

    def whole(a):
        return pl.BlockSpec(a.shape, lambda i, order: (0,) * a.ndim)

    extra = [] if before is None else [before]
    return pl.pallas_call(
        functools.partial(project_kernel, wq.shape[0], count, before is None),
        out_shape=jax.ShapeDtypeStruct((rows, columns), F32),
        grid_spec=pltpu.PrefetchScalarGridSpec(
            num_scalar_prefetch=1,
            grid=(count,),
            in_specs=[whole(sums)]
            + [whole(b) for b in blocks]
            + [pl.BlockSpec((1, 1, part), lambda i, order: (order[i], 0, 0))]
            + [
                pl.BlockSpec((part, w.shape[1]), lambda i, order: (order[i], 0))
                for w in (wq, wk, wv)
            ]
            + [whole(a) for a in extra],
            out_specs=pl.BlockSpec((rows, columns), lambda i, order: (0, 0)),
            scratch_shapes=[
                pltpu.VMEM((rows, part), BF16),
                pltpu.VMEM((rows, 128), F32),
                pltpu.VMEM((part, 2 * HEAD), BF16),
            ],
        ),
        compiler_params=pltpu.CompilerParams(vmem_limit_bytes=32 * 2**20),
        cost_estimate=pl.CostEstimate(
            flops=2 * rows * part * count * columns * 3,
            bytes_accessed=2 * part * count * columns,
            transcendentals=0,
        ),
    )(order, sums, *blocks, gain, wq, wk, wv, *extra)


def attend_kernel(
    width,
    order_ref,
    info_ref,
    sum_ref,
    low_ref,
    high_ref,
    gain_ref,
    wq_ref,
    wk_ref,
    wv_ref,
    before_ref,
    cos_ref,
    sin_ref,
    pool_ref,
    back_ref,
    out_ref,
    acc_ref,
    x_ref,
    wkv_ref,
    q_ref,
    k_ref,
    v_ref,
    o_ref,
):
    scale = row_scale(sum_ref, width)[:, 0:1]
    half = low_ref.shape[0]
    x_ref[:half] = normed(low_ref[...], scale[:half], gain_ref[0])
    x_ref[half:] = normed(high_ref[...], scale[half:], gain_ref[0])
    acc_ref[...] = before_ref[...]
    add_products(acc_ref, x_ref[...], wq_ref, wk_ref, wv_ref, wkv_ref)

    cos = cos_ref[...]
    sin = sin_ref[...]

    def turn(part):
        return (part * cos + pltpu.roll(part, HEAD // 2, 1) * sin).astype(BF16)

    heads = wq_ref.shape[1] // HEAD
    for h in range(heads):
        cut = slice(h * HEAD, (h + 1) * HEAD)
        q_ref[:, cut] = turn(acc_ref[:, cut])
    k_ref[...] = turn(acc_ref[:, heads * HEAD : (heads + 1) * HEAD])
    v_ref[...] = acc_ref[:, (heads + 1) * HEAD :].astype(BF16)

    family = FORK * STEPS
    scale = 1.0 / math.sqrt(HEAD)
    row_at = iota((heads * family, family), 0) % family
    key_at = iota((heads * family, family), 1)
    own_mask = (row_at // STEPS == key_at // STEPS) & (row_at >= key_at)

    @pl.loop(0, PARENTS_HERE)
    def _(j):
        at = pl.ds(pl.multiple_of(j * family, family), family)
        q = jnp.concatenate([q_ref[at, h * HEAD : (h + 1) * HEAD] for h in range(heads)], axis=0)
        own = jnp.where(own_mask, mm_nt(q, k_ref[at, :]) * scale, -jnp.inf)
        own_top = jnp.max(own, axis=1, keepdims=True)
        own_weight = jnp.exp(own - own_top)
        own_total = jnp.sum(own_weight, axis=1, keepdims=True)
        own_mix = mm(own_weight.astype(BF16), v_ref[at, :])
        length = info_ref[j, MOST_PAGES]
        for n in range(1, MOST_PAGES + 1):

            @pl.when(length == n)
            def _(n=n):
                ids = [info_ref[j, i] for i in range(n)]
                keys = jnp.concatenate([pool_ref[i, 0] for i in ids], axis=0)
                values = jnp.concatenate([pool_ref[i, 1] for i in ids], axis=0)
                path = mm_nt(q, keys) * scale
                path_top = jnp.max(path, axis=1, keepdims=True)
                weight = jnp.exp(path - path_top)
                path_total = jnp.sum(weight, axis=1, keepdims=True)
                path_mix = mm(weight.astype(BF16), values)
                top = jnp.maximum(path_top, own_top)
                path_factor = jnp.exp(path_top - top)
                own_factor = jnp.exp(own_top - top)
                both = path_mix * path_factor + own_mix * own_factor
                out = both / (path_total * path_factor + own_total * own_factor)
                out = out.astype(BF16)
                for h in range(heads):
                    o_ref[at, h * HEAD : (h + 1) * HEAD] = out[h * family : (h + 1) * family]

    out_ref[...] = mm_tn(back_ref[...], o_ref[...]).astype(BF16)


def attend(order, info, sums, low, high, gain, wq, wk, wv, before, cos, sin, pool, back):
    rows, columns = before.shape
    part = low.shape[1]
    wide = back.shape[1]

    def whole(a):
        return pl.BlockSpec(a.shape, lambda i, order, info: (0,) * a.ndim)

    return pl.pallas_call(
        functools.partial(attend_kernel, wq.shape[0]),
        out_shape=jax.ShapeDtypeStruct((wide, wq.shape[1]), BF16),
        grid_spec=pltpu.PrefetchScalarGridSpec(
            num_scalar_prefetch=2,
            grid=(1,),
            in_specs=[whole(a) for a in (sums, low, high)]
            + [pl.BlockSpec((1, 1, part), lambda i, order, info: (order[0], 0, 0))]
            + [
                pl.BlockSpec((part, w.shape[1]), lambda i, order, info: (order[0], 0))
                for w in (wq, wk, wv)
            ]
            + [whole(a) for a in (before, cos, sin, pool, back)],
            out_specs=pl.BlockSpec((wide, wq.shape[1]), lambda i, order, info: (0, 0)),
            scratch_shapes=[
                pltpu.VMEM((rows, columns), F32),
                pltpu.VMEM((rows, part), BF16),
                pltpu.VMEM((part, 2 * HEAD), BF16),
                pltpu.VMEM((rows, wq.shape[1]), BF16),
                pltpu.VMEM((rows, HEAD), BF16),
                pltpu.VMEM((rows, HEAD), BF16),
                pltpu.VMEM((rows, wq.shape[1]), BF16),
            ],
        ),
        compiler_params=pltpu.CompilerParams(vmem_limit_bytes=48 * 2**20),
        cost_estimate=pl.CostEstimate(
            flops=2 * rows * part * columns * 6, bytes_accessed=2 * part * columns, transcendentals=0
        ),
    )(order, info, sums, low, high, gain, wq, wk, wv, before, cos, sin, pool, back)


def moves(dy, dz):
    return [(t, ((t // 2 + dy) % 4) * 2 + (t + dz) % 2) for t in range(8)]


def after_route(slots, groups, arrays, routed):
    (norm_gain, wq, wk, wv, kv_pool) = arrays
    send, to_hot, from_hot, info = routed
    rows = from_hot.shape[0]
    wide, width = send.shape
    team = lax.axis_size("tensor")
    came = lax.all_to_all(send.reshape(groups, wide // groups, width), "sample", 0, 0)
    mine, sums = pick_and_sum(from_hot, came.reshape(wide, width), team)

    def shift(block, dy, dz):
        return lax.ppermute(block, "tensor", moves(dy, dz))

    t = lax.axis_index("tensor")

    def order(*keys):
        places = [((t // 2 + dy) % 4) * 2 + (t + dz) % 2 for dy, dz in keys]
        return jnp.stack(places).astype(jnp.int32)

    gain = norm_gain.reshape(team, 1, -1)

    sums = lax.all_to_all(sums, "tensor", 0, 0)
    b30, b10, b01, sums = lax.optimization_barrier(
        (shift(mine, 1, 0), shift(mine, -1, 0), shift(mine, 0, 1), sums)
    )
    second = (shift(b30, 1, 0), shift(b01, -1, 0), shift(b30, 0, 1))
    acc = project(
        order((0, 0), (3, 0), (1, 0), (0, 1)), sums, [mine, b30, b10, b01], gain, wq, wk, wv
    )
    b20, b11, b31, acc = lax.optimization_barrier((*second, acc))
    half = rows // 2
    low, high = shift(b31[:half], 1, 0), shift(b11[half:], -1, 0)
    acc = project(order((2, 0), (1, 1), (3, 1)), sums, [b20, b11, b31], gain, wq, wk, wv, acc)
    low, high, acc = lax.optimization_barrier((low, high, acc))

    pages = info[:, MOST_PAGES]
    positions = (
        jnp.repeat(pages * PAGE, FORK * STEPS)
        + jnp.tile(jnp.arange(STEPS, dtype=jnp.int32), PARENTS_HERE * FORK)
    ).astype(F32)
    inverse = ROPE_THETA ** (-2.0 * jnp.arange(HEAD // 2, dtype=F32) / HEAD)
    angles = positions[:, None] * inverse[None, :]
    cos, sin = jnp.cos(angles), jnp.sin(angles)
    cos = jnp.concatenate([cos, cos], axis=1)
    sin = jnp.concatenate([-sin, sin], axis=1)
    back = attend(
        order((2, 1)), info, sums, low, high, gain, wq, wk, wv, acc, cos, sin, kv_pool, from_hot
    )
    home = lax.all_to_all(back.reshape(groups, wide // groups, back.shape[1]), "sample", 0, 0)
    return pick_rows(pick_tn_kernel, to_hot, home.reshape(wide, back.shape[1]), rows)


def local(
    branch_tokens,
    norm_gain,
    query_weight,
    key_weight,
    value_weight,
    kv_pool,
    parent_owner,
    parent_pages,
    page_table,
    child_parent,
):
    groups = lax.axis_size("sample")
    me = lax.axis_index("sample").astype(jnp.int32).reshape(1)
    tables = (child_parent, parent_owner, parent_pages, page_table)
    arrays = (norm_gain, query_weight, key_weight, value_weight, kv_pool)
    *routed, most = route(SLOTS, groups, me, *tables, branch_tokens)

    def usual():
        return after_route(SLOTS, groups, arrays, routed)

    def crowded():
        slots = branch_tokens.shape[0] // STEPS
        *wider, _ = route(slots, groups, me, *tables, branch_tokens)
        return after_route(slots, groups, arrays, wider)

    return lax.cond(most[0] <= SLOTS, usual, crowded)


def solution(mesh):
    return jax.shard_map(
        local,
        mesh=mesh,
        in_specs=(
            P("sample", "tensor"),
            P(),
            P(None, "tensor"),
            P(None, "tensor"),
            P(None, "tensor"),
            P("sample", None, None, "tensor"),
            P(),
            P(),
            P(),
            P(),
        ),
        out_specs=P("sample", "tensor"),
        check_vma=False,
    )
```

```python
import functools
import math

import jax
import jax.numpy as jnp
from jax import lax
from jax.experimental import pallas as pl
from jax.experimental.pallas import tpu as pltpu
from jax.sharding import PartitionSpec as P

HEAD = 128
PAGE = 128
STEPS = 4
FORK = 8
PARENTS_HERE = 8
MOST_PAGES = 5
ROPE_THETA = 10000.0
EPSILON = 1e-06
SLOTS = 10
BACK_SLOTS = 14

BF16 = jnp.bfloat16
F32 = jnp.float32


def iota(shape, dim):
    return lax.broadcasted_iota(jnp.int32, shape, dim)


def one(mask):
    return jnp.where(mask, 1.0, 0.0).astype(BF16)


def mm(a, b):
    return lax.dot_general(a, b, (((1,), (0,)), ((), ())), preferred_element_type=F32)


def mm_nt(a, b):
    return lax.dot_general(a, b, (((1,), (1,)), ((), ())), preferred_element_type=F32)


def mm_tn(a, b):
    return lax.dot_general(a, b, (((0,), (0,)), ((), ())), preferred_element_type=F32)


def leave_kernel(slots, limits, me_ref, child_ref, owner_ref, own_ref, other_ref, fits_ref, mask_ref):
    groups = mask_ref.shape[0]
    me = me_ref[0]
    core = lax.rem(me, 2)
    children = child_ref.shape[1]
    parents = owner_ref.shape[1]
    rows = own_ref.shape[1]
    here = rows // STEPS
    parent_hot = one(iota((parents, children), 0) == child_ref[...])
    owner = jnp.broadcast_to(owner_ref[...].astype(F32), (16, parents)).astype(BF16)
    owner_of = mm(owner, parent_hot)[0:1].astype(jnp.int32)
    mask = jnp.where(iota((groups, children), 0) == owner_of, 1.0, 0.0)
    mask_ref[...] = mask
    column, child = iota((children, 128), 1), iota((children, 128), 0)
    counted = (column == child // here) | (column == groups + child // (2 * here))
    counts = mm(mask.astype(BF16), one(counted))
    limit = jnp.where(iota(counts.shape, 1) < groups, limits[0], limits[1])
    fits_ref[0] = jnp.min(jnp.where(counts.astype(jnp.int32) <= limit, 1, 0))

    chip = lax.div(me, 2)
    mask = mask_ref[:, pl.ds(pl.multiple_of(chip * 2 * here, 2 * here), 2 * here)]
    ahead = mm(mask.astype(BF16), one(iota((128, 128), 0) < iota((128, 128), 1)))
    rank = jnp.sum(mask * ahead, axis=0, keepdims=True).astype(jnp.int32)
    owner = jnp.sum(mask * iota(mask.shape, 0).astype(F32), axis=0, keepdims=True)
    keep = jnp.where(rank % 2 == core, 1.0, 0.0)
    turn = (rank // 2).astype(F32)
    at = iota((16, 2 * here), 0)
    facts = jnp.where(at == 0, owner, jnp.where(at == 1, turn, keep)).astype(BF16)
    for ref, side in ((own_ref, core), (other_ref, 1 - core)):
        grow = one(iota((2 * here, rows), 0) == side * here + iota((2 * here, rows), 1) // STEPS)
        of_row = mm(facts, grow)
        target = of_row[0:1] * (slots * STEPS) + of_row[1:2] * STEPS
        target = target.astype(jnp.int32) + iota((1, rows), 1) % STEPS
        target = jnp.where(of_row[2:3] > 0.5, target, -1)
        ref[...] = one(iota(ref.shape, 0) == target)


def leave(slots, back_slots, groups, me, child_parent, parent_owner, rows):
    vmem = pl.BlockSpec(memory_space=pltpu.VMEM)
    smem = pl.BlockSpec(memory_space=pltpu.SMEM)
    hot = jax.ShapeDtypeStruct((groups * slots * STEPS, rows), BF16)
    return pl.pallas_call(
        functools.partial(leave_kernel, slots, (back_slots, 2 * slots)),
        out_shape=(hot, hot, jax.ShapeDtypeStruct((1,), jnp.int32)),
        in_specs=[smem, vmem, vmem],
        out_specs=(vmem, vmem, smem),
        scratch_shapes=[pltpu.VMEM((groups, child_parent.shape[0]), F32)],
        compiler_params=pltpu.CompilerParams(vmem_limit_bytes=32 * 2**20),
        cost_estimate=pl.CostEstimate(flops=10**9, bytes_accessed=2**20, transcendentals=0),
    )(me, child_parent.reshape(1, -1), parent_owner.reshape(1, -1))


def arrive_kernel(
    slots,
    back_slots,
    me_ref,
    child_ref,
    owner_ref,
    pages_ref,
    table_ref,
    from_ref,
    back_ref,
    home_ref,
    info_ref,
):
    groups = home_ref.shape[0] // (back_slots * STEPS)
    me = me_ref[0]
    children = child_ref.shape[1]
    parents = owner_ref.shape[1]
    rows = from_ref.shape[0]
    here = rows // STEPS
    child = child_ref[...]
    owner = owner_ref[...]
    parent_hot = one(iota((parents, children), 0) == child)
    owner_of = mm(jnp.broadcast_to(owner.astype(F32), (16, parents)).astype(BF16), parent_hot)[0:1]
    owner_mask = one(iota((groups, children), 0) == owner_of.astype(jnp.int32))
    pick = one(iota((children, rows), 0) == me * here + iota((children, rows), 1) // STEPS)
    home_mask = mm(owner_mask, pick)
    before = one(
        (iota((rows, rows), 0) // STEPS < iota((rows, rows), 1) // STEPS)
        & (iota((rows, rows), 0) % STEPS == 0)
    )
    rank = mm(home_mask.astype(BF16), before)
    target = jnp.sum(
        home_mask * (iota((groups, rows), 0).astype(F32) * (back_slots * STEPS) + rank * STEPS),
        axis=0,
        keepdims=True,
    ).astype(jnp.int32) + iota((1, rows), 1) % STEPS
    home_ref[...] = one(iota(home_ref.shape, 0) == target)

    mine_parent = owner == me
    tri_block = one(iota((128, 128), 0) < iota((128, 128), 1))
    tri_home = one(
        (iota((128, 128), 0) < iota((128, 128), 1))
        & (iota((128, 128), 0) // here == iota((128, 128), 1) // here)
    )
    parent_rank = mm(one(jnp.broadcast_to(mine_parent, (16, parents))), tri_block)
    parent_rank = parent_rank[0:1].astype(jnp.int32)
    mine_hot = (iota((PARENTS_HERE, parents), 0) == parent_rank) & mine_parent
    pages = jnp.sum(jnp.where(mine_hot, pages_ref[...], 0), axis=1, keepdims=True)
    mine_hot = one(mine_hot)
    table = mm(mine_hot, table_ref[...].astype(F32).astype(BF16)).astype(jnp.int32)
    info_ref[...] = jnp.where(iota((PARENTS_HERE, 8), 1) == MOST_PAGES, pages, table)
    member = mm(mine_hot, parent_hot)
    carry = jnp.zeros((PARENTS_HERE, 1), F32)
    places, spots, back_spots = [], [], []
    for block in range(children // 128):
        part = member[:, block * 128 : (block + 1) * 128]
        ahead = mm(part.astype(BF16), tri_block) + carry
        carry = carry + jnp.sum(part, axis=1, keepdims=True)
        is_mine = jnp.sum(part, axis=0, keepdims=True)
        place = jnp.sum(
            part * (iota((PARENTS_HERE, 128), 0).astype(F32) * FORK + ahead), axis=0, keepdims=True
        ).astype(jnp.int32)
        is_mine_wide = jnp.broadcast_to(is_mine, (16, 128)).astype(BF16)
        in_chip = mm(is_mine_wide, tri_block)[0:1].astype(jnp.int32)
        in_home = mm(is_mine_wide, tri_home)[0:1].astype(jnp.int32)
        number = block * 128 + iota((1, 128), 1)
        sender = number // (2 * here) * 2 + in_chip % 2
        spot = sender * slots + in_chip // 2
        back_spot = number // here * back_slots + in_home
        for found, value in ((places, place), (spots, spot), (back_spots, back_spot)):
            found.append(jnp.where(is_mine > 0.5, value, -1))
    place_hot = one(iota((here, children), 0) == jnp.concatenate(places, axis=1))
    grow_rows = one(iota((rows, here), 0) // STEPS == iota((rows, here), 1))
    for ref, found, count in ((from_ref, spots, slots), (back_ref, back_spots, back_slots)):
        deep, wide = groups * count, groups * count * STEPS
        spot_hot = one(iota((deep, children), 0) == jnp.concatenate(found, axis=1))
        by_child = mm_nt(place_hot, spot_hot).astype(BF16)
        grow_columns = one(iota((deep, wide), 0) == iota((deep, wide), 1) // STEPS)
        by_row = mm(mm(grow_rows, by_child).astype(BF16), grow_columns)
        same_step = iota((rows, wide), 0) % STEPS == iota((rows, wide), 1) % STEPS
        ref[...] = jnp.where(same_step, by_row, 0.0).astype(BF16)


def arrive(
    slots, back_slots, groups, me, child_parent, parent_owner, parent_pages, page_table, rows
):
    vmem = pl.BlockSpec(memory_space=pltpu.VMEM)
    smem = pl.BlockSpec(memory_space=pltpu.SMEM)
    return pl.pallas_call(
        functools.partial(arrive_kernel, slots, back_slots),
        out_shape=(
            jax.ShapeDtypeStruct((rows, groups * slots * STEPS), BF16),
            jax.ShapeDtypeStruct((rows, groups * back_slots * STEPS), BF16),
            jax.ShapeDtypeStruct((groups * back_slots * STEPS, rows), BF16),
            jax.ShapeDtypeStruct((PARENTS_HERE, 8), jnp.int32),
        ),
        in_specs=[smem] + [vmem] * 4,
        out_specs=(vmem, vmem, vmem, vmem),
        compiler_params=pltpu.CompilerParams(vmem_limit_bytes=32 * 2**20),
        cost_estimate=pl.CostEstimate(flops=2 * 10**9, bytes_accessed=2**20, transcendentals=0),
    )(
        me,
        child_parent.reshape(1, -1),
        parent_owner.reshape(1, -1),
        parent_pages.reshape(1, -1),
        jnp.pad(page_table, ((0, 0), (0, 8 - page_table.shape[1]))),
    )


def fill_kernel(own_hot_ref, other_hot_ref, own_ref, other_ref, out_ref):
    filled = mm(own_hot_ref[...], own_ref[...]) + mm(other_hot_ref[...], other_ref[...])
    out_ref[...] = filled.astype(BF16)


def fill_slots(own_hot, other_hot, own, other):
    vmem = pl.BlockSpec(memory_space=pltpu.VMEM)
    return pl.pallas_call(
        fill_kernel,
        out_shape=jax.ShapeDtypeStruct((own_hot.shape[0], own.shape[1]), BF16),
        in_specs=[vmem] * 4,
        out_specs=vmem,
        compiler_params=pltpu.CompilerParams(vmem_limit_bytes=48 * 2**20),
    )(own_hot, other_hot, own, other)


def settle_kernel(hot_ref, rows_ref, out_ref, buffer_ref, sems):
    parts = sems.shape[0]
    size = buffer_ref.shape[0] // parts
    copies = []
    for i in range(parts):
        cut = slice(i * size, (i + 1) * size)
        buffer_ref[cut] = mm_tn(hot_ref[:, cut], rows_ref[...]).astype(BF16)
        copies.append(pltpu.make_async_copy(buffer_ref.at[cut], out_ref.at[cut], sems.at[i]))
        copies[-1].start()
    for copy in copies:
        copy.wait()


def settle(hot, rows, count):
    vmem = pl.BlockSpec(memory_space=pltpu.VMEM)
    return pl.pallas_call(
        settle_kernel,
        out_shape=jax.ShapeDtypeStruct((count, rows.shape[1]), BF16),
        in_specs=[vmem, vmem],
        out_specs=pl.BlockSpec(memory_space=pltpu.HBM),
        scratch_shapes=[
            pltpu.VMEM((count, rows.shape[1]), BF16),
            pltpu.SemaphoreType.DMA((2,)),
        ],
        compiler_params=pltpu.CompilerParams(vmem_limit_bytes=48 * 2**20),
    )(hot, rows)


def pick_sum_kernel(hot_ref, rows_ref, out_ref, sum_ref):
    x = mm(hot_ref[...], rows_ref[...])
    out_ref[...] = x.astype(BF16)
    total = jnp.sum(x * x, axis=1, keepdims=True)
    total = jnp.broadcast_to(total, (total.shape[0], 128)).T
    sum_ref[...] = jnp.broadcast_to(total[0:1], sum_ref.shape[:1] + total.shape[1:])[:, None, :]


def pick_and_sum(hot, rows, copies):
    vmem = pl.BlockSpec(memory_space=pltpu.VMEM)
    count = hot.shape[0]
    return pl.pallas_call(
        pick_sum_kernel,
        out_shape=(
            jax.ShapeDtypeStruct((count, rows.shape[1]), BF16),
            jax.ShapeDtypeStruct((copies, 1, count), F32),
        ),
        in_specs=[vmem, vmem],
        out_specs=(vmem, vmem),
        compiler_params=pltpu.CompilerParams(vmem_limit_bytes=48 * 2**20),
    )(hot, rows)


def row_scale(sum_ref, width):
    total = jnp.sum(sum_ref[:, 0, :], axis=0, keepdims=True)
    scale = lax.rsqrt(total * (1.0 / width) + EPSILON)
    return jnp.broadcast_to(scale, (128, scale.shape[1])).T


def normed(x, scale, gain):
    return (x.astype(F32) * scale * gain.astype(F32)).astype(BF16)


def add_products(acc, x, wq_ref, wk_ref, wv_ref, wkv_ref):
    wide = wq_ref.shape[1]
    wkv_ref[:, :HEAD] = wk_ref[...]
    wkv_ref[:, HEAD:] = wv_ref[...]
    acc[:, :wide] += mm(x, wq_ref[...])
    acc[:, wide:] += mm(x, wkv_ref[...])


def project_kernel(width, count, first, order_ref, sum_ref, *refs):
    blocks = refs[:count]
    gain_ref, wq_ref, wk_ref, wv_ref = refs[count : count + 4]
    before = None if first else refs[count + 4]
    acc_ref, x_ref, scale_ref, wkv_ref = refs[-4:]
    step = pl.program_id(0)

    @pl.when(step == 0)
    def _():
        scale_ref[...] = row_scale(sum_ref, width)
        acc_ref[...] = jnp.zeros_like(acc_ref) if first else before[...]

    for i, block in enumerate(blocks):

        @pl.when(step == i)
        def _(block=block):
            x_ref[...] = normed(block[...], scale_ref[:, 0:1], gain_ref[0])

    add_products(acc_ref, x_ref[...], wq_ref, wk_ref, wv_ref, wkv_ref)


def project(order, sums, blocks, gain, wq, wk, wv, before=None):
    rows, part = blocks[0].shape
    columns = wq.shape[1] + wk.shape[1] + wv.shape[1]
    count = len(blocks)

    def whole(a):
        return pl.BlockSpec(a.shape, lambda i, order: (0,) * a.ndim)

    extra = [] if before is None else [before]
    return pl.pallas_call(
        functools.partial(project_kernel, wq.shape[0], count, before is None),
        out_shape=jax.ShapeDtypeStruct((rows, columns), F32),
        grid_spec=pltpu.PrefetchScalarGridSpec(
            num_scalar_prefetch=1,
            grid=(count,),
            in_specs=[whole(sums)]
            + [whole(b) for b in blocks]
            + [pl.BlockSpec((1, 1, part), lambda i, order: (order[i], 0, 0))]
            + [
                pl.BlockSpec((part, w.shape[1]), lambda i, order: (order[i], 0))
                for w in (wq, wk, wv)
            ]
            + [whole(a) for a in extra],
            out_specs=pl.BlockSpec((rows, columns), lambda i, order: (0, 0)),
            scratch_shapes=[
                pltpu.VMEM((rows, part), BF16),
                pltpu.VMEM((rows, 128), F32),
                pltpu.VMEM((part, 2 * HEAD), BF16),
            ],
        ),
        compiler_params=pltpu.CompilerParams(vmem_limit_bytes=32 * 2**20),
        cost_estimate=pl.CostEstimate(
            flops=2 * rows * part * count * columns * 3,
            bytes_accessed=2 * part * count * columns,
            transcendentals=0,
        ),
    )(order, sums, *blocks, gain, wq, wk, wv, *extra)


def attend_kernel(
    width,
    order_ref,
    info_ref,
    sum_ref,
    low_ref,
    high_ref,
    gain_ref,
    wq_ref,
    wk_ref,
    wv_ref,
    before_ref,
    cos_ref,
    sin_ref,
    pool_ref,
    back_ref,
    out_ref,
    acc_ref,
    x_ref,
    wkv_ref,
    q_ref,
    k_ref,
    v_ref,
    o_ref,
):
    scale = row_scale(sum_ref, width)[:, 0:1]
    half = low_ref.shape[0]
    x_ref[:half] = normed(low_ref[...], scale[:half], gain_ref[0])
    x_ref[half:] = normed(high_ref[...], scale[half:], gain_ref[0])
    acc_ref[...] = before_ref[...]
    add_products(acc_ref, x_ref[...], wq_ref, wk_ref, wv_ref, wkv_ref)

    cos = cos_ref[...]
    sin = sin_ref[...]

    def turn(part):
        return (part * cos + pltpu.roll(part, HEAD // 2, 1) * sin).astype(BF16)

    heads = wq_ref.shape[1] // HEAD
    for h in range(heads):
        cut = slice(h * HEAD, (h + 1) * HEAD)
        q_ref[:, cut] = turn(acc_ref[:, cut])
    k_ref[...] = turn(acc_ref[:, heads * HEAD : (heads + 1) * HEAD])
    v_ref[...] = acc_ref[:, (heads + 1) * HEAD :].astype(BF16)

    family = FORK * STEPS
    scale = 1.0 / math.sqrt(HEAD)
    row_at = iota((heads * family, family), 0) % family
    key_at = iota((heads * family, family), 1)
    own_mask = (row_at // STEPS == key_at // STEPS) & (row_at >= key_at)

    @pl.loop(0, PARENTS_HERE)
    def _(j):
        at = pl.ds(pl.multiple_of(j * family, family), family)
        q = jnp.concatenate([q_ref[at, h * HEAD : (h + 1) * HEAD] for h in range(heads)], axis=0)
        own = jnp.where(own_mask, mm_nt(q, k_ref[at, :]) * scale, -jnp.inf)
        own_top = jnp.max(own, axis=1, keepdims=True)
        own_weight = jnp.exp(own - own_top)
        own_total = jnp.sum(own_weight, axis=1, keepdims=True)
        own_mix = mm(own_weight.astype(BF16), v_ref[at, :])
        length = info_ref[j, MOST_PAGES]
        for n in range(1, MOST_PAGES + 1):

            @pl.when(length == n)
            def _(n=n):
                ids = [info_ref[j, i] for i in range(n)]
                keys = jnp.concatenate([pool_ref[i, 0] for i in ids], axis=0)
                values = jnp.concatenate([pool_ref[i, 1] for i in ids], axis=0)
                path = mm_nt(q, keys) * scale
                path_top = jnp.max(path, axis=1, keepdims=True)
                weight = jnp.exp(path - path_top)
                path_total = jnp.sum(weight, axis=1, keepdims=True)
                path_mix = mm(weight.astype(BF16), values)
                top = jnp.maximum(path_top, own_top)
                path_factor = jnp.exp(path_top - top)
                own_factor = jnp.exp(own_top - top)
                both = path_mix * path_factor + own_mix * own_factor
                out = both / (path_total * path_factor + own_total * own_factor)
                out = out.astype(BF16)
                for h in range(heads):
                    o_ref[at, h * HEAD : (h + 1) * HEAD] = out[h * family : (h + 1) * family]

    out_ref[...] = mm_tn(back_ref[...], o_ref[...]).astype(BF16)


def attend(order, info, sums, low, high, gain, wq, wk, wv, before, cos, sin, pool, back):
    rows, columns = before.shape
    part = low.shape[1]
    wide = back.shape[1]

    def whole(a):
        return pl.BlockSpec(a.shape, lambda i, order, info: (0,) * a.ndim)

    return pl.pallas_call(
        functools.partial(attend_kernel, 8 * wq.shape[0]),
        out_shape=jax.ShapeDtypeStruct((wide, wq.shape[1]), BF16),
        grid_spec=pltpu.PrefetchScalarGridSpec(
            num_scalar_prefetch=2,
            grid=(1,),
            in_specs=[whole(a) for a in (sums, low, high)]
            + [pl.BlockSpec((1, 1, part), lambda i, order, info: (order[0], 0, 0))]
            + [whole(a) for a in (wq, wk, wv, before, cos, sin, pool, back)],
            out_specs=pl.BlockSpec((wide, wq.shape[1]), lambda i, order, info: (0, 0)),
            scratch_shapes=[
                pltpu.VMEM((rows, columns), F32),
                pltpu.VMEM((rows, part), BF16),
                pltpu.VMEM((part, 2 * HEAD), BF16),
                pltpu.VMEM((rows, wq.shape[1]), BF16),
                pltpu.VMEM((rows, HEAD), BF16),
                pltpu.VMEM((rows, HEAD), BF16),
                pltpu.VMEM((rows, wq.shape[1]), BF16),
            ],
        ),
        compiler_params=pltpu.CompilerParams(vmem_limit_bytes=48 * 2**20),
        cost_estimate=pl.CostEstimate(
            flops=2 * rows * part * columns * 6, bytes_accessed=2 * part * columns, transcendentals=0
        ),
    )(order, info, sums, low, high, gain, wq, wk, wv, before, cos, sin, pool, back)


def moves(dy, dz):
    return [(t, ((t // 2 + dy) % 4) * 2 + (t + dz) % 2) for t in range(8)]


def after_leave(slots, back_slots, groups, me, tables, arrays, send):
    (norm_gain, wq, wk, wv, kv_pool) = arrays
    wide, width = send.shape
    rows = PARENTS_HERE * FORK * STEPS
    team = lax.axis_size("tensor")
    t = lax.axis_index("tensor")
    came = lax.all_to_all(send.reshape(groups, wide // groups, width), "sample", 0, 0)
    from_hot, back_hot, home_hot, info = arrive(slots, back_slots, groups, me, *tables, rows)

    def place(dy, dz):
        return ((t // 2 + dy) % 4) * 2 + (t + dz) % 2

    def order(*keys):
        return jnp.stack([place(*key) for key in keys]).astype(jnp.int32)

    last = [lax.dynamic_slice_in_dim(w, place(2, 1) * width, width) for w in (wq, wk, wv)]
    gain = norm_gain.reshape(team, 1, -1)

    pages = info[:, MOST_PAGES]
    positions = (
        jnp.repeat(pages * PAGE, FORK * STEPS)
        + jnp.tile(jnp.arange(STEPS, dtype=jnp.int32), PARENTS_HERE * FORK)
    ).astype(F32)
    inverse = ROPE_THETA ** (-2.0 * jnp.arange(HEAD // 2, dtype=F32) / HEAD)
    angles = positions[:, None] * inverse[None, :]
    cos, sin = jnp.cos(angles), jnp.sin(angles)
    cos = jnp.concatenate([cos, cos], axis=1)
    sin = jnp.concatenate([-sin, sin], axis=1)
    came, from_hot, back_hot, home_hot, info, cos, sin, gain, *last = lax.optimization_barrier(
        (came, from_hot, back_hot, home_hot, info, cos, sin, gain, *last)
    )
    mine, sums = pick_and_sum(from_hot, came.reshape(wide, width), team)

    def shift(block, dy, dz):
        return lax.ppermute(block, "tensor", moves(dy, dz))

    sums = lax.all_to_all(sums, "tensor", 0, 0)
    b30, b10, b01 = lax.optimization_barrier(
        (shift(mine, 1, 0), shift(mine, -1, 0), shift(mine, 0, 1))
    )
    second = (shift(b30, 1, 0), shift(b01, -1, 0), shift(b30, 0, 1))
    acc = project(
        order((0, 0), (3, 0), (1, 0), (0, 1)), sums, [mine, b30, b10, b01], gain, wq, wk, wv
    )
    b20, b11, b31, acc = lax.optimization_barrier((*second, acc))
    half = rows // 2
    low, high = shift(b31[:half], 1, 0), shift(b11[half:], -1, 0)
    acc = project(order((2, 0), (1, 1), (3, 1)), sums, [b20, b11, b31], gain, wq, wk, wv, acc)
    low, high, acc = lax.optimization_barrier((low, high, acc))
    back = attend(
        order((2, 1)), info, sums, low, high, gain, *last, acc, cos, sin, kv_pool, back_hot
    )
    home = lax.all_to_all(back.reshape(groups, -1, back.shape[1]), "sample", 0, 0)
    return settle(home_hot, home.reshape(-1, back.shape[1]), rows)


def local(
    branch_tokens,
    norm_gain,
    query_weight,
    key_weight,
    value_weight,
    kv_pool,
    parent_owner,
    parent_pages,
    page_table,
    child_parent,
):
    groups = lax.axis_size("sample")
    rows = branch_tokens.shape[0]
    me = lax.axis_index("sample").astype(jnp.int32).reshape(1)
    tables = (child_parent, parent_owner, parent_pages, page_table)
    arrays = (norm_gain, query_weight, key_weight, value_weight, kv_pool)
    other = lax.ppermute(branch_tokens, "sample", [(i, i ^ 1) for i in range(groups)])
    own_hot, other_hot, fits = leave(SLOTS, BACK_SLOTS, groups, me, *tables[:2], rows)
    other, own_hot, other_hot, fits = lax.optimization_barrier((other, own_hot, other_hot, fits))
    send = fill_slots(own_hot, other_hot, branch_tokens, other)

    def usual():
        return after_leave(SLOTS, BACK_SLOTS, groups, me, tables, arrays, send)

    def crowded():
        most = rows // STEPS
        own, others, _ = leave(most // 2, most, groups, me, *tables[:2], rows)
        wider = fill_slots(own, others, branch_tokens, other)
        return after_leave(most // 2, most, groups, me, tables, arrays, wider)

    return lax.cond(fits[0] == 1, usual, crowded)


def solution(mesh):
    return jax.shard_map(
        local,
        mesh=mesh,
        in_specs=(
            P("sample", "tensor"),
            P(),
            P(None, "tensor"),
            P(None, "tensor"),
            P(None, "tensor"),
            P("sample", None, None, "tensor"),
            P(),
            P(),
            P(),
            P(),
        ),
        out_specs=P("sample", "tensor"),
        check_vma=False,
    )
```

```python
import functools
import math

import jax
import jax.numpy as jnp
from jax import lax
from jax.experimental import pallas as pl
from jax.experimental.pallas import tpu as pltpu
from jax.sharding import PartitionSpec as P

HEAD = 128
PAGE = 128
STEPS = 4
FORK = 8
PARENTS_HERE = 8
MOST_PAGES = 5
ROPE_THETA = 10000.0
EPSILON = 1e-06
SLOTS = 10
BACK_SLOTS = 14

BF16 = jnp.bfloat16
F32 = jnp.float32


def iota(shape, dim):
    return lax.broadcasted_iota(jnp.int32, shape, dim)


def one(mask):
    return jnp.where(mask, 1.0, 0.0).astype(BF16)


def mm(a, b):
    return lax.dot_general(a, b, (((1,), (0,)), ((), ())), preferred_element_type=F32)


def mm_nt(a, b):
    return lax.dot_general(a, b, (((1,), (1,)), ((), ())), preferred_element_type=F32)


def mm_tn(a, b):
    return lax.dot_general(a, b, (((0,), (0,)), ((), ())), preferred_element_type=F32)


def leave_kernel(slots, limits, me_ref, child_ref, owner_ref, own_ref, other_ref, fits_ref, mask_ref):
    groups = mask_ref.shape[0]
    me = me_ref[0]
    core = lax.rem(me, 2)
    children = child_ref.shape[1]
    parents = owner_ref.shape[1]
    rows = own_ref.shape[1]
    here = rows // STEPS
    parent_hot = one(iota((parents, children), 0) == child_ref[...])
    owner = jnp.broadcast_to(owner_ref[...].astype(F32), (16, parents)).astype(BF16)
    owner_of = mm(owner, parent_hot)[0:1].astype(jnp.int32)
    mask = jnp.where(iota((groups, children), 0) == owner_of, 1.0, 0.0)
    mask_ref[...] = mask
    column, child = iota((children, 128), 1), iota((children, 128), 0)
    counted = (column == child // here) | (column == groups + child // (2 * here))
    counts = mm(mask.astype(BF16), one(counted))
    limit = jnp.where(iota(counts.shape, 1) < groups, limits[0], limits[1])
    fits_ref[0] = jnp.min(jnp.where(counts.astype(jnp.int32) <= limit, 1, 0))

    chip = lax.div(me, 2)
    mask = mask_ref[:, pl.ds(pl.multiple_of(chip * 2 * here, 2 * here), 2 * here)]
    ahead = mm(mask.astype(BF16), one(iota((128, 128), 0) < iota((128, 128), 1)))
    rank = jnp.sum(mask * ahead, axis=0, keepdims=True).astype(jnp.int32)
    owner = jnp.sum(mask * iota(mask.shape, 0).astype(F32), axis=0, keepdims=True)
    keep = jnp.where(rank % 2 == core, 1.0, 0.0)
    turn = (rank // 2).astype(F32)
    at = iota((16, 2 * here), 0)
    facts = jnp.where(at == 0, owner, jnp.where(at == 1, turn, keep)).astype(BF16)
    for ref, side in ((own_ref, core), (other_ref, 1 - core)):
        grow = one(iota((2 * here, rows), 0) == side * here + iota((2 * here, rows), 1) // STEPS)
        of_row = mm(facts, grow)
        target = of_row[0:1] * (slots * STEPS) + of_row[1:2] * STEPS
        target = target.astype(jnp.int32) + iota((1, rows), 1) % STEPS
        target = jnp.where(of_row[2:3] > 0.5, target, -1)
        ref[...] = one(iota(ref.shape, 0) == target)


def leave(slots, back_slots, groups, me, child_parent, parent_owner, rows):
    vmem = pl.BlockSpec(memory_space=pltpu.VMEM)
    smem = pl.BlockSpec(memory_space=pltpu.SMEM)
    hot = jax.ShapeDtypeStruct((groups * slots * STEPS, rows), BF16)
    return pl.pallas_call(
        functools.partial(leave_kernel, slots, (back_slots, 2 * slots)),
        out_shape=(hot, hot, jax.ShapeDtypeStruct((1,), jnp.int32)),
        in_specs=[smem, vmem, vmem],
        out_specs=(vmem, vmem, smem),
        scratch_shapes=[pltpu.VMEM((groups, child_parent.shape[0]), F32)],
        compiler_params=pltpu.CompilerParams(vmem_limit_bytes=32 * 2**20),
        cost_estimate=pl.CostEstimate(flops=10**9, bytes_accessed=2**20, transcendentals=0),
    )(me, child_parent.reshape(1, -1), parent_owner.reshape(1, -1))


def arrive_kernel(
    slots,
    back_slots,
    me_ref,
    child_ref,
    owner_ref,
    pages_ref,
    table_ref,
    from_ref,
    back_ref,
    home_ref,
    info_ref,
):
    groups = home_ref.shape[0] // (back_slots * STEPS)
    me = me_ref[0]
    children = child_ref.shape[1]
    parents = owner_ref.shape[1]
    rows = from_ref.shape[0]
    here = rows // STEPS
    child = child_ref[...]
    owner = owner_ref[...]
    parent_hot = one(iota((parents, children), 0) == child)
    owner_of = mm(jnp.broadcast_to(owner.astype(F32), (16, parents)).astype(BF16), parent_hot)[0:1]
    owner_mask = one(iota((groups, children), 0) == owner_of.astype(jnp.int32))
    pick = one(iota((children, rows), 0) == me * here + iota((children, rows), 1) // STEPS)
    home_mask = mm(owner_mask, pick)
    before = one(
        (iota((rows, rows), 0) // STEPS < iota((rows, rows), 1) // STEPS)
        & (iota((rows, rows), 0) % STEPS == 0)
    )
    rank = mm(home_mask.astype(BF16), before)
    target = jnp.sum(
        home_mask * (iota((groups, rows), 0).astype(F32) * (back_slots * STEPS) + rank * STEPS),
        axis=0,
        keepdims=True,
    ).astype(jnp.int32) + iota((1, rows), 1) % STEPS
    home_ref[...] = one(iota(home_ref.shape, 0) == target)

    mine_parent = owner == me
    tri_block = one(iota((128, 128), 0) < iota((128, 128), 1))
    tri_home = one(
        (iota((128, 128), 0) < iota((128, 128), 1))
        & (iota((128, 128), 0) // here == iota((128, 128), 1) // here)
    )
    parent_rank = mm(one(jnp.broadcast_to(mine_parent, (16, parents))), tri_block)
    parent_rank = parent_rank[0:1].astype(jnp.int32)
    mine_hot = (iota((PARENTS_HERE, parents), 0) == parent_rank) & mine_parent
    pages = jnp.sum(jnp.where(mine_hot, pages_ref[...], 0), axis=1, keepdims=True)
    mine_hot = one(mine_hot)
    table = mm(mine_hot, table_ref[...].astype(F32).astype(BF16)).astype(jnp.int32)
    info_ref[...] = jnp.where(iota((PARENTS_HERE, 8), 1) == MOST_PAGES, pages, table)
    member = mm(mine_hot, parent_hot)
    carry = jnp.zeros((PARENTS_HERE, 1), F32)
    places, spots, back_spots = [], [], []
    for block in range(children // 128):
        part = member[:, block * 128 : (block + 1) * 128]
        ahead = mm(part.astype(BF16), tri_block) + carry
        carry = carry + jnp.sum(part, axis=1, keepdims=True)
        is_mine = jnp.sum(part, axis=0, keepdims=True)
        place = jnp.sum(
            part * (iota((PARENTS_HERE, 128), 0).astype(F32) * FORK + ahead), axis=0, keepdims=True
        ).astype(jnp.int32)
        is_mine_wide = jnp.broadcast_to(is_mine, (16, 128)).astype(BF16)
        in_chip = mm(is_mine_wide, tri_block)[0:1].astype(jnp.int32)
        in_home = mm(is_mine_wide, tri_home)[0:1].astype(jnp.int32)
        number = block * 128 + iota((1, 128), 1)
        sender = number // (2 * here) * 2 + in_chip % 2
        spot = sender * slots + in_chip // 2
        back_spot = number // here * back_slots + in_home
        for found, value in ((places, place), (spots, spot), (back_spots, back_spot)):
            found.append(jnp.where(is_mine > 0.5, value, -1))
    place_hot = one(iota((here, children), 0) == jnp.concatenate(places, axis=1))
    grow_rows = one(iota((rows, here), 0) // STEPS == iota((rows, here), 1))
    for ref, found, count in ((from_ref, spots, slots), (back_ref, back_spots, back_slots)):
        deep, wide = groups * count, groups * count * STEPS
        spot_hot = one(iota((deep, children), 0) == jnp.concatenate(found, axis=1))
        by_child = mm_nt(place_hot, spot_hot).astype(BF16)
        grow_columns = one(iota((deep, wide), 0) == iota((deep, wide), 1) // STEPS)
        by_row = mm(mm(grow_rows, by_child).astype(BF16), grow_columns)
        same_step = iota((rows, wide), 0) % STEPS == iota((rows, wide), 1) % STEPS
        ref[...] = jnp.where(same_step, by_row, 0.0).astype(BF16)


def arrive(
    slots, back_slots, groups, me, child_parent, parent_owner, parent_pages, page_table, rows
):
    vmem = pl.BlockSpec(memory_space=pltpu.VMEM)
    smem = pl.BlockSpec(memory_space=pltpu.SMEM)
    return pl.pallas_call(
        functools.partial(arrive_kernel, slots, back_slots),
        out_shape=(
            jax.ShapeDtypeStruct((rows, groups * slots * STEPS), BF16),
            jax.ShapeDtypeStruct((rows, groups * back_slots * STEPS), BF16),
            jax.ShapeDtypeStruct((groups * back_slots * STEPS, rows), BF16),
            jax.ShapeDtypeStruct((PARENTS_HERE, 8), jnp.int32),
        ),
        in_specs=[smem] + [vmem] * 4,
        out_specs=(vmem, vmem, vmem, vmem),
        compiler_params=pltpu.CompilerParams(vmem_limit_bytes=32 * 2**20),
        cost_estimate=pl.CostEstimate(flops=2 * 10**9, bytes_accessed=2**20, transcendentals=0),
    )(
        me,
        child_parent.reshape(1, -1),
        parent_owner.reshape(1, -1),
        parent_pages.reshape(1, -1),
        jnp.pad(page_table, ((0, 0), (0, 8 - page_table.shape[1]))),
    )


def fill_kernel(own_hot_ref, other_hot_ref, own_ref, other_ref, out_ref):
    filled = mm(own_hot_ref[...], own_ref[...]) + mm(other_hot_ref[...], other_ref[...])
    out_ref[...] = filled.astype(BF16)


def fill_slots(own_hot, other_hot, own, other):
    vmem = pl.BlockSpec(memory_space=pltpu.VMEM)
    return pl.pallas_call(
        fill_kernel,
        out_shape=jax.ShapeDtypeStruct((own_hot.shape[0], own.shape[1]), BF16),
        in_specs=[vmem] * 4,
        out_specs=vmem,
        compiler_params=pltpu.CompilerParams(vmem_limit_bytes=48 * 2**20),
    )(own_hot, other_hot, own, other)


def settle_kernel(hot_ref, rows_ref, out_ref, buffer_ref, sems):
    parts = sems.shape[0]
    size = buffer_ref.shape[0] // parts
    copies = []
    for i in range(parts):
        cut = slice(i * size, (i + 1) * size)
        buffer_ref[cut] = mm_tn(hot_ref[:, cut], rows_ref[...]).astype(BF16)
        copies.append(pltpu.make_async_copy(buffer_ref.at[cut], out_ref.at[cut], sems.at[i]))
        copies[-1].start()
    for copy in copies:
        copy.wait()


def settle(hot, rows, count):
    vmem = pl.BlockSpec(memory_space=pltpu.VMEM)
    return pl.pallas_call(
        settle_kernel,
        out_shape=jax.ShapeDtypeStruct((count, rows.shape[1]), BF16),
        in_specs=[vmem, vmem],
        out_specs=pl.BlockSpec(memory_space=pltpu.HBM),
        scratch_shapes=[
            pltpu.VMEM((count, rows.shape[1]), BF16),
            pltpu.SemaphoreType.DMA((2,)),
        ],
        compiler_params=pltpu.CompilerParams(vmem_limit_bytes=48 * 2**20),
    )(hot, rows)


def pick_sum_kernel(hot_ref, rows_ref, out_ref, sum_ref):
    x = mm(hot_ref[...], rows_ref[...])
    out_ref[...] = x.astype(BF16)
    total = jnp.sum(x * x, axis=1, keepdims=True)
    total = jnp.broadcast_to(total, (total.shape[0], 128)).T
    sum_ref[...] = jnp.broadcast_to(total[0:1], sum_ref.shape[:1] + total.shape[1:])[:, None, :]


def pick_and_sum(hot, rows, copies):
    vmem = pl.BlockSpec(memory_space=pltpu.VMEM)
    count = hot.shape[0]
    return pl.pallas_call(
        pick_sum_kernel,
        out_shape=(
            jax.ShapeDtypeStruct((count, rows.shape[1]), BF16),
            jax.ShapeDtypeStruct((copies, 1, count), F32),
        ),
        in_specs=[vmem, vmem],
        out_specs=(vmem, vmem),
        compiler_params=pltpu.CompilerParams(vmem_limit_bytes=48 * 2**20),
    )(hot, rows)


def row_scale(sum_ref, width):
    total = jnp.sum(sum_ref[:, 0, :], axis=0, keepdims=True)
    scale = lax.rsqrt(total * (1.0 / width) + EPSILON)
    return jnp.broadcast_to(scale, (128, scale.shape[1])).T


def normed(x, scale, gain):
    return (x.astype(F32) * scale * gain.astype(F32)).astype(BF16)


def add_products(acc, x, wq_ref, wk_ref, wv_ref, wkv_ref):
    wide = wq_ref.shape[1]
    wkv_ref[:, :HEAD] = wk_ref[...]
    wkv_ref[:, HEAD:] = wv_ref[...]
    acc[:, :wide] += mm(x, wq_ref[...])
    acc[:, wide:] += mm(x, wkv_ref[...])


def project_kernel(width, count, first, order_ref, sum_ref, *refs):
    blocks = refs[:count]
    gain_ref, wq_ref, wk_ref, wv_ref = refs[count : count + 4]
    before = None if first else refs[count + 4]
    acc_ref, x_ref, scale_ref, wkv_ref = refs[-4:]
    step = pl.program_id(0)

    @pl.when(step == 0)
    def _():
        scale_ref[...] = row_scale(sum_ref, width)
        acc_ref[...] = jnp.zeros_like(acc_ref) if first else before[...]

    for i, block in enumerate(blocks):

        @pl.when(step == i)
        def _(block=block):
            x_ref[...] = normed(block[...], scale_ref[:, 0:1], gain_ref[0])

    add_products(acc_ref, x_ref[...], wq_ref, wk_ref, wv_ref, wkv_ref)


def project(order, sums, blocks, gain, wq, wk, wv, before=None):
    rows, part = blocks[0].shape
    columns = wq.shape[1] + wk.shape[1] + wv.shape[1]
    count = len(blocks)

    def whole(a):
        return pl.BlockSpec(a.shape, lambda i, order: (0,) * a.ndim)

    extra = [] if before is None else [before]
    return pl.pallas_call(
        functools.partial(project_kernel, wq.shape[0], count, before is None),
        out_shape=jax.ShapeDtypeStruct((rows, columns), F32),
        grid_spec=pltpu.PrefetchScalarGridSpec(
            num_scalar_prefetch=1,
            grid=(count,),
            in_specs=[whole(sums)]
            + [whole(b) for b in blocks]
            + [pl.BlockSpec((1, 1, part), lambda i, order: (order[i], 0, 0))]
            + [
                pl.BlockSpec((part, w.shape[1]), lambda i, order: (order[i], 0))
                for w in (wq, wk, wv)
            ]
            + [whole(a) for a in extra],
            out_specs=pl.BlockSpec((rows, columns), lambda i, order: (0, 0)),
            scratch_shapes=[
                pltpu.VMEM((rows, part), BF16),
                pltpu.VMEM((rows, 128), F32),
                pltpu.VMEM((part, 2 * HEAD), BF16),
            ],
        ),
        compiler_params=pltpu.CompilerParams(vmem_limit_bytes=32 * 2**20),
        cost_estimate=pl.CostEstimate(
            flops=2 * rows * part * count * columns * 3,
            bytes_accessed=2 * part * count * columns,
            transcendentals=0,
        ),
    )(order, sums, *blocks, gain, wq, wk, wv, *extra)


def attend_kernel(
    width,
    order_ref,
    info_ref,
    sum_ref,
    low_ref,
    high_ref,
    gain_ref,
    wq_ref,
    wk_ref,
    wv_ref,
    before_ref,
    cos_ref,
    sin_ref,
    pool_ref,
    back_ref,
    o_ref,
    out_ref,
    acc_ref,
    x_ref,
    wkv_ref,
    q_ref,
    k_ref,
    v_ref,
):
    scale = row_scale(sum_ref, width)[:, 0:1]
    half = low_ref.shape[0]
    x_ref[:half] = normed(low_ref[...], scale[:half], gain_ref[0])
    x_ref[half:] = normed(high_ref[...], scale[half:], gain_ref[0])
    acc_ref[...] = before_ref[...]
    add_products(acc_ref, x_ref[...], wq_ref, wk_ref, wv_ref, wkv_ref)

    cos = cos_ref[...]
    sin = sin_ref[...]

    def turn(part):
        return (part * cos + pltpu.roll(part, HEAD // 2, 1) * sin).astype(BF16)

    heads = wq_ref.shape[1] // HEAD
    for h in range(heads):
        cut = slice(h * HEAD, (h + 1) * HEAD)
        q_ref[:, cut] = turn(acc_ref[:, cut])
    k_ref[...] = turn(acc_ref[:, heads * HEAD : (heads + 1) * HEAD])
    v_ref[...] = acc_ref[:, (heads + 1) * HEAD :].astype(BF16)

    family = FORK * STEPS
    scale = 1.0 / math.sqrt(HEAD)
    row_at = iota((heads * family, family), 0) % family
    key_at = iota((heads * family, family), 1)
    own_mask = (row_at // STEPS == key_at // STEPS) & (row_at >= key_at)

    @pl.loop(0, PARENTS_HERE)
    def _(j):
        at = pl.ds(pl.multiple_of(j * family, family), family)
        q = jnp.concatenate([q_ref[at, h * HEAD : (h + 1) * HEAD] for h in range(heads)], axis=0)
        own = jnp.where(own_mask, mm_nt(q, k_ref[at, :]) * scale, -jnp.inf)
        own_top = jnp.max(own, axis=1, keepdims=True)
        own_weight = jnp.exp(own - own_top)
        own_total = jnp.sum(own_weight, axis=1, keepdims=True)
        own_mix = mm(own_weight.astype(BF16), v_ref[at, :])
        length = info_ref[j, MOST_PAGES]
        for n in range(1, MOST_PAGES + 1):

            @pl.when(length == n)
            def _(n=n):
                ids = [info_ref[j, i] for i in range(n)]
                keys = jnp.concatenate([pool_ref[i, 0] for i in ids], axis=0)
                values = jnp.concatenate([pool_ref[i, 1] for i in ids], axis=0)
                path = mm_nt(q, keys) * scale
                path_top = jnp.max(path, axis=1, keepdims=True)
                weight = jnp.exp(path - path_top)
                path_total = jnp.sum(weight, axis=1, keepdims=True)
                path_mix = mm(weight.astype(BF16), values)
                top = jnp.maximum(path_top, own_top)
                path_factor = jnp.exp(path_top - top)
                own_factor = jnp.exp(own_top - top)
                both = path_mix * path_factor + own_mix * own_factor
                out = both / (path_total * path_factor + own_total * own_factor)
                out = out.astype(BF16)
                for h in range(heads):
                    o_ref[at, h * HEAD : (h + 1) * HEAD] = out[h * family : (h + 1) * family]

    out_ref[...] = mm_tn(back_ref[...], o_ref[...]).astype(BF16)


def attend(order, info, sums, low, high, gain, wq, wk, wv, before, cos, sin, pool, back):
    rows, columns = before.shape
    part = low.shape[1]
    wide = back.shape[1]

    def whole(a):
        return pl.BlockSpec(a.shape, lambda i, order, info: (0,) * a.ndim)

    return pl.pallas_call(
        functools.partial(attend_kernel, 8 * wq.shape[0]),
        out_shape=(
            jax.ShapeDtypeStruct((rows, wq.shape[1]), BF16),
            jax.ShapeDtypeStruct((wide, wq.shape[1]), BF16),
        ),
        grid_spec=pltpu.PrefetchScalarGridSpec(
            num_scalar_prefetch=2,
            grid=(1,),
            in_specs=[whole(a) for a in (sums, low, high)]
            + [pl.BlockSpec((1, 1, part), lambda i, order, info: (order[0], 0, 0))]
            + [whole(a) for a in (wq, wk, wv, before, cos, sin, pool, back)],
            out_specs=(
                pl.BlockSpec((rows, wq.shape[1]), lambda i, order, info: (0, 0)),
                pl.BlockSpec((wide, wq.shape[1]), lambda i, order, info: (0, 0)),
            ),
            scratch_shapes=[
                pltpu.VMEM((rows, columns), F32),
                pltpu.VMEM((rows, part), BF16),
                pltpu.VMEM((part, 2 * HEAD), BF16),
                pltpu.VMEM((rows, wq.shape[1]), BF16),
                pltpu.VMEM((rows, HEAD), BF16),
                pltpu.VMEM((rows, HEAD), BF16),
            ],
        ),
        compiler_params=pltpu.CompilerParams(vmem_limit_bytes=48 * 2**20),
        cost_estimate=pl.CostEstimate(
            flops=2 * rows * part * columns * 6, bytes_accessed=2 * part * columns, transcendentals=0
        ),
    )(order, info, sums, low, high, gain, wq, wk, wv, before, cos, sin, pool, back)


def moves(dy, dz):
    return [(t, ((t // 2 + dy) % 4) * 2 + (t + dz) % 2) for t in range(8)]


def crowded_tables(me, child_parent, parent_owner, parent_pages, page_table, here):
    children = child_parent.shape[0]
    key = parent_owner[child_parent] * parent_owner.shape[0] + child_parent
    number = jnp.arange(children, dtype=jnp.int32)
    earlier = (key[None, :] < key[:, None]) | (
        (key[None, :] == key[:, None]) & (number[None, :] < number[:, None])
    )
    spot = jnp.sum(earlier.astype(jnp.int32), axis=1)
    my_spots = me[0] * here + jnp.arange(here, dtype=jnp.int32)
    mine = jnp.sum(jnp.where(spot[None, :] == my_spots[:, None], number[None, :], 0), axis=1)
    parents = child_parent[mine[::FORK]]
    info = jnp.concatenate(
        [page_table[parents], parent_pages[parents][:, None], jnp.zeros((PARENTS_HERE, 2), jnp.int32)],
        axis=1,
    )
    home = lax.dynamic_slice_in_dim(spot, me[0] * here, here)
    return mine, home, info


def take_rows(rows, which):
    places = (which[:, None] * STEPS + jnp.arange(STEPS, dtype=jnp.int32)[None, :]).reshape(-1)
    return rows[places]


def local(
    branch_tokens,
    norm_gain,
    wq,
    wk,
    wv,
    kv_pool,
    parent_owner,
    parent_pages,
    page_table,
    child_parent,
):
    groups = lax.axis_size("sample")
    team = lax.axis_size("tensor")
    rows, width = branch_tokens.shape
    here = rows // STEPS
    me = lax.axis_index("sample").astype(jnp.int32).reshape(1)
    t = lax.axis_index("tensor")
    tables = (child_parent, parent_owner, parent_pages, page_table)
    other = lax.ppermute(branch_tokens, "sample", [(i, i ^ 1) for i in range(groups)])
    own_hot, other_hot, fits = leave(SLOTS, BACK_SLOTS, groups, me, *tables[:2], rows)
    other, own_hot, other_hot, fits = lax.optimization_barrier((other, own_hot, other_hot, fits))
    send = fill_slots(own_hot, other_hot, branch_tokens, other)
    usual = fits[0] == 1
    wide = groups * SLOTS * STEPS
    back_wide = groups * BACK_SLOTS * STEPS

    def place(dy, dz):
        return ((t // 2 + dy) % 4) * 2 + (t + dz) % 2

    def order(*keys):
        return jnp.stack([place(*key) for key in keys]).astype(jnp.int32)

    def pad(a, deep):
        return jnp.pad(a, ((0, deep - a.shape[0]), (0, 0)))

    def last_weights():
        return [lax.dynamic_slice_in_dim(w, place(2, 1) * width, width) for w in (wq, wk, wv)]

    def out_usual():
        came = lax.all_to_all(send.reshape(groups, wide // groups, width), "sample", 0, 0)
        routed = arrive(SLOTS, BACK_SLOTS, groups, me, *tables, rows)
        return lax.optimization_barrier((came.reshape(wide, width), *routed, *last_weights()))

    def out_crowded():
        mine, _, info = crowded_tables(me, *tables, here)
        came = take_rows(lax.all_gather(branch_tokens, "sample", axis=0, tiled=True), mine)
        return (
            pad(came, wide),
            jnp.eye(rows, wide, dtype=BF16),
            jnp.zeros((rows, back_wide), BF16),
            jnp.eye(back_wide, rows, dtype=BF16),
            info,
            *last_weights(),
        )

    came, from_hot, back_hot, home_hot, info, *last = lax.cond(usual, out_usual, out_crowded)
    mine, sums = pick_and_sum(from_hot, came, team)

    def shift(block, dy, dz):
        return lax.ppermute(block, "tensor", moves(dy, dz))

    gain = norm_gain.reshape(team, 1, -1)
    sums = lax.all_to_all(sums, "tensor", 0, 0)
    b30, b10, b01 = lax.optimization_barrier(
        (shift(mine, 1, 0), shift(mine, -1, 0), shift(mine, 0, 1))
    )
    second = (shift(b30, 1, 0), shift(b01, -1, 0), shift(b30, 0, 1))
    acc = project(
        order((0, 0), (3, 0), (1, 0), (0, 1)), sums, [mine, b30, b10, b01], gain, wq, wk, wv
    )
    b20, b11, b31, acc = lax.optimization_barrier((*second, acc))
    half = rows // 2
    low, high = shift(b31[:half], 1, 0), shift(b11[half:], -1, 0)
    acc = project(order((2, 0), (1, 1), (3, 1)), sums, [b20, b11, b31], gain, wq, wk, wv, acc)
    pages = info[:, MOST_PAGES]
    positions = (
        jnp.repeat(pages * PAGE, FORK * STEPS)
        + jnp.tile(jnp.arange(STEPS, dtype=jnp.int32), PARENTS_HERE * FORK)
    ).astype(F32)
    inverse = ROPE_THETA ** (-2.0 * jnp.arange(HEAD // 2, dtype=F32) / HEAD)
    angles = positions[:, None] * inverse[None, :]
    cos, sin = jnp.cos(angles), jnp.sin(angles)
    cos = jnp.concatenate([cos, cos], axis=1)
    sin = jnp.concatenate([-sin, sin], axis=1)
    low, high, acc, cos, sin = lax.optimization_barrier((low, high, acc, cos, sin))
    out, back = attend(
        order((2, 1)), info, sums, low, high, gain, *last, acc, cos, sin, kv_pool, back_hot
    )

    def back_usual():
        home = lax.all_to_all(back.reshape(groups, -1, back.shape[1]), "sample", 0, 0)
        return home.reshape(back_wide, -1)

    def back_crowded():
        _, home, _ = crowded_tables(me, *tables, here)
        every = lax.all_gather(out, "sample", axis=0, tiled=True)
        return pad(take_rows(every, home), back_wide)

    home = lax.cond(usual, back_usual, back_crowded)
    return settle(home_hot, home, rows)


def solution(mesh):
    return jax.shard_map(
        local,
        mesh=mesh,
        in_specs=(
            P("sample", "tensor"),
            P(),
            P(None, "tensor"),
            P(None, "tensor"),
            P(None, "tensor"),
            P("sample", None, None, "tensor"),
            P(),
            P(),
            P(),
            P(),
        ),
        out_specs=P("sample", "tensor"),
        check_vma=False,
    )
```

```python
import functools
import math

import jax
import jax.numpy as jnp
from jax import lax
from jax.experimental import pallas as pl
from jax.experimental.pallas import tpu as pltpu
from jax.sharding import PartitionSpec as P

HEAD = 128
PAGE = 128
STEPS = 4
FORK = 8
PARENTS_HERE = 8
MOST_PAGES = 5
ROPE_THETA = 10000.0
EPSILON = 1e-06
SLOTS = 10
BACK_SLOTS = 14

BF16 = jnp.bfloat16
F32 = jnp.float32


def iota(shape, dim):
    return lax.broadcasted_iota(jnp.int32, shape, dim)


def one(mask):
    return jnp.where(mask, 1.0, 0.0).astype(BF16)


def mm(a, b):
    return lax.dot_general(a, b, (((1,), (0,)), ((), ())), preferred_element_type=F32)


def mm_nt(a, b):
    return lax.dot_general(a, b, (((1,), (1,)), ((), ())), preferred_element_type=F32)


def mm_tn(a, b):
    return lax.dot_general(a, b, (((0,), (0,)), ((), ())), preferred_element_type=F32)


def leave_kernel(slots, limits, me_ref, child_ref, owner_ref, own_ref, other_ref, fits_ref, mask_ref):
    groups = mask_ref.shape[0]
    me = me_ref[0]
    core = lax.rem(me, 2)
    children = child_ref.shape[1]
    parents = owner_ref.shape[1]
    rows = own_ref.shape[1]
    here = rows // STEPS
    parent_hot = one(iota((parents, children), 0) == child_ref[...])
    owner = jnp.broadcast_to(owner_ref[...].astype(F32), (16, parents)).astype(BF16)
    owner_of = mm(owner, parent_hot)[0:1].astype(jnp.int32)
    mask = jnp.where(iota((groups, children), 0) == owner_of, 1.0, 0.0)
    mask_ref[...] = mask
    column, child = iota((children, 128), 1), iota((children, 128), 0)
    counted = (column == child // here) | (column == groups + child // (2 * here))
    counts = mm(mask.astype(BF16), one(counted))
    limit = jnp.where(iota(counts.shape, 1) < groups, limits[0], limits[1])
    fits_ref[0] = jnp.min(jnp.where(counts.astype(jnp.int32) <= limit, 1, 0))

    chip = lax.div(me, 2)
    mask = mask_ref[:, pl.ds(pl.multiple_of(chip * 2 * here, 2 * here), 2 * here)]
    ahead = mm(mask.astype(BF16), one(iota((128, 128), 0) < iota((128, 128), 1)))
    rank = jnp.sum(mask * ahead, axis=0, keepdims=True).astype(jnp.int32)
    owner = jnp.sum(mask * iota(mask.shape, 0).astype(F32), axis=0, keepdims=True)
    keep = jnp.where(rank % 2 == core, 1.0, 0.0)
    turn = (rank // 2).astype(F32)
    at = iota((16, 2 * here), 0)
    facts = jnp.where(at == 0, owner, jnp.where(at == 1, turn, keep)).astype(BF16)
    for ref, side in ((own_ref, core), (other_ref, 1 - core)):
        grow = one(iota((2 * here, rows), 0) == side * here + iota((2 * here, rows), 1) // STEPS)
        of_row = mm(facts, grow)
        target = of_row[0:1] * (slots * STEPS) + of_row[1:2] * STEPS
        target = target.astype(jnp.int32) + iota((1, rows), 1) % STEPS
        target = jnp.where(of_row[2:3] > 0.5, target, -1)
        ref[...] = one(iota(ref.shape, 0) == target)


def leave(slots, back_slots, groups, me, child_parent, parent_owner, rows):
    vmem = pl.BlockSpec(memory_space=pltpu.VMEM)
    smem = pl.BlockSpec(memory_space=pltpu.SMEM)
    hot = jax.ShapeDtypeStruct((groups * slots * STEPS, rows), BF16)
    return pl.pallas_call(
        functools.partial(leave_kernel, slots, (back_slots, 2 * slots)),
        out_shape=(hot, hot, jax.ShapeDtypeStruct((1,), jnp.int32)),
        in_specs=[smem, vmem, vmem],
        out_specs=(vmem, vmem, smem),
        scratch_shapes=[pltpu.VMEM((groups, child_parent.shape[0]), F32)],
        compiler_params=pltpu.CompilerParams(vmem_limit_bytes=32 * 2**20),
        cost_estimate=pl.CostEstimate(flops=10**9, bytes_accessed=2**20, transcendentals=0),
    )(me, child_parent.reshape(1, -1), parent_owner.reshape(1, -1))


def arrive_kernel(
    slots,
    back_slots,
    me_ref,
    child_ref,
    owner_ref,
    pages_ref,
    table_ref,
    from_ref,
    back_ref,
    home_ref,
    info_ref,
):
    groups = home_ref.shape[0] // (back_slots * STEPS)
    me = me_ref[0]
    children = child_ref.shape[1]
    parents = owner_ref.shape[1]
    rows = from_ref.shape[0]
    here = rows // STEPS
    child = child_ref[...]
    owner = owner_ref[...]
    parent_hot = one(iota((parents, children), 0) == child)
    owner_of = mm(jnp.broadcast_to(owner.astype(F32), (16, parents)).astype(BF16), parent_hot)[0:1]
    owner_mask = one(iota((groups, children), 0) == owner_of.astype(jnp.int32))
    pick = one(iota((children, rows), 0) == me * here + iota((children, rows), 1) // STEPS)
    home_mask = mm(owner_mask, pick)
    before = one(
        (iota((rows, rows), 0) // STEPS < iota((rows, rows), 1) // STEPS)
        & (iota((rows, rows), 0) % STEPS == 0)
    )
    rank = mm(home_mask.astype(BF16), before)
    target = jnp.sum(
        home_mask * (iota((groups, rows), 0).astype(F32) * (back_slots * STEPS) + rank * STEPS),
        axis=0,
        keepdims=True,
    ).astype(jnp.int32) + iota((1, rows), 1) % STEPS
    home_ref[...] = one(iota(home_ref.shape, 0) == target)

    mine_parent = owner == me
    tri_block = one(iota((128, 128), 0) < iota((128, 128), 1))
    tri_home = one(
        (iota((128, 128), 0) < iota((128, 128), 1))
        & (iota((128, 128), 0) // here == iota((128, 128), 1) // here)
    )
    parent_rank = mm(one(jnp.broadcast_to(mine_parent, (16, parents))), tri_block)
    parent_rank = parent_rank[0:1].astype(jnp.int32)
    mine_hot = (iota((PARENTS_HERE, parents), 0) == parent_rank) & mine_parent
    pages = jnp.sum(jnp.where(mine_hot, pages_ref[...], 0), axis=1, keepdims=True)
    mine_hot = one(mine_hot)
    table = mm(mine_hot, table_ref[...].astype(F32).astype(BF16)).astype(jnp.int32)
    info_ref[...] = jnp.where(iota((PARENTS_HERE, 8), 1) == MOST_PAGES, pages, table)
    member = mm(mine_hot, parent_hot)
    carry = jnp.zeros((PARENTS_HERE, 1), F32)
    places, spots, back_spots = [], [], []
    for block in range(children // 128):
        part = member[:, block * 128 : (block + 1) * 128]
        ahead = mm(part.astype(BF16), tri_block) + carry
        carry = carry + jnp.sum(part, axis=1, keepdims=True)
        is_mine = jnp.sum(part, axis=0, keepdims=True)
        place = jnp.sum(
            part * (iota((PARENTS_HERE, 128), 0).astype(F32) * FORK + ahead), axis=0, keepdims=True
        ).astype(jnp.int32)
        is_mine_wide = jnp.broadcast_to(is_mine, (16, 128)).astype(BF16)
        in_chip = mm(is_mine_wide, tri_block)[0:1].astype(jnp.int32)
        in_home = mm(is_mine_wide, tri_home)[0:1].astype(jnp.int32)
        number = block * 128 + iota((1, 128), 1)
        sender = number // (2 * here) * 2 + in_chip % 2
        spot = sender * slots + in_chip // 2
        back_spot = number // here * back_slots + in_home
        for found, value in ((places, place), (spots, spot), (back_spots, back_spot)):
            found.append(jnp.where(is_mine > 0.5, value, -1))
    place_hot = one(iota((here, children), 0) == jnp.concatenate(places, axis=1))
    grow_rows = one(iota((rows, here), 0) // STEPS == iota((rows, here), 1))
    for ref, found, count in ((from_ref, spots, slots), (back_ref, back_spots, back_slots)):
        deep, wide = groups * count, groups * count * STEPS
        spot_hot = one(iota((deep, children), 0) == jnp.concatenate(found, axis=1))
        by_child = mm_nt(place_hot, spot_hot).astype(BF16)
        grow_columns = one(iota((deep, wide), 0) == iota((deep, wide), 1) // STEPS)
        by_row = mm(mm(grow_rows, by_child).astype(BF16), grow_columns)
        same_step = iota((rows, wide), 0) % STEPS == iota((rows, wide), 1) % STEPS
        ref[...] = jnp.where(same_step, by_row, 0.0).astype(BF16)


def arrive(
    slots, back_slots, groups, me, child_parent, parent_owner, parent_pages, page_table, rows
):
    vmem = pl.BlockSpec(memory_space=pltpu.VMEM)
    smem = pl.BlockSpec(memory_space=pltpu.SMEM)
    return pl.pallas_call(
        functools.partial(arrive_kernel, slots, back_slots),
        out_shape=(
            jax.ShapeDtypeStruct((rows, groups * slots * STEPS), BF16),
            jax.ShapeDtypeStruct((rows, groups * back_slots * STEPS), BF16),
            jax.ShapeDtypeStruct((groups * back_slots * STEPS, rows), BF16),
            jax.ShapeDtypeStruct((PARENTS_HERE, 8), jnp.int32),
        ),
        in_specs=[smem] + [vmem] * 4,
        out_specs=(vmem, vmem, vmem, vmem),
        compiler_params=pltpu.CompilerParams(vmem_limit_bytes=32 * 2**20),
        cost_estimate=pl.CostEstimate(flops=2 * 10**9, bytes_accessed=2**20, transcendentals=0),
    )(
        me,
        child_parent.reshape(1, -1),
        parent_owner.reshape(1, -1),
        parent_pages.reshape(1, -1),
        jnp.pad(page_table, ((0, 0), (0, 8 - page_table.shape[1]))),
    )


def fill_kernel(own_hot_ref, other_hot_ref, own_ref, other_ref, out_ref):
    filled = mm(own_hot_ref[...], own_ref[...]) + mm(other_hot_ref[...], other_ref[...])
    out_ref[...] = filled.astype(BF16)


def fill_slots(own_hot, other_hot, own, other):
    vmem = pl.BlockSpec(memory_space=pltpu.VMEM)
    return pl.pallas_call(
        fill_kernel,
        out_shape=jax.ShapeDtypeStruct((own_hot.shape[0], own.shape[1]), BF16),
        in_specs=[vmem] * 4,
        out_specs=vmem,
        compiler_params=pltpu.CompilerParams(vmem_limit_bytes=48 * 2**20),
    )(own_hot, other_hot, own, other)


def settle_kernel(hot_ref, rows_ref, out_ref):
    out_ref[...] = mm_tn(hot_ref[...], rows_ref[...]).astype(BF16)


def settle(hot, rows, count):
    vmem = pl.BlockSpec(memory_space=pltpu.VMEM)
    return pl.pallas_call(
        settle_kernel,
        out_shape=jax.ShapeDtypeStruct((count, rows.shape[1]), BF16),
        in_specs=[vmem, vmem],
        out_specs=vmem,
        compiler_params=pltpu.CompilerParams(vmem_limit_bytes=48 * 2**20),
    )(hot, rows)


def pick_sum_kernel(hot_ref, rows_ref, out_ref, sum_ref):
    x = mm(hot_ref[...], rows_ref[...])
    out_ref[...] = x.astype(BF16)
    total = jnp.sum(x * x, axis=1, keepdims=True)
    total = jnp.broadcast_to(total, (total.shape[0], 128)).T
    sum_ref[...] = jnp.broadcast_to(total[0:1], sum_ref.shape[:1] + total.shape[1:])[:, None, :]


def pick_and_sum(hot, rows, copies):
    vmem = pl.BlockSpec(memory_space=pltpu.VMEM)
    count = hot.shape[0]
    return pl.pallas_call(
        pick_sum_kernel,
        out_shape=(
            jax.ShapeDtypeStruct((count, rows.shape[1]), BF16),
            jax.ShapeDtypeStruct((copies, 1, count), F32),
        ),
        in_specs=[vmem, vmem],
        out_specs=(vmem, vmem),
        compiler_params=pltpu.CompilerParams(vmem_limit_bytes=48 * 2**20),
    )(hot, rows)


def row_scale(sum_ref, width):
    total = jnp.sum(sum_ref[:, 0, :], axis=0, keepdims=True)
    scale = lax.rsqrt(total * (1.0 / width) + EPSILON)
    return jnp.broadcast_to(scale, (128, scale.shape[1])).T


def normed(x, scale, gain):
    return (x.astype(F32) * scale * gain.astype(F32)).astype(BF16)


def add_products(acc, x, wq_ref, wk_ref, wv_ref, wkv_ref):
    wide = wq_ref.shape[1]
    wkv_ref[:, :HEAD] = wk_ref[...]
    wkv_ref[:, HEAD:] = wv_ref[...]
    acc[:, :wide] += mm(x, wq_ref[...])
    acc[:, wide:] += mm(x, wkv_ref[...])


def project_kernel(width, count, first, order_ref, sum_ref, *refs):
    blocks = refs[:count]
    gain_ref, wq_ref, wk_ref, wv_ref = refs[count : count + 4]
    before = None if first else refs[count + 4]
    acc_ref, x_ref, scale_ref, wkv_ref = refs[-4:]
    step = pl.program_id(0)

    @pl.when(step == 0)
    def _():
        scale_ref[...] = row_scale(sum_ref, width)
        acc_ref[...] = jnp.zeros_like(acc_ref) if first else before[...]

    for i, block in enumerate(blocks):

        @pl.when(step == i)
        def _(block=block):
            x_ref[...] = normed(block[...], scale_ref[:, 0:1], gain_ref[0])

    add_products(acc_ref, x_ref[...], wq_ref, wk_ref, wv_ref, wkv_ref)


def project(order, sums, blocks, gain, wq, wk, wv, before=None):
    rows, part = blocks[0].shape
    columns = wq.shape[1] + wk.shape[1] + wv.shape[1]
    count = len(blocks)

    def whole(a):
        return pl.BlockSpec(a.shape, lambda i, order: (0,) * a.ndim)

    extra = [] if before is None else [before]
    return pl.pallas_call(
        functools.partial(project_kernel, wq.shape[0], count, before is None),
        out_shape=jax.ShapeDtypeStruct((rows, columns), F32),
        grid_spec=pltpu.PrefetchScalarGridSpec(
            num_scalar_prefetch=1,
            grid=(count,),
            in_specs=[whole(sums)]
            + [whole(b) for b in blocks]
            + [pl.BlockSpec((1, 1, part), lambda i, order: (order[i], 0, 0))]
            + [
                pl.BlockSpec((part, w.shape[1]), lambda i, order: (order[i], 0))
                for w in (wq, wk, wv)
            ]
            + [whole(a) for a in extra],
            out_specs=pl.BlockSpec((rows, columns), lambda i, order: (0, 0)),
            scratch_shapes=[
                pltpu.VMEM((rows, part), BF16),
                pltpu.VMEM((rows, 128), F32),
                pltpu.VMEM((part, 2 * HEAD), BF16),
            ],
        ),
        compiler_params=pltpu.CompilerParams(vmem_limit_bytes=32 * 2**20),
        cost_estimate=pl.CostEstimate(
            flops=2 * rows * part * count * columns * 3,
            bytes_accessed=2 * part * count * columns,
            transcendentals=0,
        ),
    )(order, sums, *blocks, gain, wq, wk, wv, *extra)


def attend_kernel(
    width,
    order_ref,
    info_ref,
    sum_ref,
    low_ref,
    high_ref,
    gain_ref,
    wq_ref,
    wk_ref,
    wv_ref,
    before_ref,
    cos_ref,
    sin_ref,
    pool_ref,
    back_ref,
    out_ref,
    acc_ref,
    x_ref,
    wkv_ref,
    q_ref,
    k_ref,
    v_ref,
    o_ref,
):
    scale = row_scale(sum_ref, width)[:, 0:1]
    half = low_ref.shape[0]
    x_ref[:half] = normed(low_ref[...], scale[:half], gain_ref[0])
    x_ref[half:] = normed(high_ref[...], scale[half:], gain_ref[0])
    acc_ref[...] = before_ref[...]
    add_products(acc_ref, x_ref[...], wq_ref, wk_ref, wv_ref, wkv_ref)

    cos = cos_ref[...]
    sin = sin_ref[...]

    def turn(part):
        return (part * cos + pltpu.roll(part, HEAD // 2, 1) * sin).astype(BF16)

    heads = wq_ref.shape[1] // HEAD
    for h in range(heads):
        cut = slice(h * HEAD, (h + 1) * HEAD)
        q_ref[:, cut] = turn(acc_ref[:, cut])
    k_ref[...] = turn(acc_ref[:, heads * HEAD : (heads + 1) * HEAD])
    v_ref[...] = acc_ref[:, (heads + 1) * HEAD :].astype(BF16)

    family = FORK * STEPS
    scale = 1.0 / math.sqrt(HEAD)
    row_at = iota((heads * family, family), 0) % family
    key_at = iota((heads * family, family), 1)
    own_mask = (row_at // STEPS == key_at // STEPS) & (row_at >= key_at)

    @pl.loop(0, PARENTS_HERE)
    def _(j):
        at = pl.ds(pl.multiple_of(j * family, family), family)
        q = jnp.concatenate([q_ref[at, h * HEAD : (h + 1) * HEAD] for h in range(heads)], axis=0)
        own = jnp.where(own_mask, mm_nt(q, k_ref[at, :]) * scale, -jnp.inf)
        own_top = jnp.max(own, axis=1, keepdims=True)
        own_weight = jnp.exp(own - own_top)
        own_total = jnp.sum(own_weight, axis=1, keepdims=True)
        own_mix = mm(own_weight.astype(BF16), v_ref[at, :])
        length = info_ref[j, MOST_PAGES]
        for n in range(1, MOST_PAGES + 1):

            @pl.when(length == n)
            def _(n=n):
                ids = [info_ref[j, i] for i in range(n)]
                keys = jnp.concatenate([pool_ref[i, 0] for i in ids], axis=0)
                values = jnp.concatenate([pool_ref[i, 1] for i in ids], axis=0)
                path = mm_nt(q, keys) * scale
                path_top = jnp.max(path, axis=1, keepdims=True)
                weight = jnp.exp(path - path_top)
                path_total = jnp.sum(weight, axis=1, keepdims=True)
                path_mix = mm(weight.astype(BF16), values)
                top = jnp.maximum(path_top, own_top)
                path_factor = jnp.exp(path_top - top)
                own_factor = jnp.exp(own_top - top)
                both = path_mix * path_factor + own_mix * own_factor
                out = both / (path_total * path_factor + own_total * own_factor)
                out = out.astype(BF16)
                for h in range(heads):
                    o_ref[at, h * HEAD : (h + 1) * HEAD] = out[h * family : (h + 1) * family]

    out_ref[...] = mm_tn(back_ref[...], o_ref[...]).astype(BF16)


def attend(order, info, sums, low, high, gain, wq, wk, wv, before, cos, sin, pool, back):
    rows, columns = before.shape
    part = low.shape[1]
    wide = back.shape[1]

    def whole(a):
        return pl.BlockSpec(a.shape, lambda i, order, info: (0,) * a.ndim)

    return pl.pallas_call(
        functools.partial(attend_kernel, 8 * wq.shape[0]),
        out_shape=jax.ShapeDtypeStruct((wide, wq.shape[1]), BF16),
        grid_spec=pltpu.PrefetchScalarGridSpec(
            num_scalar_prefetch=2,
            grid=(1,),
            in_specs=[whole(a) for a in (sums, low, high)]
            + [pl.BlockSpec((1, 1, part), lambda i, order, info: (order[0], 0, 0))]
            + [whole(a) for a in (wq, wk, wv, before, cos, sin, pool, back)],
            out_specs=pl.BlockSpec((wide, wq.shape[1]), lambda i, order, info: (0, 0)),
            scratch_shapes=[
                pltpu.VMEM((rows, columns), F32),
                pltpu.VMEM((rows, part), BF16),
                pltpu.VMEM((part, 2 * HEAD), BF16),
                pltpu.VMEM((rows, wq.shape[1]), BF16),
                pltpu.VMEM((rows, HEAD), BF16),
                pltpu.VMEM((rows, HEAD), BF16),
                pltpu.VMEM((rows, wq.shape[1]), BF16),
            ],
        ),
        compiler_params=pltpu.CompilerParams(vmem_limit_bytes=48 * 2**20),
        cost_estimate=pl.CostEstimate(
            flops=2 * rows * part * columns * 6, bytes_accessed=2 * part * columns, transcendentals=0
        ),
    )(order, info, sums, low, high, gain, wq, wk, wv, before, cos, sin, pool, back)


def moves(dy, dz):
    return [(t, ((t // 2 + dy) % 4) * 2 + (t + dz) % 2) for t in range(8)]


def after_leave(slots, back_slots, groups, me, tables, arrays, send):
    (norm_gain, wq, wk, wv, kv_pool) = arrays
    wide, width = send.shape
    rows = PARENTS_HERE * FORK * STEPS
    team = lax.axis_size("tensor")
    t = lax.axis_index("tensor")
    came = lax.all_to_all(send.reshape(groups, wide // groups, width), "sample", 0, 0)
    from_hot, back_hot, home_hot, info = arrive(slots, back_slots, groups, me, *tables, rows)

    def place(dy, dz):
        return ((t // 2 + dy) % 4) * 2 + (t + dz) % 2

    def order(*keys):
        return jnp.stack([place(*key) for key in keys]).astype(jnp.int32)

    last = [lax.dynamic_slice_in_dim(w, place(2, 1) * width, width) for w in (wq, wk, wv)]
    gain = norm_gain.reshape(team, 1, -1)

    pages = info[:, MOST_PAGES]
    positions = (
        jnp.repeat(pages * PAGE, FORK * STEPS)
        + jnp.tile(jnp.arange(STEPS, dtype=jnp.int32), PARENTS_HERE * FORK)
    ).astype(F32)
    inverse = ROPE_THETA ** (-2.0 * jnp.arange(HEAD // 2, dtype=F32) / HEAD)
    angles = positions[:, None] * inverse[None, :]
    cos, sin = jnp.cos(angles), jnp.sin(angles)
    cos = jnp.concatenate([cos, cos], axis=1)
    sin = jnp.concatenate([-sin, sin], axis=1)
    came, from_hot, back_hot, home_hot, info, cos, sin, gain, *last = lax.optimization_barrier(
        (came, from_hot, back_hot, home_hot, info, cos, sin, gain, *last)
    )
    mine, sums = pick_and_sum(from_hot, came.reshape(wide, width), team)

    def shift(block, dy, dz):
        return lax.ppermute(block, "tensor", moves(dy, dz))

    sums = lax.all_to_all(sums, "tensor", 0, 0)
    b30, b10, b01 = lax.optimization_barrier(
        (shift(mine, 1, 0), shift(mine, -1, 0), shift(mine, 0, 1))
    )
    second = (shift(b30, 1, 0), shift(b01, -1, 0), shift(b30, 0, 1))
    acc = project(
        order((0, 0), (3, 0), (1, 0), (0, 1)), sums, [mine, b30, b10, b01], gain, wq, wk, wv
    )
    b20, b11, b31, acc = lax.optimization_barrier((*second, acc))
    half = rows // 2
    low, high = shift(b31[:half], 1, 0), shift(b11[half:], -1, 0)
    acc = project(order((2, 0), (1, 1), (3, 1)), sums, [b20, b11, b31], gain, wq, wk, wv, acc)
    low, high, acc = lax.optimization_barrier((low, high, acc))
    back = attend(
        order((2, 1)), info, sums, low, high, gain, *last, acc, cos, sin, kv_pool, back_hot
    )
    home = lax.all_to_all(back.reshape(groups, -1, back.shape[1]), "sample", 0, 0)
    return settle(home_hot, home.reshape(-1, back.shape[1]), rows)


def local(
    branch_tokens,
    norm_gain,
    query_weight,
    key_weight,
    value_weight,
    kv_pool,
    parent_owner,
    parent_pages,
    page_table,
    child_parent,
):
    groups = lax.axis_size("sample")
    rows = branch_tokens.shape[0]
    me = lax.axis_index("sample").astype(jnp.int32).reshape(1)
    tables = (child_parent, parent_owner, parent_pages, page_table)
    arrays = (norm_gain, query_weight, key_weight, value_weight, kv_pool)
    other = lax.ppermute(branch_tokens, "sample", [(i, i ^ 1) for i in range(groups)])
    own_hot, other_hot, fits = leave(SLOTS, BACK_SLOTS, groups, me, *tables[:2], rows)
    other, own_hot, other_hot, fits = lax.optimization_barrier((other, own_hot, other_hot, fits))
    send = fill_slots(own_hot, other_hot, branch_tokens, other)

    def usual():
        return after_leave(SLOTS, BACK_SLOTS, groups, me, tables, arrays, send)

    def crowded():
        most = rows // STEPS
        own, others, _ = leave(most // 2, most, groups, me, *tables[:2], rows)
        wider = fill_slots(own, others, branch_tokens, other)
        return after_leave(most // 2, most, groups, me, tables, arrays, wider)

    return lax.cond(fits[0] == 1, usual, crowded)


def solution(mesh):
    return jax.shard_map(
        local,
        mesh=mesh,
        in_specs=(
            P("sample", "tensor"),
            P(),
            P(None, "tensor"),
            P(None, "tensor"),
            P(None, "tensor"),
            P("sample", None, None, "tensor"),
            P(),
            P(),
            P(),
            P(),
        ),
        out_specs=P("sample", "tensor"),
        check_vma=False,
    )
```

```python
import functools
import math

import jax
import jax.numpy as jnp
from jax import lax
from jax.experimental import pallas as pl
from jax.experimental.pallas import tpu as pltpu
from jax.sharding import PartitionSpec as P

HEAD = 128
PAGE = 128
STEPS = 4
FORK = 8
PARENTS_HERE = 8
MOST_PAGES = 5
ROPE_THETA = 10000.0
EPSILON = 1e-06
SLOTS = 10

BF16 = jnp.bfloat16
F32 = jnp.float32


def iota(shape, dim):
    return lax.broadcasted_iota(jnp.int32, shape, dim)


def one(mask):
    return jnp.where(mask, 1.0, 0.0).astype(BF16)


def mm(a, b):
    return lax.dot_general(a, b, (((1,), (0,)), ((), ())), preferred_element_type=F32)


def mm_nt(a, b):
    return lax.dot_general(a, b, (((1,), (1,)), ((), ())), preferred_element_type=F32)


def mm_tn(a, b):
    return lax.dot_general(a, b, (((0,), (0,)), ((), ())), preferred_element_type=F32)


def leave_kernel(slots, me_ref, child_ref, owner_ref, own_ref, other_ref, fits_ref, mask_ref):
    groups = mask_ref.shape[0]
    me = me_ref[0]
    core = lax.rem(me, 2)
    children = child_ref.shape[1]
    parents = owner_ref.shape[1]
    rows = own_ref.shape[1]
    here = rows // STEPS
    parent_hot = one(iota((parents, children), 0) == child_ref[...])
    owner = jnp.broadcast_to(owner_ref[...].astype(F32), (16, parents)).astype(BF16)
    owner_of = mm(owner, parent_hot)[0:1].astype(jnp.int32)
    mask = jnp.where(iota((groups, children), 0) == owner_of, 1.0, 0.0)
    mask_ref[...] = mask
    counted = iota((children, 128), 1) == iota((children, 128), 0) // (2 * here)
    most = jnp.max(mm(mask.astype(BF16), one(counted))).astype(jnp.int32)
    fits_ref[0] = jnp.where(most <= 2 * slots, 1, 0)

    chip = lax.div(me, 2)
    mask = mask_ref[:, pl.ds(pl.multiple_of(chip * 2 * here, 2 * here), 2 * here)]
    ahead = mm(mask.astype(BF16), one(iota((128, 128), 0) < iota((128, 128), 1)))
    rank = jnp.sum(mask * ahead, axis=0, keepdims=True).astype(jnp.int32)
    owner = jnp.sum(mask * iota(mask.shape, 0).astype(F32), axis=0, keepdims=True)
    keep = jnp.where(rank % 2 == core, 1.0, 0.0)
    turn = (rank // 2).astype(F32)
    at = iota((16, 2 * here), 0)
    facts = jnp.where(at == 0, owner, jnp.where(at == 1, turn, keep)).astype(BF16)
    for ref, side in ((own_ref, core), (other_ref, 1 - core)):
        grow = one(iota((2 * here, rows), 0) == side * here + iota((2 * here, rows), 1) // STEPS)
        of_row = mm(facts, grow)
        target = of_row[0:1] * (slots * STEPS) + of_row[1:2] * STEPS
        target = target.astype(jnp.int32) + iota((1, rows), 1) % STEPS
        target = jnp.where(of_row[2:3] > 0.5, target, -1)
        ref[...] = one(iota(ref.shape, 0) == target)


def leave(slots, groups, me, child_parent, parent_owner, rows):
    vmem = pl.BlockSpec(memory_space=pltpu.VMEM)
    smem = pl.BlockSpec(memory_space=pltpu.SMEM)
    hot = jax.ShapeDtypeStruct((groups * slots * STEPS, rows), BF16)
    return pl.pallas_call(
        functools.partial(leave_kernel, slots),
        out_shape=(hot, hot, jax.ShapeDtypeStruct((1,), jnp.int32)),
        in_specs=[smem, vmem, vmem],
        out_specs=(vmem, vmem, smem),
        scratch_shapes=[pltpu.VMEM((groups, child_parent.shape[0]), F32)],
        compiler_params=pltpu.CompilerParams(vmem_limit_bytes=32 * 2**20),
        cost_estimate=pl.CostEstimate(flops=10**9, bytes_accessed=2**20, transcendentals=0),
    )(me, child_parent.reshape(1, -1), parent_owner.reshape(1, -1))


def arrive_kernel(
    slots, me_ref, child_ref, owner_ref, pages_ref, table_ref, from_ref, info_ref
):
    me = me_ref[0]
    children = child_ref.shape[1]
    parents = owner_ref.shape[1]
    rows, wide = from_ref.shape
    here = rows // STEPS
    deep = wide // STEPS
    owner = owner_ref[...]
    parent_hot = one(iota((parents, children), 0) == child_ref[...])
    mine_parent = owner == me
    tri = one(iota((128, 128), 0) < iota((128, 128), 1))
    parent_rank = mm(one(jnp.broadcast_to(mine_parent, (16, parents))), tri)
    parent_rank = parent_rank[0:1].astype(jnp.int32)
    mine_hot = (iota((PARENTS_HERE, parents), 0) == parent_rank) & mine_parent
    pages = jnp.sum(jnp.where(mine_hot, pages_ref[...], 0), axis=1, keepdims=True)
    mine_hot = one(mine_hot)
    table = mm(mine_hot, table_ref[...].astype(F32).astype(BF16)).astype(jnp.int32)
    info_ref[...] = jnp.where(iota((PARENTS_HERE, 8), 1) == MOST_PAGES, pages, table)
    member = mm(mine_hot, parent_hot)
    carry = jnp.zeros((PARENTS_HERE, 1), F32)
    places, spots = [], []
    for block in range(children // 128):
        part = member[:, block * 128 : (block + 1) * 128]
        ahead = mm(part.astype(BF16), tri) + carry
        carry = carry + jnp.sum(part, axis=1, keepdims=True)
        is_mine = jnp.sum(part, axis=0, keepdims=True)
        place = jnp.sum(
            part * (iota((PARENTS_HERE, 128), 0).astype(F32) * FORK + ahead), axis=0, keepdims=True
        ).astype(jnp.int32)
        in_chip = mm(jnp.broadcast_to(is_mine, (16, 128)).astype(BF16), tri)[0:1].astype(jnp.int32)
        chip = (block * 128 + iota((1, 128), 1)) // (2 * here)
        spot = (chip * 2 + in_chip % 2) * slots + in_chip // 2
        places.append(jnp.where(is_mine > 0.5, place, -1))
        spots.append(jnp.where(is_mine > 0.5, spot, -1))
    place_hot = one(iota((here, children), 0) == jnp.concatenate(places, axis=1))
    spot_hot = one(iota((deep, children), 0) == jnp.concatenate(spots, axis=1))
    by_child = mm_nt(place_hot, spot_hot).astype(BF16)
    grow_rows = one(iota((rows, here), 0) // STEPS == iota((rows, here), 1))
    grow_columns = one(iota((deep, wide), 0) == iota((deep, wide), 1) // STEPS)
    by_row = mm(mm(grow_rows, by_child).astype(BF16), grow_columns)
    same_step = iota((rows, wide), 0) % STEPS == iota((rows, wide), 1) % STEPS
    from_ref[...] = jnp.where(same_step, by_row, 0.0).astype(BF16)


def arrive(slots, groups, me, child_parent, parent_owner, parent_pages, page_table, rows):
    vmem = pl.BlockSpec(memory_space=pltpu.VMEM)
    smem = pl.BlockSpec(memory_space=pltpu.SMEM)
    return pl.pallas_call(
        functools.partial(arrive_kernel, slots),
        out_shape=(
            jax.ShapeDtypeStruct((rows, groups * slots * STEPS), BF16),
            jax.ShapeDtypeStruct((PARENTS_HERE, 8), jnp.int32),
        ),
        in_specs=[smem] + [vmem] * 4,
        out_specs=(vmem, vmem),
        compiler_params=pltpu.CompilerParams(vmem_limit_bytes=32 * 2**20),
        cost_estimate=pl.CostEstimate(flops=2 * 10**9, bytes_accessed=2**20, transcendentals=0),
    )(
        me,
        child_parent.reshape(1, -1),
        parent_owner.reshape(1, -1),
        parent_pages.reshape(1, -1),
        jnp.pad(page_table, ((0, 0), (0, 8 - page_table.shape[1]))),
    )


def fill_kernel(own_hot_ref, other_hot_ref, own_ref, other_ref, out_ref):
    filled = mm(own_hot_ref[...], own_ref[...]) + mm(other_hot_ref[...], other_ref[...])
    out_ref[...] = filled.astype(BF16)


def fill_slots(own_hot, other_hot, own, other):
    vmem = pl.BlockSpec(memory_space=pltpu.VMEM)
    return pl.pallas_call(
        fill_kernel,
        out_shape=jax.ShapeDtypeStruct((own_hot.shape[0], own.shape[1]), BF16),
        in_specs=[vmem] * 4,
        out_specs=vmem,
        compiler_params=pltpu.CompilerParams(vmem_limit_bytes=48 * 2**20),
    )(own_hot, other_hot, own, other)


def fetch(from_ref, held_ref, sems):
    parts = sems.shape[0]
    deep = held_ref.shape[0] // parts
    copies = []
    for i in range(parts):
        cut = pl.ds(i * deep, deep)
        copies.append(pltpu.make_async_copy(from_ref.at[cut], held_ref.at[cut], sems.at[i]))
        copies[-1].start()
    return copies


def settle_kernel(own_hot_ref, other_hot_ref, rows_ref, own_ref, other_ref, held_ref, sems):
    for copy in fetch(rows_ref, held_ref, sems):
        copy.wait()
    rows = held_ref[...]
    other_ref[...] = mm_tn(other_hot_ref[...], rows).astype(BF16)
    own_ref[...] = mm_tn(own_hot_ref[...], rows).astype(BF16)


def settle(own_hot, other_hot, rows):
    vmem = pl.BlockSpec(memory_space=pltpu.VMEM)
    out = jax.ShapeDtypeStruct((own_hot.shape[1], rows.shape[1]), BF16)
    return pl.pallas_call(
        settle_kernel,
        out_shape=(out, out),
        in_specs=[vmem, vmem, pl.BlockSpec(memory_space=pltpu.HBM)],
        out_specs=(vmem, vmem),
        scratch_shapes=[pltpu.VMEM(rows.shape, BF16), pltpu.SemaphoreType.DMA((2,))],
        compiler_params=pltpu.CompilerParams(vmem_limit_bytes=32 * 2**20),
    )(own_hot, other_hot, rows)


def pick_sum_kernel(hot_ref, rows_ref, out_ref, sum_ref, held_ref, sems):
    x = jnp.zeros(out_ref.shape, F32)
    deep = held_ref.shape[0] // sems.shape[0]
    for i, copy in enumerate(fetch(rows_ref, held_ref, sems)):
        copy.wait()
        cut = slice(i * deep, (i + 1) * deep)
        x = x + mm(hot_ref[:, cut], held_ref[cut])
    out_ref[...] = x.astype(BF16)
    total = jnp.sum(x * x, axis=1, keepdims=True)
    total = jnp.broadcast_to(total, (total.shape[0], 128)).T
    sum_ref[...] = jnp.broadcast_to(total[0:1], sum_ref.shape[:1] + total.shape[1:])[:, None, :]


def pick_and_sum(hot, rows, copies):
    vmem = pl.BlockSpec(memory_space=pltpu.VMEM)
    count = hot.shape[0]
    return pl.pallas_call(
        pick_sum_kernel,
        out_shape=(
            jax.ShapeDtypeStruct((count, rows.shape[1]), BF16),
            jax.ShapeDtypeStruct((copies, 1, count), F32),
        ),
        in_specs=[vmem, pl.BlockSpec(memory_space=pltpu.HBM)],
        out_specs=(vmem, vmem),
        scratch_shapes=[pltpu.VMEM(rows.shape, BF16), pltpu.SemaphoreType.DMA((2,))],
        compiler_params=pltpu.CompilerParams(vmem_limit_bytes=48 * 2**20),
    )(hot, rows)


def row_scale(sum_ref, width):
    total = jnp.sum(sum_ref[:, 0, :], axis=0, keepdims=True)
    scale = lax.rsqrt(total * (1.0 / width) + EPSILON)
    return jnp.broadcast_to(scale, (128, scale.shape[1])).T


def normed(x, scale, gain):
    return (x.astype(F32) * scale * gain.astype(F32)).astype(BF16)


def add_products(acc, x, wq_ref, wk_ref, wv_ref, wkv_ref):
    wide = wq_ref.shape[1]
    wkv_ref[:, :HEAD] = wk_ref[...]
    wkv_ref[:, HEAD:] = wv_ref[...]
    acc[:, :wide] += mm(x, wq_ref[...])
    acc[:, wide:] += mm(x, wkv_ref[...])


def project_kernel(width, count, first, order_ref, sum_ref, *refs):
    blocks = refs[:count]
    gain_ref, wq_ref, wk_ref, wv_ref = refs[count : count + 4]
    before = None if first else refs[count + 4]
    acc_ref, x_ref, scale_ref, wkv_ref = refs[-4:]
    step = pl.program_id(0)

    @pl.when(step == 0)
    def _():
        scale_ref[...] = row_scale(sum_ref, width)
        acc_ref[...] = jnp.zeros_like(acc_ref) if first else before[...]

    for i, block in enumerate(blocks):

        @pl.when(step == i)
        def _(block=block):
            x_ref[...] = normed(block[...], scale_ref[:, 0:1], gain_ref[0])

    add_products(acc_ref, x_ref[...], wq_ref, wk_ref, wv_ref, wkv_ref)


def project(order, sums, blocks, gain, wq, wk, wv, before=None):
    rows, part = blocks[0].shape
    columns = wq.shape[1] + wk.shape[1] + wv.shape[1]
    count = len(blocks)

    def whole(a):
        return pl.BlockSpec(a.shape, lambda i, order: (0,) * a.ndim)

    extra = [] if before is None else [before]
    return pl.pallas_call(
        functools.partial(project_kernel, wq.shape[0], count, before is None),
        out_shape=jax.ShapeDtypeStruct((rows, columns), F32),
        grid_spec=pltpu.PrefetchScalarGridSpec(
            num_scalar_prefetch=1,
            grid=(count,),
            in_specs=[whole(sums)]
            + [whole(b) for b in blocks]
            + [pl.BlockSpec((1, 1, part), lambda i, order: (order[i], 0, 0))]
            + [
                pl.BlockSpec((part, w.shape[1]), lambda i, order: (order[i], 0))
                for w in (wq, wk, wv)
            ]
            + [whole(a) for a in extra],
            out_specs=pl.BlockSpec((rows, columns), lambda i, order: (0, 0)),
            scratch_shapes=[
                pltpu.VMEM((rows, part), BF16),
                pltpu.VMEM((rows, 128), F32),
                pltpu.VMEM((part, 2 * HEAD), BF16),
            ],
        ),
        compiler_params=pltpu.CompilerParams(vmem_limit_bytes=32 * 2**20),
        cost_estimate=pl.CostEstimate(
            flops=2 * rows * part * count * columns * 3,
            bytes_accessed=2 * part * count * columns,
            transcendentals=0,
        ),
    )(order, sums, *blocks, gain, wq, wk, wv, *extra)


def attend_kernel(
    width,
    info_ref,
    sum_ref,
    low_ref,
    high_ref,
    gain_ref,
    wq_ref,
    wk_ref,
    wv_ref,
    before_ref,
    cos_ref,
    sin_ref,
    pool_ref,
    back_ref,
    out_ref,
    acc_ref,
    x_ref,
    wkv_ref,
    q_ref,
    k_ref,
    v_ref,
    o_ref,
):
    scale = row_scale(sum_ref, width)[:, 0:1]
    half = low_ref.shape[0]
    x_ref[:half] = normed(low_ref[...], scale[:half], gain_ref[...])
    x_ref[half:] = normed(high_ref[...], scale[half:], gain_ref[...])
    acc_ref[...] = before_ref[...]
    add_products(acc_ref, x_ref[...], wq_ref, wk_ref, wv_ref, wkv_ref)

    cos = cos_ref[...]
    sin = sin_ref[...]

    def turn(part):
        return (part * cos + pltpu.roll(part, HEAD // 2, 1) * sin).astype(BF16)

    heads = wq_ref.shape[1] // HEAD
    for h in range(heads):
        cut = slice(h * HEAD, (h + 1) * HEAD)
        q_ref[:, cut] = turn(acc_ref[:, cut])
    k_ref[...] = turn(acc_ref[:, heads * HEAD : (heads + 1) * HEAD])
    v_ref[...] = acc_ref[:, (heads + 1) * HEAD :].astype(BF16)

    family = FORK * STEPS
    scale = 1.0 / math.sqrt(HEAD)
    row_at = iota((heads * family, family), 0) % family
    key_at = iota((heads * family, family), 1)
    own_mask = (row_at // STEPS == key_at // STEPS) & (row_at >= key_at)

    @pl.loop(0, PARENTS_HERE)
    def _(j):
        at = pl.ds(pl.multiple_of(j * family, family), family)
        q = jnp.concatenate([q_ref[at, h * HEAD : (h + 1) * HEAD] for h in range(heads)], axis=0)
        own = jnp.where(own_mask, mm_nt(q, k_ref[at, :]) * scale, -jnp.inf)
        own_top = jnp.max(own, axis=1, keepdims=True)
        own_weight = jnp.exp(own - own_top)
        own_total = jnp.sum(own_weight, axis=1, keepdims=True)
        own_mix = mm(own_weight.astype(BF16), v_ref[at, :])
        length = info_ref[j, MOST_PAGES]
        for n in range(1, MOST_PAGES + 1):

            @pl.when(length == n)
            def _(n=n):
                ids = [info_ref[j, i] for i in range(n)]
                keys = jnp.concatenate([pool_ref[i, 0] for i in ids], axis=0)
                values = jnp.concatenate([pool_ref[i, 1] for i in ids], axis=0)
                path = mm_nt(q, keys) * scale
                path_top = jnp.max(path, axis=1, keepdims=True)
                weight = jnp.exp(path - path_top)
                path_total = jnp.sum(weight, axis=1, keepdims=True)
                path_mix = mm(weight.astype(BF16), values)
                top = jnp.maximum(path_top, own_top)
                path_factor = jnp.exp(path_top - top)
                own_factor = jnp.exp(own_top - top)
                both = path_mix * path_factor + own_mix * own_factor
                out = both / (path_total * path_factor + own_total * own_factor)
                out = out.astype(BF16)
                for h in range(heads):
                    o_ref[at, h * HEAD : (h + 1) * HEAD] = out[h * family : (h + 1) * family]

    out_ref[...] = mm_tn(back_ref[...], o_ref[...]).astype(BF16)


def attend(info, sums, low, high, gain, wq, wk, wv, before, cos, sin, pool, back):
    rows, columns = before.shape
    part = low.shape[1]
    wide = back.shape[1]
    vmem = pl.BlockSpec(memory_space=pltpu.VMEM)
    smem = pl.BlockSpec(memory_space=pltpu.SMEM)
    return pl.pallas_call(
        functools.partial(attend_kernel, 8 * part),
        out_shape=jax.ShapeDtypeStruct((wide, wq.shape[1]), BF16),
        in_specs=[smem] + [vmem] * 12,
        out_specs=vmem,
        scratch_shapes=[
            pltpu.VMEM((rows, columns), F32),
            pltpu.VMEM((rows, part), BF16),
            pltpu.VMEM((part, 2 * HEAD), BF16),
            pltpu.VMEM((rows, wq.shape[1]), BF16),
            pltpu.VMEM((rows, HEAD), BF16),
            pltpu.VMEM((rows, HEAD), BF16),
            pltpu.VMEM((rows, wq.shape[1]), BF16),
        ],
        compiler_params=pltpu.CompilerParams(vmem_limit_bytes=32 * 2**20),
        cost_estimate=pl.CostEstimate(
            flops=2 * rows * part * columns * 6, bytes_accessed=2 * part * columns, transcendentals=0
        ),
    )(info, sums, low, high, gain, wq, wk, wv, before, cos, sin, pool, back)


def moves(dy, dz):
    return [(t, ((t // 2 + dy) % 4) * 2 + (t + dz) % 2) for t in range(8)]


def after_leave(slots, groups, me, tables, arrays, send, own_hot, other_hot):
    (norm_gain, wq, wk, wv, kv_pool) = arrays
    wide, width = send.shape
    rows = PARENTS_HERE * FORK * STEPS
    team = lax.axis_size("tensor")
    t = lax.axis_index("tensor")
    came = lax.all_to_all(send.reshape(groups, wide // groups, width), "sample", 0, 0)
    from_hot, info = arrive(slots, groups, me, *tables, rows)

    def place(dy, dz):
        return ((t // 2 + dy) % 4) * 2 + (t + dz) % 2

    def order(*keys):
        return jnp.stack([place(*key) for key in keys]).astype(jnp.int32)

    last = [lax.dynamic_slice_in_dim(w, place(2, 1) * width, width) for w in (wq, wk, wv)]
    gain = norm_gain.reshape(team, 1, -1)
    last_gain = lax.dynamic_slice_in_dim(norm_gain, place(2, 1) * width, width).reshape(1, -1)

    pages = info[:, MOST_PAGES]
    positions = (
        jnp.repeat(pages * PAGE, FORK * STEPS)
        + jnp.tile(jnp.arange(STEPS, dtype=jnp.int32), PARENTS_HERE * FORK)
    ).astype(F32)
    inverse = ROPE_THETA ** (-2.0 * jnp.arange(HEAD // 2, dtype=F32) / HEAD)
    angles = positions[:, None] * inverse[None, :]
    cos, sin = jnp.cos(angles), jnp.sin(angles)
    cos = jnp.concatenate([cos, cos], axis=1)
    sin = jnp.concatenate([-sin, sin], axis=1)
    came, from_hot, info, cos, sin, gain, last_gain, *last = lax.optimization_barrier(
        (came, from_hot, info, cos, sin, gain, last_gain, *last)
    )
    mine, sums = pick_and_sum(from_hot, came.reshape(wide, width), team)

    def shift(block, dy, dz):
        return lax.ppermute(block, "tensor", moves(dy, dz))

    sums = lax.all_to_all(sums, "tensor", 0, 0)
    b30, b10, b01 = shift(mine, 1, 0), shift(mine, -1, 0), shift(mine, 0, 1)
    (b30,) = lax.optimization_barrier((b30,))
    b20, b31 = shift(b30, 1, 0), shift(b30, 0, 1)
    b10, b01 = lax.optimization_barrier((b10, b01))
    second = (b20, shift(b01, -1, 0), b31)
    acc = project(
        order((0, 0), (3, 0), (1, 0), (0, 1)), sums, [mine, b30, b10, b01], gain, wq, wk, wv
    )
    b20, b11, b31, acc = lax.optimization_barrier((*second, acc))
    half = rows // 2
    low, high = shift(b31[:half], 1, 0), shift(b11[half:], -1, 0)
    acc = project(order((2, 0), (1, 1), (3, 1)), sums, [b20, b11, b31], gain, wq, wk, wv, acc)
    low, high, acc = lax.optimization_barrier((low, high, acc))
    back = attend(
        info, sums, low, high, last_gain, *last, acc, cos, sin, kv_pool, from_hot
    )
    home = lax.all_to_all(back.reshape(groups, -1, back.shape[1]), "sample", 0, 0)
    own, other = settle(own_hot, other_hot, home.reshape(-1, back.shape[1]))
    return own + lax.ppermute(other, "sample", swap(groups))


def swap(groups):
    return [(i, i ^ 1) for i in range(groups)]


def local(
    branch_tokens,
    norm_gain,
    query_weight,
    key_weight,
    value_weight,
    kv_pool,
    parent_owner,
    parent_pages,
    page_table,
    child_parent,
):
    groups = lax.axis_size("sample")
    rows = branch_tokens.shape[0]
    me = lax.axis_index("sample").astype(jnp.int32).reshape(1)
    tables = (child_parent, parent_owner, parent_pages, page_table)
    arrays = (norm_gain, query_weight, key_weight, value_weight, kv_pool)
    other = lax.ppermute(branch_tokens, "sample", swap(groups))
    own_hot, other_hot, fits = leave(SLOTS, groups, me, *tables[:2], rows)
    other, own_hot, other_hot, fits = lax.optimization_barrier((other, own_hot, other_hot, fits))
    send = fill_slots(own_hot, other_hot, branch_tokens, other)

    def usual():
        return after_leave(SLOTS, groups, me, tables, arrays, send, own_hot, other_hot)

    def crowded():
        most = rows // STEPS // 2
        own, others, _ = leave(most, groups, me, *tables[:2], rows)
        wider = fill_slots(own, others, branch_tokens, other)
        return after_leave(most, groups, me, tables, arrays, wider, own, others)

    return lax.cond(fits[0] == 1, usual, crowded)


def solution(mesh):
    return jax.shard_map(
        local,
        mesh=mesh,
        in_specs=(
            P("sample", "tensor"),
            P(),
            P(None, "tensor"),
            P(None, "tensor"),
            P(None, "tensor"),
            P("sample", None, None, "tensor"),
            P(),
            P(),
            P(),
            P(),
        ),
        out_specs=P("sample", "tensor"),
        check_vma=False,
    )
```

```python
import functools
import math

import jax
import jax.numpy as jnp
from jax import lax
from jax.experimental import pallas as pl
from jax.experimental.pallas import tpu as pltpu
from jax.sharding import PartitionSpec as P

HEAD = 128
PAGE = 128
STEPS = 4
FORK = 8
PARENTS_HERE = 8
MOST_PAGES = 5
ROPE_THETA = 10000.0
EPSILON = 1e-06
SLOTS = 10
CHUNK = 640

BF16 = jnp.bfloat16
F32 = jnp.float32


def iota(shape, dim):
    return lax.broadcasted_iota(jnp.int32, shape, dim)


def one(mask):
    return jnp.where(mask, 1.0, 0.0).astype(BF16)


def mm(a, b):
    return lax.dot_general(a, b, (((1,), (0,)), ((), ())), preferred_element_type=F32)


def over(count, body):
    if count == 1:
        body(0)
    else:
        pl.loop(0, count)(body)


def chunk(i, size):
    return pl.ds(pl.multiple_of(i * size, size), size)


def mm_nt(a, b):
    return lax.dot_general(a, b, (((1,), (1,)), ((), ())), preferred_element_type=F32)


def owners(child_ref, owner_ref, mask_ref):
    groups, children = mask_ref.shape
    parents = owner_ref.shape[1]
    parent_hot = one(iota((parents, children), 0) == child_ref[...])
    owner = jnp.broadcast_to(owner_ref[...].astype(F32), (16, parents)).astype(BF16)
    owner_of = mm(owner, parent_hot)[0:1].astype(jnp.int32)
    mask_ref[...] = jnp.where(iota((groups, children), 0) == owner_of, 1.0, 0.0)


def targets(slots, me, mask_ref, rows):
    here = rows // STEPS
    core = lax.rem(me, 2)
    chip = lax.div(me, 2)
    mask = mask_ref[:, pl.ds(pl.multiple_of(chip * 2 * here, 2 * here), 2 * here)]
    ahead = mm(mask.astype(BF16), one(iota((128, 128), 0) < iota((128, 128), 1)))
    rank = jnp.sum(mask * ahead, axis=0, keepdims=True).astype(jnp.int32)
    owner = jnp.sum(mask * iota(mask.shape, 0).astype(F32), axis=0, keepdims=True)
    keep = jnp.where(rank % 2 == core, 1.0, 0.0)
    turn = (rank // 2).astype(F32)
    at = iota((16, 2 * here), 0)
    facts = jnp.where(at == 0, owner, jnp.where(at == 1, turn, keep)).astype(BF16)
    found = []
    for side in (core, 1 - core):
        grow = one(iota((2 * here, rows), 0) == side * here + iota((2 * here, rows), 1) // STEPS)
        of_row = mm(facts, grow)
        target = of_row[0:1] * (slots * STEPS) + of_row[1:2] * STEPS
        target = target.astype(jnp.int32) + iota((1, rows), 1) % STEPS
        found.append(jnp.where(of_row[2:3] > 0.5, target, -1))
    return found


def leave_kernel(slots, me_ref, child_ref, owner_ref, own_ref, other_ref, fits_ref, mask_ref):
    me = me_ref[0]
    rows = own_ref.shape[1]
    here = rows // STEPS
    children = child_ref.shape[1]
    owners(child_ref, owner_ref, mask_ref)
    counted = iota((children, 128), 1) == iota((children, 128), 0) // (2 * here)
    most = jnp.max(mm(mask_ref[...].astype(BF16), one(counted))).astype(jnp.int32)
    fits_ref[0] = jnp.where(most <= 2 * slots, 1, 0)

    for ref, target in zip((own_ref, other_ref), targets(slots, me, mask_ref, rows)):

        def fill(i, ref=ref, target=target):
            ref[chunk(i, CHUNK), :] = one(iota((CHUNK, rows), 0) + i * CHUNK == target)

        over(ref.shape[0] // CHUNK, fill)


def leave(slots, groups, me, child_parent, parent_owner, rows):
    vmem = pl.BlockSpec(memory_space=pltpu.VMEM)
    smem = pl.BlockSpec(memory_space=pltpu.SMEM)
    hot = jax.ShapeDtypeStruct((groups * slots * STEPS, rows), BF16)
    return pl.pallas_call(
        functools.partial(leave_kernel, slots),
        out_shape=(hot, hot, jax.ShapeDtypeStruct((1,), jnp.int32)),
        in_specs=[smem, vmem, vmem],
        out_specs=(vmem, vmem, smem),
        scratch_shapes=[pltpu.VMEM((groups, child_parent.shape[0]), F32)],
        compiler_params=pltpu.CompilerParams(vmem_limit_bytes=24 * 2**20),
        cost_estimate=pl.CostEstimate(flops=10**9, bytes_accessed=2**20, transcendentals=0),
    )(me, child_parent.reshape(1, -1), parent_owner.reshape(1, -1))


def arrive_kernel(
    slots,
    me_ref,
    child_ref,
    owner_ref,
    pages_ref,
    table_ref,
    from_ref,
    own_ref,
    other_ref,
    info_ref,
    mask_ref,
):
    me = me_ref[0]
    children = child_ref.shape[1]
    parents = owner_ref.shape[1]
    rows, wide = from_ref.shape
    here = rows // STEPS
    owner = owner_ref[...]
    parent_hot = one(iota((parents, children), 0) == child_ref[...])
    mine_parent = owner == me
    tri = one(iota((128, 128), 0) < iota((128, 128), 1))
    parent_rank = mm(one(jnp.broadcast_to(mine_parent, (16, parents))), tri)
    parent_rank = parent_rank[0:1].astype(jnp.int32)
    mine_hot = (iota((PARENTS_HERE, parents), 0) == parent_rank) & mine_parent
    pages = jnp.sum(jnp.where(mine_hot, pages_ref[...], 0), axis=1, keepdims=True)
    mine_hot = one(mine_hot)
    table = mm(mine_hot, table_ref[...].astype(F32).astype(BF16)).astype(jnp.int32)
    info_ref[...] = jnp.where(iota((PARENTS_HERE, 8), 1) == MOST_PAGES, pages, table)
    member = mm(mine_hot, parent_hot)
    carry = jnp.zeros((PARENTS_HERE, 1), F32)
    places, spots = [], []
    for block in range(children // 128):
        part = member[:, block * 128 : (block + 1) * 128]
        ahead = mm(part.astype(BF16), tri) + carry
        carry = carry + jnp.sum(part, axis=1, keepdims=True)
        is_mine = jnp.sum(part, axis=0, keepdims=True)
        place = jnp.sum(
            part * (iota((PARENTS_HERE, 128), 0).astype(F32) * FORK + ahead), axis=0, keepdims=True
        ).astype(jnp.int32)
        in_chip = mm(jnp.broadcast_to(is_mine, (16, 128)).astype(BF16), tri)[0:1].astype(jnp.int32)
        chip = (block * 128 + iota((1, 128), 1)) // (2 * here)
        spot = (chip * 2 + in_chip % 2) * slots + in_chip // 2
        places.append(jnp.where(is_mine > 0.5, place, -1))
        spots.append(jnp.where(is_mine > 0.5, spot, -1))
    place_hot = one(iota((here, children), 0) == jnp.concatenate(places, axis=1))
    spot = jnp.concatenate(spots, axis=1)
    grow_rows = one(iota((rows, here), 0) // STEPS == iota((rows, here), 1))
    size, deep = CHUNK, CHUNK // STEPS
    grow_columns = one(iota((deep, size), 0) == iota((deep, size), 1) // STEPS)
    same_step = iota((rows, size), 0) % STEPS == iota((rows, size), 1) % STEPS

    def fill(i):
        spot_hot = one(iota((deep, children), 0) + i * deep == spot)
        by_child = mm_nt(place_hot, spot_hot).astype(BF16)
        by_row = mm(mm(grow_rows, by_child).astype(BF16), grow_columns)
        from_ref[:, chunk(i, size)] = jnp.where(same_step, by_row, 0.0).astype(BF16)

    over(wide // CHUNK, fill)

    owners(child_ref, owner_ref, mask_ref)
    for ref, target in zip((own_ref, other_ref), targets(slots, me, mask_ref, rows)):
        column = jnp.broadcast_to(target.astype(F32), (128, rows)).T[:, 0:1].astype(jnp.int32)

        def put(i, ref=ref, column=column):
            ref[:, chunk(i, size)] = one(iota((rows, size), 1) + i * size == column)

        over(wide // CHUNK, put)


def arrive(slots, groups, me, child_parent, parent_owner, parent_pages, page_table, rows):
    hot = jax.ShapeDtypeStruct((rows, groups * slots * STEPS), BF16)
    vmem = pl.BlockSpec(memory_space=pltpu.VMEM)
    smem = pl.BlockSpec(memory_space=pltpu.SMEM)
    return pl.pallas_call(
        functools.partial(arrive_kernel, slots),
        out_shape=(
            hot,
            hot,
            hot,
            jax.ShapeDtypeStruct((PARENTS_HERE, 8), jnp.int32),
        ),
        in_specs=[smem] + [vmem] * 4,
        out_specs=(vmem, vmem, vmem, vmem),
        scratch_shapes=[pltpu.VMEM((groups, child_parent.shape[0]), F32)],
        compiler_params=pltpu.CompilerParams(vmem_limit_bytes=24 * 2**20),
        cost_estimate=pl.CostEstimate(flops=2 * 10**9, bytes_accessed=2**20, transcendentals=0),
    )(
        me,
        child_parent.reshape(1, -1),
        parent_owner.reshape(1, -1),
        parent_pages.reshape(1, -1),
        jnp.pad(page_table, ((0, 0), (0, 8 - page_table.shape[1]))),
    )


def fill_kernel(own_hot_ref, other_hot_ref, own_ref, other_ref, out_ref):
    def fill(i):
        at = chunk(i, CHUNK)
        filled = mm(own_hot_ref[at, :], own_ref[...]) + mm(other_hot_ref[at, :], other_ref[...])
        out_ref[at, :] = filled.astype(BF16)

    over(out_ref.shape[0] // CHUNK, fill)


def fill_slots(own_hot, other_hot, own, other):
    vmem = pl.BlockSpec(memory_space=pltpu.VMEM)
    return pl.pallas_call(
        fill_kernel,
        out_shape=jax.ShapeDtypeStruct((own_hot.shape[0], own.shape[1]), BF16),
        in_specs=[vmem] * 4,
        out_specs=vmem,
        compiler_params=pltpu.CompilerParams(vmem_limit_bytes=24 * 2**20),
    )(own_hot, other_hot, own, other)


def place_rows(hot_ref, rows_ref, acc_ref):
    if rows_ref.shape[0] == CHUNK:
        return mm(hot_ref[...], rows_ref[...])
    acc_ref[...] = jnp.zeros_like(acc_ref)

    @pl.loop(0, rows_ref.shape[0] // CHUNK)
    def _(i):
        at = chunk(i, CHUNK)
        acc_ref[...] += mm(hot_ref[:, at], rows_ref[at, :])

    return acc_ref[...]


def settle_kernel(hot_ref, rows_ref, out_ref, acc_ref):
    out_ref[...] = place_rows(hot_ref, rows_ref, acc_ref).astype(BF16)


def settle(hot, rows):
    vmem = pl.BlockSpec(memory_space=pltpu.VMEM)
    return pl.pallas_call(
        settle_kernel,
        out_shape=jax.ShapeDtypeStruct((hot.shape[0], rows.shape[1]), BF16),
        in_specs=[vmem, vmem],
        out_specs=vmem,
        scratch_shapes=[pltpu.VMEM((hot.shape[0], rows.shape[1]), F32)],
        compiler_params=pltpu.CompilerParams(vmem_limit_bytes=24 * 2**20),
        cost_estimate=pl.CostEstimate(
            flops=2 * hot.shape[0] * hot.shape[1] * rows.shape[1],
            bytes_accessed=2 * rows.shape[0] * rows.shape[1],
            transcendentals=0,
        ),
    )(hot, rows)


def pick_sum_kernel(hot_ref, rows_ref, out_ref, sum_ref, acc_ref, held_ref, sem):
    copy = pltpu.make_async_copy(hot_ref, held_ref, sem)
    copy.start()
    copy.wait()
    x = place_rows(held_ref, rows_ref, acc_ref)
    out_ref[...] = x.astype(BF16)
    total = jnp.sum(x * x, axis=1, keepdims=True)
    total = jnp.broadcast_to(total, (total.shape[0], 128)).T
    sum_ref[...] = jnp.broadcast_to(total[0:1], sum_ref.shape[:1] + total.shape[1:])[:, None, :]


def pick_and_sum(hot, rows, copies):
    vmem = pl.BlockSpec(memory_space=pltpu.VMEM)
    count = hot.shape[0]
    return pl.pallas_call(
        pick_sum_kernel,
        out_shape=(
            jax.ShapeDtypeStruct((count, rows.shape[1]), BF16),
            jax.ShapeDtypeStruct((copies, 1, count), F32),
        ),
        in_specs=[pl.BlockSpec(memory_space=pltpu.HBM), vmem],
        out_specs=(vmem, vmem),
        scratch_shapes=[
            pltpu.VMEM((count, rows.shape[1]), F32),
            pltpu.VMEM(hot.shape, BF16),
            pltpu.SemaphoreType.DMA,
        ],
        compiler_params=pltpu.CompilerParams(vmem_limit_bytes=24 * 2**20),
    )(hot, rows)


def row_scale(sum_ref, width):
    total = jnp.sum(sum_ref[:, 0, :], axis=0, keepdims=True)
    scale = lax.rsqrt(total * (1.0 / width) + EPSILON)
    return jnp.broadcast_to(scale, (128, scale.shape[1])).T


def normed(x, scale, gain):
    return (x.astype(F32) * scale * gain.astype(F32)).astype(BF16)


def add_products(acc, x, wq, wkv):
    wide = wq.shape[1]
    acc[:, :wide] += mm(x, wq)
    acc[:, wide:] += mm(x, wkv)


def project_kernel(width, count, first, order_ref, sum_ref, *refs):
    blocks = refs[:count]
    gain_ref, wq_ref, wk_ref, wv_ref = refs[count : count + 4]
    before = None if first else refs[count + 4]
    acc_ref, x_ref, wq_held, wkv_held, x_sems, w_sems = refs[-6:]
    part = x_ref.shape[2]

    def copies(i, block):
        at = chunk(order_ref[i], part)
        return [
            pltpu.make_async_copy(block, x_ref.at[i], x_sems.at[i]),
            pltpu.make_async_copy(wq_ref.at[at], wq_held.at[i], w_sems.at[i, 0]),
            pltpu.make_async_copy(wk_ref.at[at], wkv_held.at[i, :, :HEAD], w_sems.at[i, 1]),
            pltpu.make_async_copy(wv_ref.at[at], wkv_held.at[i, :, HEAD:], w_sems.at[i, 2]),
        ]

    for i in range(count):
        for copy in copies(i, blocks[i]):
            copy.start()
    scale = row_scale(sum_ref, width)[:, 0:1]
    acc_ref[...] = jnp.zeros_like(acc_ref) if first else before[...]

    @pl.loop(0, count)
    def _(i):
        for copy in copies(i, blocks[0]):
            copy.wait()
        x = normed(x_ref[i], scale, gain_ref[order_ref[i]])
        add_products(acc_ref, x, wq_held[i], wkv_held[i])


def project(order, sums, blocks, gain, wq, wk, wv, before=None):
    rows, part = blocks[0].shape
    columns = wq.shape[1] + wk.shape[1] + wv.shape[1]
    count = len(blocks)
    smem = pl.BlockSpec(memory_space=pltpu.SMEM)
    vmem = pl.BlockSpec(memory_space=pltpu.VMEM)
    hbm = pl.BlockSpec(memory_space=pltpu.HBM)
    extra = [] if before is None else [before]
    return pl.pallas_call(
        functools.partial(project_kernel, wq.shape[0], count, before is None),
        out_shape=jax.ShapeDtypeStruct((rows, columns), F32),
        in_specs=[smem, vmem] + [hbm] * count + [vmem, hbm, hbm, hbm] + [vmem] * len(extra),
        out_specs=vmem,
        scratch_shapes=[
            pltpu.VMEM((count, rows, part), BF16),
            pltpu.VMEM((count, part, wq.shape[1]), BF16),
            pltpu.VMEM((count, part, 2 * HEAD), BF16),
            pltpu.SemaphoreType.DMA((count,)),
            pltpu.SemaphoreType.DMA((count, 3)),
        ],
        compiler_params=pltpu.CompilerParams(vmem_limit_bytes=28 * 2**20),
        cost_estimate=pl.CostEstimate(
            flops=2 * rows * part * count * columns * 2,
            bytes_accessed=2 * part * count * columns,
            transcendentals=0,
        ),
    )(order, sums, *blocks, gain, wq, wk, wv, *extra)


def attend_kernel(
    width,
    info_ref,
    sum_ref,
    low_ref,
    high_ref,
    gain_ref,
    wq_ref,
    wk_ref,
    wv_ref,
    before_ref,
    cos_ref,
    sin_ref,
    pool_ref,
    back_ref,
    out_ref,
    acc_ref,
    x_ref,
    wkv_ref,
    q_ref,
    k_ref,
    v_ref,
    o_ref,
):
    scale = row_scale(sum_ref, width)[:, 0:1]
    half = low_ref.shape[0]
    x_ref[:half] = normed(low_ref[...], scale[:half], gain_ref[...])
    x_ref[half:] = normed(high_ref[...], scale[half:], gain_ref[...])
    acc_ref[...] = before_ref[...]
    wkv_ref[:, :HEAD] = wk_ref[...]
    wkv_ref[:, HEAD:] = wv_ref[...]
    add_products(acc_ref, x_ref[...], wq_ref[...], wkv_ref[...])

    cos = cos_ref[...]
    sin = sin_ref[...]

    def turn(part):
        return (part * cos + pltpu.roll(part, HEAD // 2, 1) * sin).astype(BF16)

    heads = wq_ref.shape[1] // HEAD
    for h in range(heads):
        cut = slice(h * HEAD, (h + 1) * HEAD)
        q_ref[:, cut] = turn(acc_ref[:, cut])
    k_ref[...] = turn(acc_ref[:, heads * HEAD : (heads + 1) * HEAD])
    v_ref[...] = acc_ref[:, (heads + 1) * HEAD :].astype(BF16)

    family = FORK * STEPS
    scale = 1.0 / math.sqrt(HEAD)
    row_at = iota((heads * family, family), 0) % family
    key_at = iota((heads * family, family), 1)
    page_at = iota((heads * family, MOST_PAGES * PAGE), 1) // PAGE
    own_mask = (row_at // STEPS == key_at // STEPS) & (row_at >= key_at)

    @pl.loop(0, PARENTS_HERE, unroll=4)
    def _(j):
        at = pl.ds(pl.multiple_of(j * family, family), family)
        q = jnp.concatenate([q_ref[at, h * HEAD : (h + 1) * HEAD] for h in range(heads)], axis=0)
        own = jnp.where(own_mask, mm_nt(q, k_ref[at, :]) * scale, -jnp.inf)
        own_top = jnp.max(own, axis=1, keepdims=True)
        own_weight = jnp.exp(own - own_top)
        own_total = jnp.sum(own_weight, axis=1, keepdims=True)
        own_mix = mm(own_weight.astype(BF16), v_ref[at, :])
        length = info_ref[j, MOST_PAGES]
        ids = [info_ref[j, i] for i in range(MOST_PAGES)]
        keys = jnp.concatenate([pool_ref[i, 0] for i in ids], axis=0)
        values = jnp.concatenate([pool_ref[i, 1] for i in ids], axis=0)
        path = jnp.where(page_at < length, mm_nt(q, keys) * scale, -jnp.inf)
        path_top = jnp.max(path, axis=1, keepdims=True)
        weight = jnp.exp(path - path_top)
        path_total = jnp.sum(weight, axis=1, keepdims=True)
        path_mix = mm(weight.astype(BF16), values)
        top = jnp.maximum(path_top, own_top)
        path_factor = jnp.exp(path_top - top)
        own_factor = jnp.exp(own_top - top)
        both = path_mix * path_factor + own_mix * own_factor
        out = both / (path_total * path_factor + own_total * own_factor)
        out = out.astype(BF16)
        for h in range(heads):
            o_ref[at, h * HEAD : (h + 1) * HEAD] = out[h * family : (h + 1) * family]


    def fill(i):
        at = chunk(i, CHUNK)
        out_ref[at, :] = mm(back_ref[at, :], o_ref[...]).astype(BF16)

    over(out_ref.shape[0] // CHUNK, fill)


def attend(info, sums, low, high, gain, wq, wk, wv, before, cos, sin, pool, back):
    rows, columns = before.shape
    part = low.shape[1]
    wide = back.shape[0]
    vmem = pl.BlockSpec(memory_space=pltpu.VMEM)
    smem = pl.BlockSpec(memory_space=pltpu.SMEM)
    return pl.pallas_call(
        functools.partial(attend_kernel, 8 * part),
        out_shape=jax.ShapeDtypeStruct((wide, wq.shape[1]), BF16),
        in_specs=[smem] + [vmem] * 12,
        out_specs=vmem,
        scratch_shapes=[
            pltpu.VMEM((rows, columns), F32),
            pltpu.VMEM((rows, part), BF16),
            pltpu.VMEM((part, 2 * HEAD), BF16),
            pltpu.VMEM((rows, wq.shape[1]), BF16),
            pltpu.VMEM((rows, HEAD), BF16),
            pltpu.VMEM((rows, HEAD), BF16),
            pltpu.VMEM((rows, wq.shape[1]), BF16),
        ],
        compiler_params=pltpu.CompilerParams(vmem_limit_bytes=24 * 2**20),
        cost_estimate=pl.CostEstimate(
            flops=2 * rows * part * columns * 6, bytes_accessed=2 * part * columns, transcendentals=0
        ),
    )(info, sums, low, high, gain, wq, wk, wv, before, cos, sin, pool, back)


def moves(dy, dz):
    return [(t, ((t // 2 + dy) % 4) * 2 + (t + dz) % 2) for t in range(8)]


def after_leave(slots, groups, me, tables, arrays, send):
    (norm_gain, wq, wk, wv, kv_pool) = arrays
    wide, width = send.shape
    rows = PARENTS_HERE * FORK * STEPS
    team = lax.axis_size("tensor")
    t = lax.axis_index("tensor")
    came = lax.all_to_all(send.reshape(groups, wide // groups, width), "sample", 0, 0)
    from_hot, own_hot, other_hot, info = arrive(slots, groups, me, *tables, rows)
    back_hot = from_hot.T

    def place(dy, dz):
        return ((t // 2 + dy) % 4) * 2 + (t + dz) % 2

    def order(*keys):
        return jnp.stack([place(*key) for key in keys]).astype(jnp.int32)

    last = [lax.dynamic_slice_in_dim(w, place(2, 1) * width, width) for w in (wq, wk, wv)]
    gain = norm_gain.reshape(team, 1, -1)
    last_gain = lax.dynamic_slice_in_dim(norm_gain, place(2, 1) * width, width).reshape(1, -1)

    pages = info[:, MOST_PAGES]
    positions = (
        jnp.repeat(pages * PAGE, FORK * STEPS)
        + jnp.tile(jnp.arange(STEPS, dtype=jnp.int32), PARENTS_HERE * FORK)
    ).astype(F32)
    inverse = ROPE_THETA ** (-2.0 * jnp.arange(HEAD // 2, dtype=F32) / HEAD)
    angles = positions[:, None] * inverse[None, :]
    cos, sin = jnp.cos(angles), jnp.sin(angles)
    cos = jnp.concatenate([cos, cos], axis=1)
    sin = jnp.concatenate([-sin, sin], axis=1)
    came, from_hot, info, cos, sin, gain, last_gain, *last = lax.optimization_barrier(
        (came, from_hot, info, cos, sin, gain, last_gain, *last)
    )
    back_hot, own_hot, other_hot, from_hot = lax.optimization_barrier(
        (back_hot, own_hot, other_hot, from_hot)
    )
    mine, sums = pick_and_sum(from_hot, came.reshape(wide, width), team)

    def shift(block, dy, dz):
        return lax.ppermute(block, "tensor", moves(dy, dz))

    sums = lax.all_to_all(sums, "tensor", 0, 0)
    b30, b10, b01 = shift(mine, 1, 0), shift(mine, -1, 0), shift(mine, 0, 1)
    (b30,) = lax.optimization_barrier((b30,))
    b20, b31 = shift(b30, 1, 0), shift(b30, 0, 1)
    second = (b20, shift(b01, -1, 0), b31)
    acc = project(
        order((0, 0), (3, 0), (1, 0), (0, 1)), sums, [mine, b30, b10, b01], gain, wq, wk, wv
    )
    b20, b11, b31, acc = lax.optimization_barrier((*second, acc))
    half = rows // 2
    low, high = shift(b31[:half], 1, 0), shift(b11[half:], -1, 0)
    acc = project(order((2, 0), (1, 1), (3, 1)), sums, [b20, b11, b31], gain, wq, wk, wv, acc)
    low, high, acc = lax.optimization_barrier((low, high, acc))
    back = attend(
        info, sums, low, high, last_gain, *last, acc, cos, sin, kv_pool, back_hot
    )
    home = lax.all_to_all(back.reshape(groups, -1, back.shape[1]), "sample", 0, 0)
    home = home.reshape(-1, back.shape[1])
    other = settle(other_hot, home)
    return settle(own_hot, home) + lax.ppermute(other, "sample", swap(groups))


def swap(groups):
    return [(i, i ^ 1) for i in range(groups)]


def local(
    branch_tokens,
    norm_gain,
    query_weight,
    key_weight,
    value_weight,
    kv_pool,
    parent_owner,
    parent_pages,
    page_table,
    child_parent,
):
    groups = lax.axis_size("sample")
    rows = branch_tokens.shape[0]
    me = lax.axis_index("sample").astype(jnp.int32).reshape(1)
    tables = (child_parent, parent_owner, parent_pages, page_table)
    arrays = (norm_gain, query_weight, key_weight, value_weight, kv_pool)
    other = lax.ppermute(branch_tokens, "sample", swap(groups))
    own_hot, other_hot, fits = leave(SLOTS, groups, me, *tables[:2], rows)
    other, own_hot, other_hot, fits = lax.optimization_barrier((other, own_hot, other_hot, fits))
    send = fill_slots(own_hot, other_hot, branch_tokens, other)

    def usual():
        return after_leave(SLOTS, groups, me, tables, arrays, send)

    def crowded():
        most = 4 * SLOTS
        own, others, _ = leave(most, groups, me, *tables[:2], rows)
        wider = fill_slots(own, others, branch_tokens, other)
        return after_leave(most, groups, me, tables, arrays, wider)

    return lax.switch(fits[0], [crowded, usual])


def solution(mesh):
    return jax.shard_map(
        local,
        mesh=mesh,
        in_specs=(
            P("sample", "tensor"),
            P(),
            P(None, "tensor"),
            P(None, "tensor"),
            P(None, "tensor"),
            P("sample", None, None, "tensor"),
            P(),
            P(),
            P(),
            P(),
        ),
        out_specs=P("sample", "tensor"),
        check_vma=False,
    )
```

```python
import functools
import math

import jax
import jax.numpy as jnp
from jax import lax
from jax.experimental import pallas as pl
from jax.experimental.pallas import tpu as pltpu
from jax.sharding import PartitionSpec as P

HEAD = 128
PAGE = 128
STEPS = 4
FORK = 8
PARENTS_HERE = 8
MOST_PAGES = 5
ROPE_THETA = 10000.0
EPSILON = 1e-06
SLOTS = 10
CHUNK = 640

BF16 = jnp.bfloat16
F32 = jnp.float32


def iota(shape, dim):
    return lax.broadcasted_iota(jnp.int32, shape, dim)


def one(mask):
    return jnp.where(mask, 1.0, 0.0).astype(BF16)


def mm(a, b):
    return lax.dot_general(a, b, (((1,), (0,)), ((), ())), preferred_element_type=F32)


def over(count, body):
    if count == 1:
        body(0)
    else:
        pl.loop(0, count)(body)


def chunk(i, size):
    return pl.ds(pl.multiple_of(i * size, size), size)


def mm_nt(a, b):
    return lax.dot_general(a, b, (((1,), (1,)), ((), ())), preferred_element_type=F32)


def owners(child_ref, owner_ref, mask_ref):
    groups, children = mask_ref.shape
    parents = owner_ref.shape[1]
    parent_hot = one(iota((parents, children), 0) == child_ref[...])
    owner = jnp.broadcast_to(owner_ref[...].astype(F32), (16, parents)).astype(BF16)
    owner_of = mm(owner, parent_hot)[0:1].astype(jnp.int32)
    mask_ref[...] = jnp.where(iota((groups, children), 0) == owner_of, 1.0, 0.0)


def targets(slots, me, mask_ref, rows):
    here = rows // STEPS
    core = lax.rem(me, 2)
    chip = lax.div(me, 2)
    mask = mask_ref[:, pl.ds(pl.multiple_of(chip * 2 * here, 2 * here), 2 * here)]
    ahead = mm(mask.astype(BF16), one(iota((128, 128), 0) < iota((128, 128), 1)))
    rank = jnp.sum(mask * ahead, axis=0, keepdims=True).astype(jnp.int32)
    owner = jnp.sum(mask * iota(mask.shape, 0).astype(F32), axis=0, keepdims=True)
    keep = jnp.where(rank % 2 == core, 1.0, 0.0)
    turn = (rank // 2).astype(F32)
    at = iota((16, 2 * here), 0)
    facts = jnp.where(at == 0, owner, jnp.where(at == 1, turn, keep)).astype(BF16)
    found = []
    for side in (core, 1 - core):
        grow = one(iota((2 * here, rows), 0) == side * here + iota((2 * here, rows), 1) // STEPS)
        of_row = mm(facts, grow)
        target = of_row[0:1] * (slots * STEPS) + of_row[1:2] * STEPS
        target = target.astype(jnp.int32) + iota((1, rows), 1) % STEPS
        found.append(jnp.where(of_row[2:3] > 0.5, target, -1))
    return found


def leave_kernel(slots, me_ref, child_ref, owner_ref, own_ref, other_ref, fits_ref, mask_ref):
    me = me_ref[0]
    rows = own_ref.shape[1]
    here = rows // STEPS
    children = child_ref.shape[1]
    owners(child_ref, owner_ref, mask_ref)
    counted = iota((children, 128), 1) == iota((children, 128), 0) // (2 * here)
    most = jnp.max(mm(mask_ref[...].astype(BF16), one(counted))).astype(jnp.int32)
    fits_ref[0] = jnp.where(most <= 2 * slots, 1, 0)

    for ref, target in zip((own_ref, other_ref), targets(slots, me, mask_ref, rows)):

        def fill(i, ref=ref, target=target):
            ref[chunk(i, CHUNK), :] = one(iota((CHUNK, rows), 0) + i * CHUNK == target)

        over(ref.shape[0] // CHUNK, fill)


def leave(slots, groups, me, child_parent, parent_owner, rows):
    vmem = pl.BlockSpec(memory_space=pltpu.VMEM)
    smem = pl.BlockSpec(memory_space=pltpu.SMEM)
    hot = jax.ShapeDtypeStruct((groups * slots * STEPS, rows), BF16)
    return pl.pallas_call(
        functools.partial(leave_kernel, slots),
        out_shape=(hot, hot, jax.ShapeDtypeStruct((1,), jnp.int32)),
        in_specs=[smem, vmem, vmem],
        out_specs=(vmem, vmem, smem),
        scratch_shapes=[pltpu.VMEM((groups, child_parent.shape[0]), F32)],
        compiler_params=pltpu.CompilerParams(vmem_limit_bytes=24 * 2**20),
        cost_estimate=pl.CostEstimate(flops=10**9, bytes_accessed=2**20, transcendentals=0),
    )(me, child_parent.reshape(1, -1), parent_owner.reshape(1, -1))


def arrive_kernel(
    slots,
    me_ref,
    child_ref,
    owner_ref,
    pages_ref,
    table_ref,
    from_ref,
    back_ref,
    own_ref,
    other_ref,
    info_ref,
    mask_ref,
):
    me = me_ref[0]
    children = child_ref.shape[1]
    parents = owner_ref.shape[1]
    rows, wide = from_ref.shape
    here = rows // STEPS
    owner = owner_ref[...]
    parent_hot = one(iota((parents, children), 0) == child_ref[...])
    mine_parent = owner == me
    tri = one(iota((128, 128), 0) < iota((128, 128), 1))
    parent_rank = mm(one(jnp.broadcast_to(mine_parent, (16, parents))), tri)
    parent_rank = parent_rank[0:1].astype(jnp.int32)
    mine_hot = (iota((PARENTS_HERE, parents), 0) == parent_rank) & mine_parent
    pages = jnp.sum(jnp.where(mine_hot, pages_ref[...], 0), axis=1, keepdims=True)
    mine_hot = one(mine_hot)
    table = mm(mine_hot, table_ref[...].astype(F32).astype(BF16)).astype(jnp.int32)
    info_ref[...] = jnp.where(iota((PARENTS_HERE, 8), 1) == MOST_PAGES, pages, table)
    member = mm(mine_hot, parent_hot)
    carry = jnp.zeros((PARENTS_HERE, 1), F32)
    places, spots = [], []
    for block in range(children // 128):
        part = member[:, block * 128 : (block + 1) * 128]
        ahead = mm(part.astype(BF16), tri) + carry
        carry = carry + jnp.sum(part, axis=1, keepdims=True)
        is_mine = jnp.sum(part, axis=0, keepdims=True)
        place = jnp.sum(
            part * (iota((PARENTS_HERE, 128), 0).astype(F32) * FORK + ahead), axis=0, keepdims=True
        ).astype(jnp.int32)
        in_chip = mm(jnp.broadcast_to(is_mine, (16, 128)).astype(BF16), tri)[0:1].astype(jnp.int32)
        chip = (block * 128 + iota((1, 128), 1)) // (2 * here)
        spot = (chip * 2 + in_chip % 2) * slots + in_chip // 2
        places.append(jnp.where(is_mine > 0.5, place, -1))
        spots.append(jnp.where(is_mine > 0.5, spot, -1))
    place_hot = one(iota((here, children), 0) == jnp.concatenate(places, axis=1))
    spot = jnp.concatenate(spots, axis=1)
    grow_rows = one(iota((rows, here), 0) // STEPS == iota((rows, here), 1))
    size, deep = CHUNK, CHUNK // STEPS
    grow_columns = one(iota((deep, size), 0) == iota((deep, size), 1) // STEPS)
    same_step = iota((rows, size), 0) % STEPS == iota((rows, size), 1) % STEPS

    def fill(i):
        spot_hot = one(iota((deep, children), 0) + i * deep == spot)
        by_child = mm_nt(place_hot, spot_hot).astype(BF16)
        by_row = mm(mm(grow_rows, by_child).astype(BF16), grow_columns)
        by_row = jnp.where(same_step, by_row, 0.0)
        from_ref[:, chunk(i, size)] = by_row.astype(BF16)
        back_ref[chunk(i, size), :] = by_row.T.astype(BF16)

    over(wide // CHUNK, fill)

    owners(child_ref, owner_ref, mask_ref)
    for ref, target in zip((own_ref, other_ref), targets(slots, me, mask_ref, rows)):
        column = jnp.broadcast_to(target.astype(F32), (128, rows)).T[:, 0:1].astype(jnp.int32)

        def put(i, ref=ref, column=column):
            ref[:, chunk(i, size)] = one(iota((rows, size), 1) + i * size == column)

        over(wide // CHUNK, put)


def arrive(slots, groups, me, child_parent, parent_owner, parent_pages, page_table, rows):
    hot = jax.ShapeDtypeStruct((rows, groups * slots * STEPS), BF16)
    vmem = pl.BlockSpec(memory_space=pltpu.VMEM)
    smem = pl.BlockSpec(memory_space=pltpu.SMEM)
    return pl.pallas_call(
        functools.partial(arrive_kernel, slots),
        out_shape=(
            hot,
            jax.ShapeDtypeStruct(hot.shape[::-1], BF16),
            hot,
            hot,
            jax.ShapeDtypeStruct((PARENTS_HERE, 8), jnp.int32),
        ),
        in_specs=[smem] + [vmem] * 4,
        out_specs=(vmem,) * 5,
        scratch_shapes=[pltpu.VMEM((groups, child_parent.shape[0]), F32)],
        compiler_params=pltpu.CompilerParams(vmem_limit_bytes=24 * 2**20),
        cost_estimate=pl.CostEstimate(flops=2 * 10**9, bytes_accessed=2**20, transcendentals=0),
    )(
        me,
        child_parent.reshape(1, -1),
        parent_owner.reshape(1, -1),
        parent_pages.reshape(1, -1),
        jnp.pad(page_table, ((0, 0), (0, 8 - page_table.shape[1]))),
    )


def fill_kernel(own_hot_ref, other_hot_ref, own_ref, other_ref, out_ref):
    def fill(i):
        at = chunk(i, CHUNK)
        filled = mm(own_hot_ref[at, :], own_ref[...]) + mm(other_hot_ref[at, :], other_ref[...])
        out_ref[at, :] = filled.astype(BF16)

    over(out_ref.shape[0] // CHUNK, fill)


def fill_slots(own_hot, other_hot, own, other):
    vmem = pl.BlockSpec(memory_space=pltpu.VMEM)
    return pl.pallas_call(
        fill_kernel,
        out_shape=jax.ShapeDtypeStruct((own_hot.shape[0], own.shape[1]), BF16),
        in_specs=[vmem] * 4,
        out_specs=vmem,
        compiler_params=pltpu.CompilerParams(vmem_limit_bytes=24 * 2**20),
    )(own_hot, other_hot, own, other)


def place_rows(hot_ref, rows_ref, acc_ref):
    if rows_ref.shape[0] == CHUNK:
        return mm(hot_ref[...], rows_ref[...])
    acc_ref[...] = jnp.zeros_like(acc_ref)

    @pl.loop(0, rows_ref.shape[0] // CHUNK)
    def _(i):
        at = chunk(i, CHUNK)
        acc_ref[...] += mm(hot_ref[:, at], rows_ref[at, :])

    return acc_ref[...]


def place_kernel(hot_ref, rows_ref, out_ref, acc_ref):
    out_ref[...] = place_rows(hot_ref, rows_ref, acc_ref).astype(BF16)


def place_slots(hot, rows):
    vmem = pl.BlockSpec(memory_space=pltpu.VMEM)
    return pl.pallas_call(
        place_kernel,
        out_shape=jax.ShapeDtypeStruct((hot.shape[0], rows.shape[1]), BF16),
        in_specs=[vmem, vmem],
        out_specs=vmem,
        scratch_shapes=[pltpu.VMEM((hot.shape[0], rows.shape[1]), F32)],
        compiler_params=pltpu.CompilerParams(vmem_limit_bytes=24 * 2**20),
        cost_estimate=pl.CostEstimate(
            flops=2 * hot.shape[0] * hot.shape[1] * rows.shape[1],
            bytes_accessed=2 * rows.shape[0] * rows.shape[1],
            transcendentals=0,
        ),
    )(hot, rows)


def sum_kernel(rows_ref, sum_ref):
    x = rows_ref[...].astype(F32)
    total = jnp.sum(x * x, axis=1, keepdims=True)
    total = jnp.broadcast_to(total, (total.shape[0], 128)).T
    sum_ref[...] = jnp.broadcast_to(total[0:1], sum_ref.shape[:1] + total.shape[1:])[:, None, :]


def row_sums(rows, copies):
    vmem = pl.BlockSpec(memory_space=pltpu.VMEM)
    return pl.pallas_call(
        sum_kernel,
        out_shape=jax.ShapeDtypeStruct((copies, 1, rows.shape[0]), F32),
        in_specs=[vmem],
        out_specs=vmem,
        compiler_params=pltpu.CompilerParams(vmem_limit_bytes=24 * 2**20),
    )(rows)


def row_scale(sum_ref, width):
    total = jnp.sum(sum_ref[:, 0, :], axis=0, keepdims=True)
    scale = lax.rsqrt(total * (1.0 / width) + EPSILON)
    return jnp.broadcast_to(scale, (128, scale.shape[1])).T


def normed(x, scale, gain):
    return (x.astype(F32) * scale * gain.astype(F32)).astype(BF16)


def add_products(acc, x, wq, wkv):
    wide = wq.shape[1]
    acc[:, :wide] += mm(x, wq)
    acc[:, wide:] += mm(x, wkv)


def project_kernel(width, count, first, order_ref, sum_ref, *refs):
    blocks = refs[:count]
    gain_ref, wq_ref, wk_ref, wv_ref = refs[count : count + 4]
    before = None if first else refs[count + 4]
    acc_ref, x_ref, wq_held, wkv_held, x_sems, w_sems = refs[-6:]
    part = x_ref.shape[2]

    def copies(i, block):
        at = chunk(order_ref[i], part)
        return [
            pltpu.make_async_copy(block, x_ref.at[i], x_sems.at[i]),
            pltpu.make_async_copy(wq_ref.at[at], wq_held.at[i], w_sems.at[i, 0]),
            pltpu.make_async_copy(wk_ref.at[at], wkv_held.at[i, :, :HEAD], w_sems.at[i, 1]),
            pltpu.make_async_copy(wv_ref.at[at], wkv_held.at[i, :, HEAD:], w_sems.at[i, 2]),
        ]

    for i in range(count):
        for copy in copies(i, blocks[i]):
            copy.start()
    scale = row_scale(sum_ref, width)[:, 0:1]
    acc_ref[...] = jnp.zeros_like(acc_ref) if first else before[...]

    @pl.loop(0, count)
    def _(i):
        for copy in copies(i, blocks[0]):
            copy.wait()
        x = normed(x_ref[i], scale, gain_ref[order_ref[i]])
        add_products(acc_ref, x, wq_held[i], wkv_held[i])


def project(order, sums, blocks, gain, wq, wk, wv, before=None):
    rows, part = blocks[0].shape
    columns = wq.shape[1] + wk.shape[1] + wv.shape[1]
    count = len(blocks)
    smem = pl.BlockSpec(memory_space=pltpu.SMEM)
    vmem = pl.BlockSpec(memory_space=pltpu.VMEM)
    hbm = pl.BlockSpec(memory_space=pltpu.HBM)
    extra = [] if before is None else [before]
    return pl.pallas_call(
        functools.partial(project_kernel, wq.shape[0], count, before is None),
        out_shape=jax.ShapeDtypeStruct((rows, columns), F32),
        in_specs=[smem, vmem] + [hbm] * count + [vmem, hbm, hbm, hbm] + [vmem] * len(extra),
        out_specs=vmem,
        scratch_shapes=[
            pltpu.VMEM((count, rows, part), BF16),
            pltpu.VMEM((count, part, wq.shape[1]), BF16),
            pltpu.VMEM((count, part, 2 * HEAD), BF16),
            pltpu.SemaphoreType.DMA((count,)),
            pltpu.SemaphoreType.DMA((count, 3)),
        ],
        compiler_params=pltpu.CompilerParams(vmem_limit_bytes=28 * 2**20),
        cost_estimate=pl.CostEstimate(
            flops=2 * rows * part * count * columns * 2,
            bytes_accessed=2 * part * count * columns,
            transcendentals=0,
        ),
    )(order, sums, *blocks, gain, wq, wk, wv, *extra)


def attend_kernel(
    width,
    info_ref,
    sum_ref,
    low_ref,
    high_ref,
    gain_ref,
    wq_ref,
    wk_ref,
    wv_ref,
    before_ref,
    cos_ref,
    sin_ref,
    pool_ref,
    back_ref,
    out_ref,
    acc_ref,
    x_ref,
    wkv_ref,
    q_ref,
    k_ref,
    v_ref,
    o_ref,
):
    scale = row_scale(sum_ref, width)[:, 0:1]
    half = low_ref.shape[0]
    x_ref[:half] = normed(low_ref[...], scale[:half], gain_ref[...])
    x_ref[half:] = normed(high_ref[...], scale[half:], gain_ref[...])
    acc_ref[...] = before_ref[...]
    wkv_ref[:, :HEAD] = wk_ref[...]
    wkv_ref[:, HEAD:] = wv_ref[...]
    add_products(acc_ref, x_ref[...], wq_ref[...], wkv_ref[...])

    cos = cos_ref[...]
    sin = sin_ref[...]

    def turn(part):
        return (part * cos + pltpu.roll(part, HEAD // 2, 1) * sin).astype(BF16)

    heads = wq_ref.shape[1] // HEAD
    for h in range(heads):
        cut = slice(h * HEAD, (h + 1) * HEAD)
        q_ref[:, cut] = turn(acc_ref[:, cut])
    k_ref[...] = turn(acc_ref[:, heads * HEAD : (heads + 1) * HEAD])
    v_ref[...] = acc_ref[:, (heads + 1) * HEAD :].astype(BF16)

    family = FORK * STEPS
    scale = 1.0 / math.sqrt(HEAD)
    row_at = iota((heads * family, family), 0) % family
    key_at = iota((heads * family, family), 1)
    page_at = iota((heads * family, MOST_PAGES * PAGE), 1) // PAGE
    own_mask = (row_at // STEPS == key_at // STEPS) & (row_at >= key_at)

    @pl.loop(0, PARENTS_HERE, unroll=4)
    def _(j):
        at = pl.ds(pl.multiple_of(j * family, family), family)
        q = jnp.concatenate([q_ref[at, h * HEAD : (h + 1) * HEAD] for h in range(heads)], axis=0)
        own = jnp.where(own_mask, mm_nt(q, k_ref[at, :]) * scale, -jnp.inf)
        own_top = jnp.max(own, axis=1, keepdims=True)
        own_weight = jnp.exp(own - own_top)
        own_total = jnp.sum(own_weight, axis=1, keepdims=True)
        own_mix = mm(own_weight.astype(BF16), v_ref[at, :])
        length = info_ref[j, MOST_PAGES]
        ids = [info_ref[j, i] for i in range(MOST_PAGES)]
        keys = jnp.concatenate([pool_ref[i, 0] for i in ids], axis=0)
        values = jnp.concatenate([pool_ref[i, 1] for i in ids], axis=0)
        path = jnp.where(page_at < length, mm_nt(q, keys) * scale, -jnp.inf)
        path_top = jnp.max(path, axis=1, keepdims=True)
        weight = jnp.exp(path - path_top)
        path_total = jnp.sum(weight, axis=1, keepdims=True)
        path_mix = mm(weight.astype(BF16), values)
        top = jnp.maximum(path_top, own_top)
        path_factor = jnp.exp(path_top - top)
        own_factor = jnp.exp(own_top - top)
        both = path_mix * path_factor + own_mix * own_factor
        out = both / (path_total * path_factor + own_total * own_factor)
        out = out.astype(BF16)
        for h in range(heads):
            o_ref[at, h * HEAD : (h + 1) * HEAD] = out[h * family : (h + 1) * family]


    def fill(i):
        at = chunk(i, CHUNK)
        out_ref[at, :] = mm(back_ref[at, :], o_ref[...]).astype(BF16)

    over(out_ref.shape[0] // CHUNK, fill)


def attend(info, sums, low, high, gain, wq, wk, wv, before, cos, sin, pool, back):
    rows, columns = before.shape
    part = low.shape[1]
    wide = back.shape[0]
    vmem = pl.BlockSpec(memory_space=pltpu.VMEM)
    smem = pl.BlockSpec(memory_space=pltpu.SMEM)
    return pl.pallas_call(
        functools.partial(attend_kernel, 8 * part),
        out_shape=jax.ShapeDtypeStruct((wide, wq.shape[1]), BF16),
        in_specs=[smem] + [vmem] * 12,
        out_specs=vmem,
        scratch_shapes=[
            pltpu.VMEM((rows, columns), F32),
            pltpu.VMEM((rows, part), BF16),
            pltpu.VMEM((part, 2 * HEAD), BF16),
            pltpu.VMEM((rows, wq.shape[1]), BF16),
            pltpu.VMEM((rows, HEAD), BF16),
            pltpu.VMEM((rows, HEAD), BF16),
            pltpu.VMEM((rows, wq.shape[1]), BF16),
        ],
        compiler_params=pltpu.CompilerParams(vmem_limit_bytes=24 * 2**20),
        cost_estimate=pl.CostEstimate(
            flops=2 * rows * part * columns * 6, bytes_accessed=2 * part * columns, transcendentals=0
        ),
    )(info, sums, low, high, gain, wq, wk, wv, before, cos, sin, pool, back)


def moves(dy, dz):
    return [(t, ((t // 2 + dy) % 4) * 2 + (t + dz) % 2) for t in range(8)]


def after_leave(slots, groups, me, tables, arrays, send):
    (norm_gain, wq, wk, wv, kv_pool) = arrays
    wide, width = send.shape
    rows = PARENTS_HERE * FORK * STEPS
    team = lax.axis_size("tensor")
    t = lax.axis_index("tensor")
    came = lax.all_to_all(send.reshape(groups, wide // groups, width), "sample", 0, 0)
    from_hot, back_hot, own_hot, other_hot, info = arrive(slots, groups, me, *tables, rows)

    def place(dy, dz):
        return ((t // 2 + dy) % 4) * 2 + (t + dz) % 2

    def order(*keys):
        return jnp.stack([place(*key) for key in keys]).astype(jnp.int32)

    last = [lax.dynamic_slice_in_dim(w, place(2, 1) * width, width) for w in (wq, wk, wv)]
    gain = norm_gain.reshape(team, 1, -1)
    last_gain = lax.dynamic_slice_in_dim(norm_gain, place(2, 1) * width, width).reshape(1, -1)

    pages = info[:, MOST_PAGES]
    positions = (
        jnp.repeat(pages * PAGE, FORK * STEPS)
        + jnp.tile(jnp.arange(STEPS, dtype=jnp.int32), PARENTS_HERE * FORK)
    ).astype(F32)
    inverse = ROPE_THETA ** (-2.0 * jnp.arange(HEAD // 2, dtype=F32) / HEAD)
    angles = positions[:, None] * inverse[None, :]
    cos, sin = jnp.cos(angles), jnp.sin(angles)
    cos = jnp.concatenate([cos, cos], axis=1)
    sin = jnp.concatenate([-sin, sin], axis=1)
    came, from_hot, info, cos, sin, gain, last_gain, *last = lax.optimization_barrier(
        (came, from_hot, info, cos, sin, gain, last_gain, *last)
    )
    back_hot, own_hot, other_hot, from_hot = lax.optimization_barrier(
        (back_hot, own_hot, other_hot, from_hot)
    )
    mine = place_slots(from_hot, came.reshape(wide, width))

    def shift(block, dy, dz):
        return lax.ppermute(block, "tensor", moves(dy, dz))

    sums = lax.all_to_all(row_sums(mine, team), "tensor", 0, 0)
    b30, b10, b01 = shift(mine, 1, 0), shift(mine, -1, 0), shift(mine, 0, 1)
    (b30,) = lax.optimization_barrier((b30,))
    b20, b31 = shift(b30, 1, 0), shift(b30, 0, 1)
    second = (b20, shift(b01, -1, 0), b31)
    acc = project(
        order((0, 0), (3, 0), (1, 0), (0, 1)), sums, [mine, b30, b10, b01], gain, wq, wk, wv
    )
    b20, b11, b31, acc = lax.optimization_barrier((*second, acc))
    half = rows // 2
    low, high = shift(b31[:half], 1, 0), shift(b11[half:], -1, 0)
    acc = project(order((2, 0), (1, 1), (3, 1)), sums, [b20, b11, b31], gain, wq, wk, wv, acc)
    low, high, acc = lax.optimization_barrier((low, high, acc))
    back = attend(
        info, sums, low, high, last_gain, *last, acc, cos, sin, kv_pool, back_hot
    )
    home = lax.all_to_all(back.reshape(groups, -1, back.shape[1]), "sample", 0, 0)
    home = home.reshape(-1, back.shape[1])
    other = place_slots(other_hot, home)
    return place_slots(own_hot, home) + lax.ppermute(other, "sample", swap(groups))


def swap(groups):
    return [(i, i ^ 1) for i in range(groups)]


def local(
    branch_tokens,
    norm_gain,
    query_weight,
    key_weight,
    value_weight,
    kv_pool,
    parent_owner,
    parent_pages,
    page_table,
    child_parent,
):
    groups = lax.axis_size("sample")
    rows = branch_tokens.shape[0]
    me = lax.axis_index("sample").astype(jnp.int32).reshape(1)
    tables = (child_parent, parent_owner, parent_pages, page_table)
    arrays = (norm_gain, query_weight, key_weight, value_weight, kv_pool)
    other = lax.ppermute(branch_tokens, "sample", swap(groups))
    own_hot, other_hot, fits = leave(SLOTS, groups, me, *tables[:2], rows)
    other, own_hot, other_hot, fits = lax.optimization_barrier((other, own_hot, other_hot, fits))
    send = fill_slots(own_hot, other_hot, branch_tokens, other)

    def usual():
        return after_leave(SLOTS, groups, me, tables, arrays, send)

    def crowded():
        most = 4 * SLOTS
        own, others, _ = leave(most, groups, me, *tables[:2], rows)
        wider = fill_slots(own, others, branch_tokens, other)
        return after_leave(most, groups, me, tables, arrays, wider)

    return lax.switch(fits[0], [crowded, usual])


def solution(mesh):
    return jax.shard_map(
        local,
        mesh=mesh,
        in_specs=(
            P("sample", "tensor"),
            P(),
            P(None, "tensor"),
            P(None, "tensor"),
            P(None, "tensor"),
            P("sample", None, None, "tensor"),
            P(),
            P(),
            P(),
            P(),
        ),
        out_specs=P("sample", "tensor"),
        check_vma=False,
    )
```

```python
import functools
import math

import jax
import jax.numpy as jnp
from jax import lax
from jax.experimental import pallas as pl
from jax.experimental.pallas import tpu as pltpu
from jax.sharding import PartitionSpec as P

HEAD = 128
PAGE = 128
STEPS = 4
FORK = 8
PARENTS_HERE = 8
MOST_PAGES = 5
ROPE_THETA = 10000.0
EPSILON = 1e-06
SLOTS = 10
CHUNK = 640

BF16 = jnp.bfloat16
F32 = jnp.float32


def iota(shape, dim):
    return lax.broadcasted_iota(jnp.int32, shape, dim)


def one(mask):
    return jnp.where(mask, 1.0, 0.0).astype(BF16)


def mm(a, b):
    return lax.dot_general(a, b, (((1,), (0,)), ((), ())), preferred_element_type=F32)


def over(count, body):
    if count == 1:
        body(0)
    else:
        pl.loop(0, count)(body)


def chunk(i, size):
    return pl.ds(pl.multiple_of(i * size, size), size)


def mm_nt(a, b):
    return lax.dot_general(a, b, (((1,), (1,)), ((), ())), preferred_element_type=F32)


def owners(child_ref, owner_ref, mask_ref):
    groups, children = mask_ref.shape
    parents = owner_ref.shape[1]
    parent_hot = one(iota((parents, children), 0) == child_ref[...])
    owner = jnp.broadcast_to(owner_ref[...].astype(F32), (16, parents)).astype(BF16)
    owner_of = mm(owner, parent_hot)[0:1].astype(jnp.int32)
    mask_ref[...] = jnp.where(iota((groups, children), 0) == owner_of, 1.0, 0.0)


def targets(slots, me, mask_ref, rows):
    here = rows // STEPS
    core = lax.rem(me, 2)
    chip = lax.div(me, 2)
    mask = mask_ref[:, pl.ds(pl.multiple_of(chip * 2 * here, 2 * here), 2 * here)]
    ahead = mm(mask.astype(BF16), one(iota((128, 128), 0) < iota((128, 128), 1)))
    rank = jnp.sum(mask * ahead, axis=0, keepdims=True).astype(jnp.int32)
    owner = jnp.sum(mask * iota(mask.shape, 0).astype(F32), axis=0, keepdims=True)
    keep = jnp.where(rank % 2 == core, 1.0, 0.0)
    turn = (rank // 2).astype(F32)
    at = iota((16, 2 * here), 0)
    facts = jnp.where(at == 0, owner, jnp.where(at == 1, turn, keep)).astype(BF16)
    found = []
    for side in (core, 1 - core):
        grow = one(iota((2 * here, rows), 0) == side * here + iota((2 * here, rows), 1) // STEPS)
        of_row = mm(facts, grow)
        target = of_row[0:1] * (slots * STEPS) + of_row[1:2] * STEPS
        target = target.astype(jnp.int32) + iota((1, rows), 1) % STEPS
        found.append(jnp.where(of_row[2:3] > 0.5, target, -1))
    return found


def leave_kernel(slots, me_ref, child_ref, owner_ref, own_ref, other_ref, fits_ref, mask_ref):
    me = me_ref[0]
    rows = own_ref.shape[1]
    here = rows // STEPS
    children = child_ref.shape[1]
    owners(child_ref, owner_ref, mask_ref)
    counted = iota((children, 128), 1) == iota((children, 128), 0) // (2 * here)
    most = jnp.max(mm(mask_ref[...].astype(BF16), one(counted))).astype(jnp.int32)
    fits_ref[0] = jnp.where(most <= 2 * slots, 1, 0)

    for ref, target in zip((own_ref, other_ref), targets(slots, me, mask_ref, rows)):

        def fill(i, ref=ref, target=target):
            ref[chunk(i, CHUNK), :] = one(iota((CHUNK, rows), 0) + i * CHUNK == target)

        over(ref.shape[0] // CHUNK, fill)


def leave(slots, groups, me, child_parent, parent_owner, rows):
    vmem = pl.BlockSpec(memory_space=pltpu.VMEM)
    smem = pl.BlockSpec(memory_space=pltpu.SMEM)
    hot = jax.ShapeDtypeStruct((groups * slots * STEPS, rows), BF16)
    return pl.pallas_call(
        functools.partial(leave_kernel, slots),
        out_shape=(hot, hot, jax.ShapeDtypeStruct((1,), jnp.int32)),
        in_specs=[smem, vmem, vmem],
        out_specs=(vmem, vmem, smem),
        scratch_shapes=[pltpu.VMEM((groups, child_parent.shape[0]), F32)],
        compiler_params=pltpu.CompilerParams(vmem_limit_bytes=24 * 2**20),
        cost_estimate=pl.CostEstimate(flops=10**9, bytes_accessed=2**20, transcendentals=0),
    )(me, child_parent.reshape(1, -1), parent_owner.reshape(1, -1))


def arrive_kernel(
    slots,
    me_ref,
    child_ref,
    owner_ref,
    pages_ref,
    table_ref,
    from_ref,
    back_ref,
    own_ref,
    other_ref,
    info_ref,
    mask_ref,
):
    me = me_ref[0]
    children = child_ref.shape[1]
    parents = owner_ref.shape[1]
    rows, wide = from_ref.shape
    here = rows // STEPS
    owner = owner_ref[...]
    parent_hot = one(iota((parents, children), 0) == child_ref[...])
    mine_parent = owner == me
    tri = one(iota((128, 128), 0) < iota((128, 128), 1))
    parent_rank = mm(one(jnp.broadcast_to(mine_parent, (16, parents))), tri)
    parent_rank = parent_rank[0:1].astype(jnp.int32)
    mine_hot = (iota((PARENTS_HERE, parents), 0) == parent_rank) & mine_parent
    pages = jnp.sum(jnp.where(mine_hot, pages_ref[...], 0), axis=1, keepdims=True)
    mine_hot = one(mine_hot)
    table = mm(mine_hot, table_ref[...].astype(F32).astype(BF16)).astype(jnp.int32)
    info_ref[...] = jnp.where(iota((PARENTS_HERE, 8), 1) == MOST_PAGES, pages, table)
    member = mm(mine_hot, parent_hot)
    carry = jnp.zeros((PARENTS_HERE, 1), F32)
    places, spots = [], []
    for block in range(children // 128):
        part = member[:, block * 128 : (block + 1) * 128]
        ahead = mm(part.astype(BF16), tri) + carry
        carry = carry + jnp.sum(part, axis=1, keepdims=True)
        is_mine = jnp.sum(part, axis=0, keepdims=True)
        place = jnp.sum(
            part * (iota((PARENTS_HERE, 128), 0).astype(F32) * FORK + ahead), axis=0, keepdims=True
        ).astype(jnp.int32)
        in_chip = mm(jnp.broadcast_to(is_mine, (16, 128)).astype(BF16), tri)[0:1].astype(jnp.int32)
        chip = (block * 128 + iota((1, 128), 1)) // (2 * here)
        spot = (chip * 2 + in_chip % 2) * slots + in_chip // 2
        places.append(jnp.where(is_mine > 0.5, place, -1))
        spots.append(jnp.where(is_mine > 0.5, spot, -1))
    place_hot = one(iota((here, children), 0) == jnp.concatenate(places, axis=1))
    spot = jnp.concatenate(spots, axis=1)
    grow_rows = one(iota((rows, here), 0) // STEPS == iota((rows, here), 1))
    size, deep = CHUNK, CHUNK // STEPS
    grow_columns = one(iota((deep, size), 0) == iota((deep, size), 1) // STEPS)
    same_step = iota((rows, size), 0) % STEPS == iota((rows, size), 1) % STEPS

    def fill(i):
        spot_hot = one(iota((deep, children), 0) + i * deep == spot)
        by_child = mm_nt(place_hot, spot_hot).astype(BF16)
        by_row = mm(mm(grow_rows, by_child).astype(BF16), grow_columns)
        by_row = jnp.where(same_step, by_row, 0.0)
        from_ref[:, chunk(i, size)] = by_row.astype(BF16)
        back_ref[chunk(i, size), :] = by_row.T.astype(BF16)

    over(wide // CHUNK, fill)

    owners(child_ref, owner_ref, mask_ref)
    for ref, target in zip((own_ref, other_ref), targets(slots, me, mask_ref, rows)):
        column = jnp.broadcast_to(target.astype(F32), (128, rows)).T[:, 0:1].astype(jnp.int32)

        def put(i, ref=ref, column=column):
            ref[:, chunk(i, size)] = one(iota((rows, size), 1) + i * size == column)

        over(wide // CHUNK, put)


def arrive(slots, groups, me, child_parent, parent_owner, parent_pages, page_table, rows):
    hot = jax.ShapeDtypeStruct((rows, groups * slots * STEPS), BF16)
    vmem = pl.BlockSpec(memory_space=pltpu.VMEM)
    smem = pl.BlockSpec(memory_space=pltpu.SMEM)
    return pl.pallas_call(
        functools.partial(arrive_kernel, slots),
        out_shape=(
            hot,
            jax.ShapeDtypeStruct(hot.shape[::-1], BF16),
            hot,
            hot,
            jax.ShapeDtypeStruct((PARENTS_HERE, 8), jnp.int32),
        ),
        in_specs=[smem] + [vmem] * 4,
        out_specs=(vmem,) * 5,
        scratch_shapes=[pltpu.VMEM((groups, child_parent.shape[0]), F32)],
        compiler_params=pltpu.CompilerParams(vmem_limit_bytes=24 * 2**20),
        cost_estimate=pl.CostEstimate(flops=2 * 10**9, bytes_accessed=2**20, transcendentals=0),
    )(
        me,
        child_parent.reshape(1, -1),
        parent_owner.reshape(1, -1),
        parent_pages.reshape(1, -1),
        jnp.pad(page_table, ((0, 0), (0, 8 - page_table.shape[1]))),
    )


def fill_kernel(own_hot_ref, other_hot_ref, own_ref, other_ref, out_ref):
    def fill(i):
        at = chunk(i, CHUNK)
        filled = mm(own_hot_ref[at, :], own_ref[...]) + mm(other_hot_ref[at, :], other_ref[...])
        out_ref[at, :] = filled.astype(BF16)

    over(out_ref.shape[0] // CHUNK, fill)


def fill_slots(own_hot, other_hot, own, other):
    vmem = pl.BlockSpec(memory_space=pltpu.VMEM)
    return pl.pallas_call(
        fill_kernel,
        out_shape=jax.ShapeDtypeStruct((own_hot.shape[0], own.shape[1]), BF16),
        in_specs=[vmem] * 4,
        out_specs=vmem,
        compiler_params=pltpu.CompilerParams(vmem_limit_bytes=24 * 2**20),
    )(own_hot, other_hot, own, other)


def place_rows(hot_ref, rows_ref, acc_ref):
    if rows_ref.shape[0] == CHUNK:
        return mm(hot_ref[...], rows_ref[...])
    acc_ref[...] = jnp.zeros_like(acc_ref)

    @pl.loop(0, rows_ref.shape[0] // CHUNK)
    def _(i):
        at = chunk(i, CHUNK)
        acc_ref[...] += mm(hot_ref[:, at], rows_ref[at, :])

    return acc_ref[...]


def place_kernel(hot_ref, rows_ref, out_ref, acc_ref):
    out_ref[...] = place_rows(hot_ref, rows_ref, acc_ref).astype(BF16)


def place_slots(hot, rows):
    vmem = pl.BlockSpec(memory_space=pltpu.VMEM)
    return pl.pallas_call(
        place_kernel,
        out_shape=jax.ShapeDtypeStruct((hot.shape[0], rows.shape[1]), BF16),
        in_specs=[vmem, vmem],
        out_specs=vmem,
        scratch_shapes=[pltpu.VMEM((hot.shape[0], rows.shape[1]), F32)],
        compiler_params=pltpu.CompilerParams(vmem_limit_bytes=24 * 2**20),
        cost_estimate=pl.CostEstimate(
            flops=2 * hot.shape[0] * hot.shape[1] * rows.shape[1],
            bytes_accessed=2 * rows.shape[0] * rows.shape[1],
            transcendentals=0,
        ),
    )(hot, rows)


def sum_kernel(rows_ref, sum_ref):
    x = rows_ref[...].astype(F32)
    total = jnp.sum(x * x, axis=1, keepdims=True)
    total = jnp.broadcast_to(total, (total.shape[0], 128)).T
    sum_ref[...] = jnp.broadcast_to(total[0:1], sum_ref.shape[:1] + total.shape[1:])[:, None, :]


def row_sums(rows, copies):
    vmem = pl.BlockSpec(memory_space=pltpu.VMEM)
    return pl.pallas_call(
        sum_kernel,
        out_shape=jax.ShapeDtypeStruct((copies, 1, rows.shape[0]), F32),
        in_specs=[vmem],
        out_specs=vmem,
        compiler_params=pltpu.CompilerParams(vmem_limit_bytes=24 * 2**20),
    )(rows)


def row_scale(sum_ref, width):
    total = jnp.sum(sum_ref[:, 0, :], axis=0, keepdims=True)
    scale = lax.rsqrt(total * (1.0 / width) + EPSILON)
    return jnp.broadcast_to(scale, (128, scale.shape[1])).T


def normed(x, scale, gain):
    return (x.astype(F32) * scale * gain.astype(F32)).astype(BF16)


def add_products(acc, x, wq, wkv):
    wide = wq.shape[1]
    acc[:, :wide] += mm(x, wq)
    acc[:, wide:] += mm(x, wkv)


def project_kernel(width, places, first, order_ref, sum_ref, *refs):
    count = len(places)
    pieces = sum(len(place) for place in places)
    blocks = refs[:pieces]
    gain_ref, wq_ref, wk_ref, wv_ref = refs[pieces : pieces + 4]
    before = None if first else refs[pieces + 4]
    acc_ref, x_ref, wq_held, wkv_held, x_sems, w_sems = refs[-6:]
    part = x_ref.shape[2]

    def copies(i):
        at = chunk(order_ref[i], part)
        return [
            pltpu.make_async_copy(wq_ref.at[at], wq_held.at[i], w_sems.at[i, 0]),
            pltpu.make_async_copy(wk_ref.at[at], wkv_held.at[i, :, :HEAD], w_sems.at[i, 1]),
            pltpu.make_async_copy(wv_ref.at[at], wkv_held.at[i, :, HEAD:], w_sems.at[i, 2]),
        ]

    for i, place in enumerate(places):
        for block, first_row in place:
            cut = pl.ds(first_row, blocks[block].shape[0])
            pltpu.make_async_copy(blocks[block], x_ref.at[i, cut], x_sems.at[i]).start()
        for copy in copies(i):
            copy.start()
    scale = row_scale(sum_ref, width)[:, 0:1]
    acc_ref[...] = jnp.zeros_like(acc_ref) if first else before[...]

    @pl.loop(0, count)
    def _(i):
        pltpu.make_async_copy(x_ref.at[i], x_ref.at[i], x_sems.at[i]).wait()
        for copy in copies(i):
            copy.wait()
        x = normed(x_ref[i], scale, gain_ref[order_ref[i]])
        add_products(acc_ref, x, wq_held[i], wkv_held[i])


def project(order, sums, blocks, gain, wq, wk, wv, before=None):
    part = blocks[0][0].shape[1]
    rows = sum(piece.shape[0] for piece in blocks[0])
    columns = wq.shape[1] + wk.shape[1] + wv.shape[1]
    count = len(blocks)
    pieces = [piece for block in blocks for piece in block]
    places, number = [], 0
    for block in blocks:
        starts = [sum(piece.shape[0] for piece in block[:i]) for i in range(len(block))]
        places.append([(number + i, start) for i, start in enumerate(starts)])
        number += len(block)
    smem = pl.BlockSpec(memory_space=pltpu.SMEM)
    vmem = pl.BlockSpec(memory_space=pltpu.VMEM)
    hbm = pl.BlockSpec(memory_space=pltpu.HBM)
    extra = [] if before is None else [before]
    return pl.pallas_call(
        functools.partial(project_kernel, wq.shape[0], places, before is None),
        out_shape=jax.ShapeDtypeStruct((rows, columns), F32),
        in_specs=[smem, vmem] + [hbm] * number + [vmem, hbm, hbm, hbm] + [vmem] * len(extra),
        out_specs=vmem,
        scratch_shapes=[
            pltpu.VMEM((count, rows, part), BF16),
            pltpu.VMEM((count, part, wq.shape[1]), BF16),
            pltpu.VMEM((count, part, 2 * HEAD), BF16),
            pltpu.SemaphoreType.DMA((count,)),
            pltpu.SemaphoreType.DMA((count, 3)),
        ],
        compiler_params=pltpu.CompilerParams(vmem_limit_bytes=28 * 2**20),
        cost_estimate=pl.CostEstimate(
            flops=2 * rows * part * count * columns * 2,
            bytes_accessed=2 * part * count * columns,
            transcendentals=0,
        ),
    )(order, sums, *pieces, gain, wq, wk, wv, *extra)


def attend_kernel(
    width,
    info_ref,
    sum_ref,
    low_ref,
    high_ref,
    gain_ref,
    wq_ref,
    wk_ref,
    wv_ref,
    before_ref,
    cos_ref,
    sin_ref,
    pool_ref,
    back_ref,
    out_ref,
    acc_ref,
    x_ref,
    wkv_ref,
    q_ref,
    k_ref,
    v_ref,
    o_ref,
):
    scale = row_scale(sum_ref, width)[:, 0:1]
    half = low_ref.shape[0]
    x_ref[:half] = normed(low_ref[...], scale[:half], gain_ref[...])
    x_ref[half:] = normed(high_ref[...], scale[half:], gain_ref[...])
    acc_ref[...] = before_ref[...]
    wkv_ref[:, :HEAD] = wk_ref[...]
    wkv_ref[:, HEAD:] = wv_ref[...]
    add_products(acc_ref, x_ref[...], wq_ref[...], wkv_ref[...])

    cos = cos_ref[...]
    sin = sin_ref[...]

    def turn(part):
        return (part * cos + pltpu.roll(part, HEAD // 2, 1) * sin).astype(BF16)

    heads = wq_ref.shape[1] // HEAD
    for h in range(heads):
        cut = slice(h * HEAD, (h + 1) * HEAD)
        q_ref[:, cut] = turn(acc_ref[:, cut])
    k_ref[...] = turn(acc_ref[:, heads * HEAD : (heads + 1) * HEAD])
    v_ref[...] = acc_ref[:, (heads + 1) * HEAD :].astype(BF16)

    family = FORK * STEPS
    scale = 1.0 / math.sqrt(HEAD)
    row_at = iota((heads * family, family), 0) % family
    key_at = iota((heads * family, family), 1)
    page_at = iota((heads * family, MOST_PAGES * PAGE), 1) // PAGE
    own_mask = (row_at // STEPS == key_at // STEPS) & (row_at >= key_at)

    @pl.loop(0, PARENTS_HERE, unroll=4)
    def _(j):
        at = pl.ds(pl.multiple_of(j * family, family), family)
        q = jnp.concatenate([q_ref[at, h * HEAD : (h + 1) * HEAD] for h in range(heads)], axis=0)
        own = jnp.where(own_mask, mm_nt(q, k_ref[at, :]) * scale, -jnp.inf)
        own_top = jnp.max(own, axis=1, keepdims=True)
        own_weight = jnp.exp(own - own_top)
        own_total = jnp.sum(own_weight, axis=1, keepdims=True)
        own_mix = mm(own_weight.astype(BF16), v_ref[at, :])
        length = info_ref[j, MOST_PAGES]
        ids = [info_ref[j, i] for i in range(MOST_PAGES)]
        keys = jnp.concatenate([pool_ref[i, 0] for i in ids], axis=0)
        values = jnp.concatenate([pool_ref[i, 1] for i in ids], axis=0)
        path = jnp.where(page_at < length, mm_nt(q, keys) * scale, -jnp.inf)
        path_top = jnp.max(path, axis=1, keepdims=True)
        weight = jnp.exp(path - path_top)
        path_total = jnp.sum(weight, axis=1, keepdims=True)
        path_mix = mm(weight.astype(BF16), values)
        top = jnp.maximum(path_top, own_top)
        path_factor = jnp.exp(path_top - top)
        own_factor = jnp.exp(own_top - top)
        both = path_mix * path_factor + own_mix * own_factor
        out = both / (path_total * path_factor + own_total * own_factor)
        out = out.astype(BF16)
        for h in range(heads):
            o_ref[at, h * HEAD : (h + 1) * HEAD] = out[h * family : (h + 1) * family]


    def fill(i):
        at = chunk(i, CHUNK)
        out_ref[at, :] = mm(back_ref[at, :], o_ref[...]).astype(BF16)

    over(out_ref.shape[0] // CHUNK, fill)


def attend(info, sums, low, high, gain, wq, wk, wv, before, cos, sin, pool, back):
    rows, columns = before.shape
    part = low.shape[1]
    wide = back.shape[0]
    vmem = pl.BlockSpec(memory_space=pltpu.VMEM)
    smem = pl.BlockSpec(memory_space=pltpu.SMEM)
    return pl.pallas_call(
        functools.partial(attend_kernel, 8 * part),
        out_shape=jax.ShapeDtypeStruct((wide, wq.shape[1]), BF16),
        in_specs=[smem] + [vmem] * 12,
        out_specs=vmem,
        scratch_shapes=[
            pltpu.VMEM((rows, columns), F32),
            pltpu.VMEM((rows, part), BF16),
            pltpu.VMEM((part, 2 * HEAD), BF16),
            pltpu.VMEM((rows, wq.shape[1]), BF16),
            pltpu.VMEM((rows, HEAD), BF16),
            pltpu.VMEM((rows, HEAD), BF16),
            pltpu.VMEM((rows, wq.shape[1]), BF16),
        ],
        compiler_params=pltpu.CompilerParams(vmem_limit_bytes=24 * 2**20),
        cost_estimate=pl.CostEstimate(
            flops=2 * rows * part * columns * 6, bytes_accessed=2 * part * columns, transcendentals=0
        ),
    )(info, sums, low, high, gain, wq, wk, wv, before, cos, sin, pool, back)


def moves(dy, dz):
    return [(t, ((t // 2 + dy) % 4) * 2 + (t + dz) % 2) for t in range(8)]


def after_leave(slots, groups, me, tables, arrays, send):
    (norm_gain, wq, wk, wv, kv_pool) = arrays
    wide, width = send.shape
    rows = PARENTS_HERE * FORK * STEPS
    team = lax.axis_size("tensor")
    t = lax.axis_index("tensor")
    came = lax.all_to_all(send.reshape(groups, wide // groups, width), "sample", 0, 0)
    from_hot, back_hot, own_hot, other_hot, info = arrive(slots, groups, me, *tables, rows)

    def place(dy, dz):
        return ((t // 2 + dy) % 4) * 2 + (t + dz) % 2

    def order(*keys):
        return jnp.stack([place(*key) for key in keys]).astype(jnp.int32)

    last = [lax.dynamic_slice_in_dim(w, place(2, 1) * width, width) for w in (wq, wk, wv)]
    gain = norm_gain.reshape(team, 1, -1)
    last_gain = lax.dynamic_slice_in_dim(norm_gain, place(2, 1) * width, width).reshape(1, -1)

    pages = info[:, MOST_PAGES]
    positions = (
        jnp.repeat(pages * PAGE, FORK * STEPS)
        + jnp.tile(jnp.arange(STEPS, dtype=jnp.int32), PARENTS_HERE * FORK)
    ).astype(F32)
    inverse = ROPE_THETA ** (-2.0 * jnp.arange(HEAD // 2, dtype=F32) / HEAD)
    angles = positions[:, None] * inverse[None, :]
    cos, sin = jnp.cos(angles), jnp.sin(angles)
    cos = jnp.concatenate([cos, cos], axis=1)
    sin = jnp.concatenate([-sin, sin], axis=1)
    came, from_hot, info, cos, sin, gain, last_gain, *last = lax.optimization_barrier(
        (came, from_hot, info, cos, sin, gain, last_gain, *last)
    )
    back_hot, own_hot, other_hot, from_hot = lax.optimization_barrier(
        (back_hot, own_hot, other_hot, from_hot)
    )
    mine = place_slots(from_hot, came.reshape(wide, width))

    def shift(block, dy, dz):
        return lax.ppermute(block, "tensor", moves(dy, dz))

    sums = lax.all_to_all(row_sums(mine, team), "tensor", 0, 0)
    b30, b10, b01 = shift(mine, 1, 0), shift(mine, -1, 0), shift(mine, 0, 1)
    half = rows // 2
    (b30,) = lax.optimization_barrier((b30,))
    b20, b31_low = shift(b30, 1, 0), shift(b30[:half], 0, 1)
    b01, b10, sums = lax.optimization_barrier((b01, b10, sums))
    b11_high = shift(b01[half:], -1, 0)
    b31_high, b11_low = shift(b30[half:], 0, 1), shift(b01[:half], -1, 0)
    b31_low, b11_high = lax.optimization_barrier((b31_low, b11_high))
    low, high = shift(b31_low, 1, 0), shift(b11_high, -1, 0)
    acc = project(
        order((0, 0), (3, 0), (1, 0), (0, 1)), sums, [[mine], [b30], [b10], [b01]], gain, wq, wk, wv
    )
    b20, b11_low, b31_high, acc = lax.optimization_barrier((b20, b11_low, b31_high, acc))
    acc = project(
        order((2, 0), (1, 1), (3, 1)),
        sums,
        [[b20], [b11_low, b11_high], [b31_low, b31_high]],
        gain,
        wq,
        wk,
        wv,
        acc,
    )
    low, high, acc = lax.optimization_barrier((low, high, acc))
    back = attend(
        info, sums, low, high, last_gain, *last, acc, cos, sin, kv_pool, back_hot
    )
    home = lax.all_to_all(back.reshape(groups, -1, back.shape[1]), "sample", 0, 0)
    home = home.reshape(-1, back.shape[1])
    other = place_slots(other_hot, home)
    return place_slots(own_hot, home) + lax.ppermute(other, "sample", swap(groups))


def swap(groups):
    return [(i, i ^ 1) for i in range(groups)]


def local(
    branch_tokens,
    norm_gain,
    query_weight,
    key_weight,
    value_weight,
    kv_pool,
    parent_owner,
    parent_pages,
    page_table,
    child_parent,
):
    groups = lax.axis_size("sample")
    rows = branch_tokens.shape[0]
    me = lax.axis_index("sample").astype(jnp.int32).reshape(1)
    tables = (child_parent, parent_owner, parent_pages, page_table)
    arrays = (norm_gain, query_weight, key_weight, value_weight, kv_pool)
    other = lax.ppermute(branch_tokens, "sample", swap(groups))
    own_hot, other_hot, fits = leave(SLOTS, groups, me, *tables[:2], rows)
    other, own_hot, other_hot, fits = lax.optimization_barrier((other, own_hot, other_hot, fits))
    send = fill_slots(own_hot, other_hot, branch_tokens, other)

    def usual():
        return after_leave(SLOTS, groups, me, tables, arrays, send)

    def crowded():
        most = 4 * SLOTS
        own, others, _ = leave(most, groups, me, *tables[:2], rows)
        wider = fill_slots(own, others, branch_tokens, other)
        return after_leave(most, groups, me, tables, arrays, wider)

    return lax.switch(fits[0], [crowded, usual])


def solution(mesh):
    return jax.shard_map(
        local,
        mesh=mesh,
        in_specs=(
            P("sample", "tensor"),
            P(),
            P(None, "tensor"),
            P(None, "tensor"),
            P(None, "tensor"),
            P("sample", None, None, "tensor"),
            P(),
            P(),
            P(),
            P(),
        ),
        out_specs=P("sample", "tensor"),
        check_vma=False,
    )
```

```python
import functools
import math

import jax
import jax.numpy as jnp
from jax import lax
from jax.experimental import pallas as pl
from jax.experimental.pallas import tpu as pltpu
from jax.sharding import PartitionSpec as P

HEAD = 128
PAGE = 128
STEPS = 4
FORK = 8
PARENTS_HERE = 8
MOST_PAGES = 5
ROPE_THETA = 10000.0
EPSILON = 1e-06
SLOTS = 10
CHUNK = 640

BF16 = jnp.bfloat16
F32 = jnp.float32


def iota(shape, dim):
    return lax.broadcasted_iota(jnp.int32, shape, dim)


def one(mask):
    return jnp.where(mask, 1.0, 0.0).astype(BF16)


def mm(a, b):
    return lax.dot_general(a, b, (((1,), (0,)), ((), ())), preferred_element_type=F32)


def over(count, body):
    if count == 1:
        body(0)
    else:
        pl.loop(0, count)(body)


def chunk(i, size):
    return pl.ds(pl.multiple_of(i * size, size), size)


def mm_nt(a, b):
    return lax.dot_general(a, b, (((1,), (1,)), ((), ())), preferred_element_type=F32)


def owners(child_ref, owner_ref, mask_ref):
    groups, children = mask_ref.shape
    parents = owner_ref.shape[1]
    parent_hot = one(iota((parents, children), 0) == child_ref[...])
    owner = jnp.broadcast_to(owner_ref[...].astype(F32), (16, parents)).astype(BF16)
    owner_of = mm(owner, parent_hot)[0:1].astype(jnp.int32)
    mask_ref[...] = jnp.where(iota((groups, children), 0) == owner_of, 1.0, 0.0)


def targets(slots, me, mask_ref, rows):
    here = rows // STEPS
    core = lax.rem(me, 2)
    chip = lax.div(me, 2)
    mask = mask_ref[:, pl.ds(pl.multiple_of(chip * 2 * here, 2 * here), 2 * here)]
    ahead = mm(mask.astype(BF16), one(iota((128, 128), 0) < iota((128, 128), 1)))
    rank = jnp.sum(mask * ahead, axis=0, keepdims=True).astype(jnp.int32)
    owner = jnp.sum(mask * iota(mask.shape, 0).astype(F32), axis=0, keepdims=True)
    keep = jnp.where(rank % 2 == core, 1.0, 0.0)
    turn = (rank // 2).astype(F32)
    at = iota((16, 2 * here), 0)
    facts = jnp.where(at == 0, owner, jnp.where(at == 1, turn, keep)).astype(BF16)
    found = []
    for side in (core, 1 - core):
        grow = one(iota((2 * here, rows), 0) == side * here + iota((2 * here, rows), 1) // STEPS)
        of_row = mm(facts, grow)
        target = of_row[0:1] * (slots * STEPS) + of_row[1:2] * STEPS
        target = target.astype(jnp.int32) + iota((1, rows), 1) % STEPS
        found.append(jnp.where(of_row[2:3] > 0.5, target, -1))
    return found


def leave_kernel(slots, me_ref, child_ref, owner_ref, own_ref, other_ref, fits_ref, mask_ref):
    me = me_ref[0]
    rows = own_ref.shape[1]
    here = rows // STEPS
    children = child_ref.shape[1]
    owners(child_ref, owner_ref, mask_ref)
    counted = iota((children, 128), 1) == iota((children, 128), 0) // (2 * here)
    most = jnp.max(mm(mask_ref[...].astype(BF16), one(counted))).astype(jnp.int32)
    fits_ref[0] = jnp.where(most <= 2 * slots, 1, 0)

    for ref, target in zip((own_ref, other_ref), targets(slots, me, mask_ref, rows)):

        def fill(i, ref=ref, target=target):
            ref[chunk(i, CHUNK), :] = one(iota((CHUNK, rows), 0) + i * CHUNK == target)

        over(ref.shape[0] // CHUNK, fill)


def leave(slots, groups, me, child_parent, parent_owner, rows):
    vmem = pl.BlockSpec(memory_space=pltpu.VMEM)
    smem = pl.BlockSpec(memory_space=pltpu.SMEM)
    hot = jax.ShapeDtypeStruct((groups * slots * STEPS, rows), BF16)
    return pl.pallas_call(
        functools.partial(leave_kernel, slots),
        out_shape=(hot, hot, jax.ShapeDtypeStruct((1,), jnp.int32)),
        in_specs=[smem, vmem, vmem],
        out_specs=(vmem, vmem, smem),
        scratch_shapes=[pltpu.VMEM((groups, child_parent.shape[0]), F32)],
        compiler_params=pltpu.CompilerParams(vmem_limit_bytes=24 * 2**20),
        cost_estimate=pl.CostEstimate(flops=10**9, bytes_accessed=2**20, transcendentals=0),
    )(me, child_parent.reshape(1, -1), parent_owner.reshape(1, -1))


def arrive_kernel(
    slots,
    me_ref,
    child_ref,
    owner_ref,
    pages_ref,
    table_ref,
    from_ref,
    back_ref,
    own_ref,
    other_ref,
    info_ref,
    mask_ref,
):
    me = me_ref[0]
    children = child_ref.shape[1]
    parents = owner_ref.shape[1]
    rows, wide = from_ref.shape
    here = rows // STEPS
    owner = owner_ref[...]
    parent_hot = one(iota((parents, children), 0) == child_ref[...])
    mine_parent = owner == me
    tri = one(iota((128, 128), 0) < iota((128, 128), 1))
    parent_rank = mm(one(jnp.broadcast_to(mine_parent, (16, parents))), tri)
    parent_rank = parent_rank[0:1].astype(jnp.int32)
    mine_hot = (iota((PARENTS_HERE, parents), 0) == parent_rank) & mine_parent
    pages = jnp.sum(jnp.where(mine_hot, pages_ref[...], 0), axis=1, keepdims=True)
    mine_hot = one(mine_hot)
    table = mm(mine_hot, table_ref[...].astype(F32).astype(BF16)).astype(jnp.int32)
    info_ref[...] = jnp.where(iota((PARENTS_HERE, 8), 1) == MOST_PAGES, pages, table)
    member = mm(mine_hot, parent_hot)
    carry = jnp.zeros((PARENTS_HERE, 1), F32)
    places, spots = [], []
    for block in range(children // 128):
        part = member[:, block * 128 : (block + 1) * 128]
        ahead = mm(part.astype(BF16), tri) + carry
        carry = carry + jnp.sum(part, axis=1, keepdims=True)
        is_mine = jnp.sum(part, axis=0, keepdims=True)
        place = jnp.sum(
            part * (iota((PARENTS_HERE, 128), 0).astype(F32) * FORK + ahead), axis=0, keepdims=True
        ).astype(jnp.int32)
        in_chip = mm(jnp.broadcast_to(is_mine, (16, 128)).astype(BF16), tri)[0:1].astype(jnp.int32)
        chip = (block * 128 + iota((1, 128), 1)) // (2 * here)
        spot = (chip * 2 + in_chip % 2) * slots + in_chip // 2
        places.append(jnp.where(is_mine > 0.5, place, -1))
        spots.append(jnp.where(is_mine > 0.5, spot, -1))
    place_hot = one(iota((here, children), 0) == jnp.concatenate(places, axis=1))
    spot = jnp.concatenate(spots, axis=1)
    grow_rows = one(iota((rows, here), 0) // STEPS == iota((rows, here), 1))
    size, deep = CHUNK, CHUNK // STEPS
    grow_columns = one(iota((deep, size), 0) == iota((deep, size), 1) // STEPS)
    same_step = iota((rows, size), 0) % STEPS == iota((rows, size), 1) % STEPS

    def fill(i):
        spot_hot = one(iota((deep, children), 0) + i * deep == spot)
        by_child = mm_nt(place_hot, spot_hot).astype(BF16)
        by_row = mm(mm(grow_rows, by_child).astype(BF16), grow_columns)
        by_row = jnp.where(same_step, by_row, 0.0)
        from_ref[:, chunk(i, size)] = by_row.astype(BF16)
        back_ref[chunk(i, size), :] = by_row.T.astype(BF16)

    over(wide // CHUNK, fill)

    owners(child_ref, owner_ref, mask_ref)
    for ref, target in zip((own_ref, other_ref), targets(slots, me, mask_ref, rows)):
        column = jnp.broadcast_to(target.astype(F32), (128, rows)).T[:, 0:1].astype(jnp.int32)

        def put(i, ref=ref, column=column):
            ref[:, chunk(i, size)] = one(iota((rows, size), 1) + i * size == column)

        over(wide // CHUNK, put)


def arrive(slots, groups, me, child_parent, parent_owner, parent_pages, page_table, rows):
    hot = jax.ShapeDtypeStruct((rows, groups * slots * STEPS), BF16)
    vmem = pl.BlockSpec(memory_space=pltpu.VMEM)
    smem = pl.BlockSpec(memory_space=pltpu.SMEM)
    return pl.pallas_call(
        functools.partial(arrive_kernel, slots),
        out_shape=(
            hot,
            jax.ShapeDtypeStruct(hot.shape[::-1], BF16),
            hot,
            hot,
            jax.ShapeDtypeStruct((PARENTS_HERE, 8), jnp.int32),
        ),
        in_specs=[smem] + [vmem] * 4,
        out_specs=(vmem,) * 5,
        scratch_shapes=[pltpu.VMEM((groups, child_parent.shape[0]), F32)],
        compiler_params=pltpu.CompilerParams(vmem_limit_bytes=24 * 2**20),
        cost_estimate=pl.CostEstimate(flops=2 * 10**9, bytes_accessed=2**20, transcendentals=0),
    )(
        me,
        child_parent.reshape(1, -1),
        parent_owner.reshape(1, -1),
        parent_pages.reshape(1, -1),
        jnp.pad(page_table, ((0, 0), (0, 8 - page_table.shape[1]))),
    )


def fill_kernel(own_hot_ref, other_hot_ref, own_ref, other_ref, out_ref):
    def fill(i):
        at = chunk(i, CHUNK)
        filled = mm(own_hot_ref[at, :], own_ref[...]) + mm(other_hot_ref[at, :], other_ref[...])
        out_ref[at, :] = filled.astype(BF16)

    over(out_ref.shape[0] // CHUNK, fill)


def fill_slots(own_hot, other_hot, own, other):
    vmem = pl.BlockSpec(memory_space=pltpu.VMEM)
    return pl.pallas_call(
        fill_kernel,
        out_shape=jax.ShapeDtypeStruct((own_hot.shape[0], own.shape[1]), BF16),
        in_specs=[vmem] * 4,
        out_specs=vmem,
        compiler_params=pltpu.CompilerParams(vmem_limit_bytes=24 * 2**20),
    )(own_hot, other_hot, own, other)


def place_rows(hot_ref, rows_ref, acc_ref):
    if rows_ref.shape[0] == CHUNK:
        return mm(hot_ref[...], rows_ref[...])
    acc_ref[...] = jnp.zeros_like(acc_ref)

    @pl.loop(0, rows_ref.shape[0] // CHUNK)
    def _(i):
        at = chunk(i, CHUNK)
        acc_ref[...] += mm(hot_ref[:, at], rows_ref[at, :])

    return acc_ref[...]


def place_kernel(hot_ref, rows_ref, out_ref, acc_ref):
    out_ref[...] = place_rows(hot_ref, rows_ref, acc_ref).astype(BF16)


def place_slots(hot, rows):
    vmem = pl.BlockSpec(memory_space=pltpu.VMEM)
    return pl.pallas_call(
        place_kernel,
        out_shape=jax.ShapeDtypeStruct((hot.shape[0], rows.shape[1]), BF16),
        in_specs=[vmem, vmem],
        out_specs=vmem,
        scratch_shapes=[pltpu.VMEM((hot.shape[0], rows.shape[1]), F32)],
        compiler_params=pltpu.CompilerParams(vmem_limit_bytes=24 * 2**20),
        cost_estimate=pl.CostEstimate(
            flops=2 * hot.shape[0] * hot.shape[1] * rows.shape[1],
            bytes_accessed=2 * rows.shape[0] * rows.shape[1],
            transcendentals=0,
        ),
    )(hot, rows)


def sum_kernel(rows_ref, sum_ref):
    x = rows_ref[...].astype(F32)
    total = jnp.sum(x * x, axis=1, keepdims=True)
    total = jnp.broadcast_to(total, (total.shape[0], 128)).T
    sum_ref[...] = jnp.broadcast_to(total[0:1], sum_ref.shape[:1] + total.shape[1:])[:, None, :]


def row_sums(rows, copies):
    vmem = pl.BlockSpec(memory_space=pltpu.VMEM)
    return pl.pallas_call(
        sum_kernel,
        out_shape=jax.ShapeDtypeStruct((copies, 1, rows.shape[0]), F32),
        in_specs=[vmem],
        out_specs=vmem,
        compiler_params=pltpu.CompilerParams(vmem_limit_bytes=24 * 2**20),
    )(rows)


def row_scale(sum_ref, width):
    total = jnp.sum(sum_ref[:, 0, :], axis=0, keepdims=True)
    scale = lax.rsqrt(total * (1.0 / width) + EPSILON)
    return jnp.broadcast_to(scale, (128, scale.shape[1])).T


def normed(x, scale, gain):
    return (x.astype(F32) * scale * gain.astype(F32)).astype(BF16)


def add_products(acc, x, wq, wkv):
    wide = wq.shape[1]
    acc[:, :wide] += mm(x, wq)
    acc[:, wide:] += mm(x, wkv)


def project_kernel(width, places, first, order_ref, sum_ref, *refs):
    count = len(places)
    pieces = sum(len(place) for place in places)
    blocks = refs[:pieces]
    gain_ref, wq_ref, wk_ref, wv_ref = refs[pieces : pieces + 4]
    before = None if first else refs[pieces + 4]
    acc_ref, x_ref, wq_held, wkv_held, x_sems, w_sems = refs[-6:]
    part = x_ref.shape[2]

    def copies(i):
        at = chunk(order_ref[i], part)
        return [
            pltpu.make_async_copy(wq_ref.at[at], wq_held.at[i], w_sems.at[i, 0]),
            pltpu.make_async_copy(wk_ref.at[at], wkv_held.at[i, :, :HEAD], w_sems.at[i, 1]),
            pltpu.make_async_copy(wv_ref.at[at], wkv_held.at[i, :, HEAD:], w_sems.at[i, 2]),
        ]

    for i, place in enumerate(places):
        for block, first_row in place:
            cut = pl.ds(first_row, blocks[block].shape[0])
            pltpu.make_async_copy(blocks[block], x_ref.at[i, cut], x_sems.at[i]).start()
        for copy in copies(i):
            copy.start()
    scale = row_scale(sum_ref, width)[:, 0:1]
    acc_ref[...] = jnp.zeros_like(acc_ref) if first else before[...]

    @pl.loop(0, count)
    def _(i):
        pltpu.make_async_copy(x_ref.at[i], x_ref.at[i], x_sems.at[i]).wait()
        for copy in copies(i):
            copy.wait()
        x = normed(x_ref[i], scale, gain_ref[order_ref[i]])
        add_products(acc_ref, x, wq_held[i], wkv_held[i])


def project(order, sums, blocks, gain, wq, wk, wv, before=None):
    part = blocks[0][0].shape[1]
    rows = sum(piece.shape[0] for piece in blocks[0])
    columns = wq.shape[1] + wk.shape[1] + wv.shape[1]
    count = len(blocks)
    pieces = [piece for block in blocks for piece in block]
    places, number = [], 0
    for block in blocks:
        starts = [sum(piece.shape[0] for piece in block[:i]) for i in range(len(block))]
        places.append([(number + i, start) for i, start in enumerate(starts)])
        number += len(block)
    smem = pl.BlockSpec(memory_space=pltpu.SMEM)
    vmem = pl.BlockSpec(memory_space=pltpu.VMEM)
    hbm = pl.BlockSpec(memory_space=pltpu.HBM)
    extra = [] if before is None else [before]
    return pl.pallas_call(
        functools.partial(project_kernel, wq.shape[0], places, before is None),
        out_shape=jax.ShapeDtypeStruct((rows, columns), F32),
        in_specs=[smem, vmem] + [hbm] * number + [vmem, hbm, hbm, hbm] + [vmem] * len(extra),
        out_specs=vmem,
        scratch_shapes=[
            pltpu.VMEM((count, rows, part), BF16),
            pltpu.VMEM((count, part, wq.shape[1]), BF16),
            pltpu.VMEM((count, part, 2 * HEAD), BF16),
            pltpu.SemaphoreType.DMA((count,)),
            pltpu.SemaphoreType.DMA((count, 3)),
        ],
        compiler_params=pltpu.CompilerParams(vmem_limit_bytes=28 * 2**20),
        cost_estimate=pl.CostEstimate(
            flops=2 * rows * part * count * columns * 2,
            bytes_accessed=2 * part * count * columns,
            transcendentals=0,
        ),
    )(order, sums, *pieces, gain, wq, wk, wv, *extra)


def attend_kernel(
    width,
    info_ref,
    sum_ref,
    low_ref,
    high_ref,
    gain_ref,
    wq_ref,
    wk_ref,
    wv_ref,
    before_ref,
    cos_ref,
    sin_ref,
    pool_ref,
    back_ref,
    out_ref,
    acc_ref,
    x_ref,
    wkv_ref,
    q_ref,
    k_ref,
    v_ref,
    o_ref,
):
    scale = row_scale(sum_ref, width)[:, 0:1]
    half = low_ref.shape[0]
    x_ref[:half] = normed(low_ref[...], scale[:half], gain_ref[...])
    x_ref[half:] = normed(high_ref[...], scale[half:], gain_ref[...])
    acc_ref[...] = before_ref[...]
    wkv_ref[:, :HEAD] = wk_ref[...]
    wkv_ref[:, HEAD:] = wv_ref[...]
    add_products(acc_ref, x_ref[...], wq_ref[...], wkv_ref[...])

    cos = cos_ref[...]
    sin = sin_ref[...]

    def turn(part):
        return (part * cos + pltpu.roll(part, HEAD // 2, 1) * sin).astype(BF16)

    heads = wq_ref.shape[1] // HEAD
    for h in range(heads):
        cut = slice(h * HEAD, (h + 1) * HEAD)
        q_ref[:, cut] = turn(acc_ref[:, cut])
    k_ref[...] = turn(acc_ref[:, heads * HEAD : (heads + 1) * HEAD])
    v_ref[...] = acc_ref[:, (heads + 1) * HEAD :].astype(BF16)

    family = FORK * STEPS
    scale = 1.0 / math.sqrt(HEAD)
    row_at = iota((heads * family, family), 0) % family
    key_at = iota((heads * family, family), 1)
    page_at = iota((heads * family, MOST_PAGES * PAGE), 1) // PAGE
    own_mask = (row_at // STEPS == key_at // STEPS) & (row_at >= key_at)

    @pl.loop(0, PARENTS_HERE, unroll=4)
    def _(j):
        at = pl.ds(pl.multiple_of(j * family, family), family)
        q = jnp.concatenate([q_ref[at, h * HEAD : (h + 1) * HEAD] for h in range(heads)], axis=0)
        own = jnp.where(own_mask, mm_nt(q, k_ref[at, :]) * scale, -jnp.inf)
        own_top = jnp.max(own, axis=1, keepdims=True)
        own_weight = jnp.exp(own - own_top)
        own_total = jnp.sum(own_weight, axis=1, keepdims=True)
        own_mix = mm(own_weight.astype(BF16), v_ref[at, :])
        length = info_ref[j, MOST_PAGES]
        ids = [info_ref[j, i] for i in range(MOST_PAGES)]
        keys = jnp.concatenate([pool_ref[i, 0] for i in ids], axis=0)
        values = jnp.concatenate([pool_ref[i, 1] for i in ids], axis=0)
        path = jnp.where(page_at < length, mm_nt(q, keys) * scale, -jnp.inf)
        path_top = jnp.max(path, axis=1, keepdims=True)
        weight = jnp.exp(path - path_top)
        path_total = jnp.sum(weight, axis=1, keepdims=True)
        path_mix = mm(weight.astype(BF16), values)
        top = jnp.maximum(path_top, own_top)
        path_factor = jnp.exp(path_top - top)
        own_factor = jnp.exp(own_top - top)
        both = path_mix * path_factor + own_mix * own_factor
        out = both / (path_total * path_factor + own_total * own_factor)
        out = out.astype(BF16)
        for h in range(heads):
            o_ref[at, h * HEAD : (h + 1) * HEAD] = out[h * family : (h + 1) * family]


    def fill(i):
        at = chunk(i, CHUNK)
        out_ref[at, :] = mm(back_ref[at, :], o_ref[...]).astype(BF16)

    over(out_ref.shape[0] // CHUNK, fill)


def attend(info, sums, low, high, gain, wq, wk, wv, before, cos, sin, pool, back):
    rows, columns = before.shape
    part = low.shape[1]
    wide = back.shape[0]
    vmem = pl.BlockSpec(memory_space=pltpu.VMEM)
    smem = pl.BlockSpec(memory_space=pltpu.SMEM)
    return pl.pallas_call(
        functools.partial(attend_kernel, 8 * part),
        out_shape=jax.ShapeDtypeStruct((wide, wq.shape[1]), BF16),
        in_specs=[smem] + [vmem] * 12,
        out_specs=vmem,
        scratch_shapes=[
            pltpu.VMEM((rows, columns), F32),
            pltpu.VMEM((rows, part), BF16),
            pltpu.VMEM((part, 2 * HEAD), BF16),
            pltpu.VMEM((rows, wq.shape[1]), BF16),
            pltpu.VMEM((rows, HEAD), BF16),
            pltpu.VMEM((rows, HEAD), BF16),
            pltpu.VMEM((rows, wq.shape[1]), BF16),
        ],
        compiler_params=pltpu.CompilerParams(vmem_limit_bytes=24 * 2**20),
        cost_estimate=pl.CostEstimate(
            flops=2 * rows * part * columns * 6, bytes_accessed=2 * part * columns, transcendentals=0
        ),
    )(info, sums, low, high, gain, wq, wk, wv, before, cos, sin, pool, back)


def moves(dy, dz):
    return [(t, ((t // 2 + dy) % 4) * 2 + (t + dz) % 2) for t in range(8)]


def after_leave(slots, groups, me, tables, arrays, send):
    (norm_gain, wq, wk, wv, kv_pool) = arrays
    wide, width = send.shape
    rows = PARENTS_HERE * FORK * STEPS
    team = lax.axis_size("tensor")
    t = lax.axis_index("tensor")
    came = lax.all_to_all(send.reshape(groups, wide // groups, width), "sample", 0, 0)
    from_hot, back_hot, own_hot, other_hot, info = arrive(slots, groups, me, *tables, rows)

    def place(dy, dz):
        return ((t // 2 + dy) % 4) * 2 + (t + dz) % 2

    def order(*keys):
        return jnp.stack([place(*key) for key in keys]).astype(jnp.int32)

    last = [lax.dynamic_slice_in_dim(w, place(2, 1) * width, width) for w in (wq, wk, wv)]
    gain = norm_gain.reshape(team, 1, -1)
    last_gain = lax.dynamic_slice_in_dim(norm_gain, place(2, 1) * width, width).reshape(1, -1)

    pages = info[:, MOST_PAGES]
    positions = (
        jnp.repeat(pages * PAGE, FORK * STEPS)
        + jnp.tile(jnp.arange(STEPS, dtype=jnp.int32), PARENTS_HERE * FORK)
    ).astype(F32)
    inverse = ROPE_THETA ** (-2.0 * jnp.arange(HEAD // 2, dtype=F32) / HEAD)
    angles = positions[:, None] * inverse[None, :]
    cos, sin = jnp.cos(angles), jnp.sin(angles)
    cos = jnp.concatenate([cos, cos], axis=1)
    sin = jnp.concatenate([-sin, sin], axis=1)
    came, from_hot, info, cos, sin, gain, last_gain, *last = lax.optimization_barrier(
        (came, from_hot, info, cos, sin, gain, last_gain, *last)
    )
    back_hot, own_hot, other_hot, from_hot = lax.optimization_barrier(
        (back_hot, own_hot, other_hot, from_hot)
    )
    mine = place_slots(from_hot, came.reshape(wide, width))

    def shift(block, dy, dz):
        return lax.ppermute(block, "tensor", moves(dy, dz))

    sums = lax.all_to_all(row_sums(mine, team), "tensor", 0, 0)
    b30, b10, b01 = shift(mine, 1, 0), shift(mine, -1, 0), shift(mine, 0, 1)
    half = rows // 2
    (b30,) = lax.optimization_barrier((b30,))
    b20, b31_low = shift(b30, 1, 0), shift(b30[:half], 0, 1)
    b01, b10 = lax.optimization_barrier((b01, b10))
    b11_high = shift(b01[half:], -1, 0)
    b30, b01, sums = lax.optimization_barrier((b30, b01, sums))
    b31_high, b11_low = shift(b30[half:], 0, 1), shift(b01[:half], -1, 0)
    b31_low, b11_high = lax.optimization_barrier((b31_low, b11_high))
    low, high = shift(b31_low, 1, 0), shift(b11_high, -1, 0)
    acc = project(
        order((0, 0), (3, 0), (1, 0), (0, 1)), sums, [[mine], [b30], [b10], [b01]], gain, wq, wk, wv
    )
    b20, b11_low, b31_high, acc = lax.optimization_barrier((b20, b11_low, b31_high, acc))
    acc = project(
        order((2, 0), (1, 1), (3, 1)),
        sums,
        [[b20], [b11_low, b11_high], [b31_low, b31_high]],
        gain,
        wq,
        wk,
        wv,
        acc,
    )
    low, high, acc = lax.optimization_barrier((low, high, acc))
    back = attend(
        info, sums, low, high, last_gain, *last, acc, cos, sin, kv_pool, back_hot
    )
    home = lax.all_to_all(back.reshape(groups, -1, back.shape[1]), "sample", 0, 0)
    home = home.reshape(-1, back.shape[1])
    other = place_slots(other_hot, home)
    return place_slots(own_hot, home) + lax.ppermute(other, "sample", swap(groups))


def swap(groups):
    return [(i, i ^ 1) for i in range(groups)]


def local(
    branch_tokens,
    norm_gain,
    query_weight,
    key_weight,
    value_weight,
    kv_pool,
    parent_owner,
    parent_pages,
    page_table,
    child_parent,
):
    groups = lax.axis_size("sample")
    rows = branch_tokens.shape[0]
    me = lax.axis_index("sample").astype(jnp.int32).reshape(1)
    tables = (child_parent, parent_owner, parent_pages, page_table)
    arrays = (norm_gain, query_weight, key_weight, value_weight, kv_pool)
    other = lax.ppermute(branch_tokens, "sample", swap(groups))
    own_hot, other_hot, fits = leave(SLOTS, groups, me, *tables[:2], rows)
    other, own_hot, other_hot, fits = lax.optimization_barrier((other, own_hot, other_hot, fits))
    send = fill_slots(own_hot, other_hot, branch_tokens, other)

    def usual():
        return after_leave(SLOTS, groups, me, tables, arrays, send)

    def crowded():
        most = 4 * SLOTS
        own, others, _ = leave(most, groups, me, *tables[:2], rows)
        wider = fill_slots(own, others, branch_tokens, other)
        return after_leave(most, groups, me, tables, arrays, wider)

    return lax.switch(fits[0], [crowded, usual])


def solution(mesh):
    return jax.shard_map(
        local,
        mesh=mesh,
        in_specs=(
            P("sample", "tensor"),
            P(),
            P(None, "tensor"),
            P(None, "tensor"),
            P(None, "tensor"),
            P("sample", None, None, "tensor"),
            P(),
            P(),
            P(),
            P(),
        ),
        out_specs=P("sample", "tensor"),
        check_vma=False,
    )
```
